256 devices in a mesh: gx: 8 (over y, core), gy: 32 (over x, z).
Axes of the slice: x: 4, y: 4, z: 8, core: 2. Of those that a mesh axis runs over, the one named last changes fastest.
Arguments:
- rhs: float32 [16, 262144], P(None, ('gx', 'gy')), may hold values from -63 to 63, as said below
- embeddings: float32 [64, 262144], P(None, ('gx', 'gy')), may hold values from -4 to 4
- leaf_order: int32 [256, 1024], P(('gx', 'gy')), may hold values from 0 to 1023, each once within a row
- basis: float32 [64, 262144], P(None, ('gx', 'gy')), may hold values from -0.1875 to 0.1875
- transfer_maps: float32 [5, 256, 64, 64], P(None, ('gx', 'gy')), may hold values from -1 to 1, as said below
- skeletons: float32 [4, 256, 64, 64], P(None, ('gx', 'gy')), may hold values from -1.4 to 1.4, as said below
- top_skeletons: float32 [8, 64, 64], replicated, may hold values from -1.4 to 1.4
- near_lists: int32 [256, 3], P(('gx', 'gy')), may hold values from 0 to 255, as said below
- far_lists: int32 [4, 256], P(None, ('gx', 'gy')), may hold values from 0 to 255, as said below
- top_lists: int32 [8, 4], replicated, may hold values from 0 to 7, as said below
Outputs:
- solution: float32 [16, 262144], P(None, ('gx', 'gy'))
- residual: float32 [16, 262144], P(None, ('gx', 'gy'))
The draws below stay inside these ranges and needn't reach their ends.
Inputs may be any that keep to these rules, and one draw needn't show every extreme that they name: `rhs`: custom law; entries are products of a random part and positive scales of points, columns and position. `leaf_order`: each row is a permutation of 0 to 1023. `transfer_maps`: rows of leaves with the same ancestor at height h are equal. `skeletons`: rows of leaves with the same ancestor at height h are equal. `near_lists`: row d holds d and the two other leaves of its aligned group of 4 (leaves 4q to 4q + 3) that are not far_lists[0, d], in some order; the relation is symmetric. far_lists[h, d] is c XOR o for the cluster c = d >> h, with o of 1 to 3 the same for all clusters of c's aligned group of 4 at height h; so the relation is symmetric and the partner shares c's group. Leaves with the same ancestor have the same entry. `top_lists`: row c holds c XOR o for 4 distinct nonzero offsets o, the same offsets in every row, one of them 4.
All inputs are finite; a program needn't handle non-finite values.
Results may differ from the reference program's by a relative error of at most 0.0003.
Values sent between devices are 32-bit elements; how exact they have to be, the bound alone decides.
No kernel may reach another device: no remote copies, remote signals or barrier semaphores. Data moves between devices by JAX's collectives and lax.ppermute only.
A program may use at most 128 MiB of HBM per device.

```python
import math
import jax
import jax.numpy as jnp
from jax import lax

LEAF = 1024
DIM = 64
RANK = 64
NRHS = 16
ITERS = 2
NEAR = 3
LEAVES = 256
POINTS = 262144
BITS_Y = 5
FARH = 4
TOPK = 4
N_GX = 8
N_GY = 32


def clipped_normal(key, shape, scale):
    return scale * jnp.clip(jax.random.normal(key, shape, jnp.float32), -4.0, 4.0)


def leaf_indexed(values):
    layers = []
    for h in range(values.shape[0]):
        sources = jnp.left_shift(jnp.right_shift(jnp.arange(LEAVES, dtype=jnp.int32), h), h)
        layers.append(values[h][sources])
    return jnp.stack(layers)


def group_offsets(key):
    return [jax.random.randint(jax.random.fold_in(key, 100 + h), (LEAVES >> h + 2,), 1, 4, dtype=jnp.int32) for h in range(FARH)]


def draw_rhs(key, part):
    key = jax.random.fold_in(key, 1)
    first_key, second_key, third_key = jax.random.split(key, 3)
    base_values = clipped_normal(first_key, (NRHS, POINTS), 1.0)
    row_scale = jnp.exp(jax.random.uniform(second_key, (1, POINTS), jnp.float32, math.log(0.3), math.log(3.0)))
    column_scale = jnp.exp(jax.random.uniform(third_key, (NRHS, 1), jnp.float32, math.log(0.3), math.log(3.0)))
    position = (jnp.arange(POINTS, dtype=jnp.int32) // LEAF).astype(jnp.float32) / (LEAVES - 1) - 0.5
    trend = jnp.power(3.0, position)[None, :]
    return base_values * row_scale * column_scale * trend


def draw_embeddings(key, part):
    key = jax.random.fold_in(key, 2)
    return clipped_normal(key, (DIM, POINTS), 1.0)


def draw_transfer_maps(key, part):
    key = jax.random.fold_in(key, 3)
    factor = 1.0 / math.sqrt(2.0 * RANK)
    values = clipped_normal(key, (BITS_Y, LEAVES, RANK, RANK), factor)
    return leaf_indexed(values)


def draw_skeletons(key, part):
    key = jax.random.fold_in(key, 5)
    values = clipped_normal(key, (FARH, LEAVES, DIM, RANK), 0.35)
    return leaf_indexed(values)


def draw_top_skeletons(key, part):
    key = jax.random.fold_in(key, 6)
    return clipped_normal(key, (N_GX, DIM, RANK), 0.35)


def draw_far_lists(key, part):
    offsets = group_offsets(key)
    leaf_ids = jnp.arange(LEAVES, dtype=jnp.int32)
    layers = []
    for h in range(FARH):
        cluster = jnp.right_shift(leaf_ids, h)
        layers.append(jnp.bitwise_xor(cluster, offsets[h][jnp.right_shift(cluster, 2)]))
    return jnp.stack(layers)


def draw_near_lists(key, part):
    offsets = group_offsets(key)
    key = jax.random.fold_in(key, 11)
    leaf_ids = jnp.arange(LEAVES, dtype=jnp.int32)
    excluded = offsets[0][jnp.right_shift(leaf_ids, 2)]
    first_offset = jnp.where(excluded == 1, 2, 1)
    second_offset = jnp.where(excluded == 3, 2, 3)
    members = jnp.stack([leaf_ids, jnp.bitwise_xor(leaf_ids, first_offset), jnp.bitwise_xor(leaf_ids, second_offset)], axis=1)
    rotation = jax.random.randint(key, (LEAVES, 1), 0, 3, dtype=jnp.int32)
    positions = (jnp.arange(3, dtype=jnp.int32)[None, :] + rotation) % 3
    return jnp.take_along_axis(members, positions, axis=1)


def draw_top_lists(key, part):
    key = jax.random.fold_in(key, 13)
    half_offset = N_GX // 2
    others = jax.random.permutation(key, max(N_GX - 2, 1))[:TOPK - 1].astype(jnp.int32) + 1
    others = jnp.where(others >= half_offset, others + 1, others)
    shifts = jnp.concatenate([jnp.full((1,), half_offset, jnp.int32), others])
    clusters = jnp.arange(N_GX, dtype=jnp.int32)
    return jnp.bitwise_xor(clusters[:, None], shifts[None, :])


def block_levels(stream_key, shape, cuts, low, largest):
    factor_of, own = 1.0, jax.random.fold_in(stream_key, 6)
    for dim, shards_of in cuts:
        steps = jnp.exp(jax.random.uniform(jax.random.fold_in(own, dim), (shards_of,), jnp.float32, low / len(cuts), largest / len(cuts)))
        factor_of = factor_of * jnp.repeat(steps, shape[dim] // shards_of).reshape([-1 if axis == dim else 1 for axis in range(len(shape))])
    return factor_of


def bell_draw(own_key, extent, spread, limit, cuts=(), kind=jnp.bfloat16):
    result = jax.random.normal(own_key, extent, jnp.float32) * spread
    if len(cuts) > 0:
        result = block_levels(own_key, extent, cuts, -0.22, 0.18) * result
    return jnp.clip(result, min=-limit, max=limit).astype(kind)


def setup_inputs(seed: int = 0) -> dict:
    key_of = jax.random.split(jax.random.key(seed), 11)
    return {
        "rhs": draw_rhs(jax.random.fold_in(key_of[10], 71), 0),
        "embeddings": draw_embeddings(jax.random.fold_in(key_of[10], 71), 0),
        "leaf_order": jax.vmap(lambda own: jax.random.permutation(own, LEAF))(jax.random.split(key_of[2], LEAVES)).reshape((LEAVES, LEAF)).astype(jnp.int32),
        "basis": bell_draw(key_of[3], (RANK, POINTS), LEAF ** -0.5, 0.1875, ((1, 256),), jnp.float32),
        "transfer_maps": draw_transfer_maps(jax.random.fold_in(key_of[10], 71), 0),
        "skeletons": draw_skeletons(jax.random.fold_in(key_of[10], 71), 0),
        "top_skeletons": draw_top_skeletons(jax.random.fold_in(key_of[10], 71), 0),
        "near_lists": draw_near_lists(jax.random.fold_in(key_of[10], 71), 0),
        "far_lists": draw_far_lists(jax.random.fold_in(key_of[10], 71), 0),
        "top_lists": draw_top_lists(jax.random.fold_in(key_of[10], 71), 0),
    }


highest = lax.Precision.HIGHEST
noise_level = 0.5
length_scale = 2.8
root_five = math.sqrt(5.0)

def matern(first_set, second_set):
    cross_dot = lax.dot_general(first_set, second_set, (((0,), (0,)), ((), ())), precision=highest, preferred_element_type=jnp.float32)
    squares = lax.optimization_barrier(jnp.sum(first_set * first_set, axis=0))[:, None] + lax.optimization_barrier(jnp.sum(second_set * second_set, axis=0))[None, :] - 2.0 * cross_dot
    scaled = root_five * jnp.sqrt(jnp.maximum(squares, 0.0)) / length_scale
    return (1.0 + scaled + scaled * scaled / 3.0) * jnp.exp(-scaled)

def reference(rhs, embeddings, leaf_order, basis, transfer_maps, skeletons, top_skeletons, near_lists, far_lists, top_lists):
    leaves = N_GX * N_GY
    gather_index = (jnp.arange(leaves, dtype=jnp.int32)[:, None] * LEAF + leaf_order.astype(jnp.int32)).reshape(-1)
    source = jnp.take(rhs, gather_index, axis=1)
    points = jnp.take(embeddings, gather_index, axis=1)
    leaf_points = points.reshape(DIM, leaves, LEAF)
    leaf_bases = basis.reshape(RANK, leaves, LEAF)
    chain_maps = [transfer_maps[h, ::1 << h] for h in range(BITS_Y)]
    partners = [far_lists[h, ::1 << h] for h in range(FARH)]
    couplings = []
    for h in range(FARH):
        own_skeletons = skeletons[h, ::1 << h]
        couplings.append(jax.vmap(matern)(own_skeletons, own_skeletons[partners[h]]))
    top_couplings = jax.vmap(lambda c, r: jax.vmap(lambda j: matern(top_skeletons[c], top_skeletons[j]))(r))(jnp.arange(N_GX, dtype=jnp.int32), top_lists)

    def operate(vector):
        blocks = vector.reshape(NRHS, leaves, LEAF)
        moment = jnp.einsum('nlp,rlp->lnr', blocks, leaf_bases, precision=highest)
        moments = [moment]
        for h in range(BITS_Y):
            lifted = jnp.einsum('cnr,crs->cns', moment, chain_maps[h], precision=highest)
            moment = lifted.reshape(-1, 2, NRHS, RANK).sum(axis=1)
            moments.append(moment)
        far_field = jnp.einsum('ckns,ckrs->cnr', moment[top_lists], top_couplings, precision=highest)
        for h in reversed(range(BITS_Y)):
            far_field = jnp.einsum('cns,crs->cnr', jnp.repeat(far_field, 2, axis=0), chain_maps[h], precision=highest)
            if h < FARH:
                far_field = far_field + jnp.einsum('cns,crs->cnr', moments[h][partners[h]], couplings[h], precision=highest)
        far_part = jnp.einsum('lnr,rlp->nlp', far_field, leaf_bases, precision=highest).reshape(NRHS, -1)

        def near_leaf(leaf_index):
            own_points = lax.dynamic_index_in_dim(leaf_points, leaf_index, 1, keepdims=False)
            running = jnp.zeros((NRHS, LEAF), jnp.float32)
            for e in range(NEAR):
                neighbour = near_lists[leaf_index, e].astype(jnp.int32)
                kernel = matern(own_points, lax.dynamic_index_in_dim(leaf_points, neighbour, 1, keepdims=False))
                running = running + lax.dot_general(lax.dynamic_index_in_dim(blocks, neighbour, 1, keepdims=False), kernel, (((1,), (1,)), ((), ())), precision=highest, preferred_element_type=jnp.float32)
            return running
        near_part = lax.map(near_leaf, jnp.arange(leaves, dtype=jnp.int32))
        near_part = jnp.transpose(near_part, (1, 0, 2)).reshape(NRHS, -1)
        return noise_level * vector + near_part + far_part
    iterate = jnp.zeros_like(source)
    remainder = source
    image = operate(remainder)
    norm_now = lax.optimization_barrier(jnp.sum(image * image, axis=1))
    direction = image
    for iteration in range(ITERS):
        direction_image = operate(direction)
        step_size = norm_now / lax.optimization_barrier(jnp.sum(direction_image * direction_image, axis=1))
        iterate = iterate + step_size[:, None] * direction
        remainder = remainder - step_size[:, None] * direction_image
        if iteration + 1 < ITERS:
            image = operate(remainder)
            norm_next = lax.optimization_barrier(jnp.sum(image * image, axis=1))
            direction = image + (norm_next / norm_now)[:, None] * direction
            norm_now = norm_next
    solution = jnp.zeros_like(iterate).at[:, gather_index].set(iterate)
    residual = jnp.zeros_like(remainder).at[:, gather_index].set(remainder)
    return (solution, residual)
```

```python
import functools
import math

import jax
import jax.numpy as jnp
from jax import lax
from jax.experimental import pallas as pl
from jax.experimental.pallas import tpu as pltpu
from jax.sharding import Mesh
from jax.sharding import PartitionSpec as P

F32 = jnp.float32
BF16 = jnp.bfloat16
HIGHEST = lax.Precision.HIGHEST
NOISE = 0.5
SCALE = math.sqrt(5.0) / 2.8
LOG2E = math.log2(math.e)
DEPTH = 208
TILE = 256

Z, X, Y, CORE, O0, O1, O2, O3, TOPS = range(9)


def dot(a, b, ca=1, cb=0, precision=None):
    return lax.dot_general(
        a, b, (((ca,), (cb,)), ((), ())), precision=precision, preferred_element_type=F32
    )


def split(a):
    high = a.astype(BF16)
    return high, (a - high.astype(F32)).astype(BF16)


def stacked(a):
    return jnp.concatenate(split(a), axis=0)


def halves(a):
    n = a.shape[0] // 2
    return a[:n] + a[n:]


def square_sum(v):
    return jnp.broadcast_to(jnp.sum(v * v, axis=1, keepdims=True), (v.shape[0], 64))


def moments(v, weighed, bases, chain):
    both = halves(dot(stacked(v), bases, 1, 1))
    own = both[:, :64] + both[:, 64:]
    lifted = dot(own, chain[:, 0:192], precision=HIGHEST)
    first = jnp.concatenate([square_sum(weighed), lifted[:, 0:64]], axis=1)
    return jnp.concatenate([own, jnp.zeros_like(own)], axis=1), first, lifted[:, 64:192]


def write_moments(extended, out, v, weighed, bases, chain):
    own, first, second = moments(v, weighed, bases[...], chain[...])
    extended[:, 0 : v.shape[1]] = v
    extended[:, v.shape[1] :] = own
    for i in range(out.shape[0]):
        out[i, 0:16, :] = first
        out[i, 16:32, :] = second


def prepare_kernel(scalars, order, basis, maps, skeletons, rhs, bases, chain, out):
    both = stacked(basis[...])
    leaf = basis.shape[1]
    for t in range(leaf // TILE):
        rows = lax.broadcasted_iota(jnp.int32, (TILE, leaf), 0) + t * TILE
        one_hot = jnp.where(rows == order[...], 1.0, 0.0).astype(BF16)
        bases[:, t * TILE : (t + 1) * TILE] = dot(both, one_hot, 1, 1).astype(BF16)
    p1 = maps[0]
    p2 = dot(p1, maps[1], precision=HIGHEST)
    p3 = dot(p2, maps[2], precision=HIGHEST)
    chain[...] = jnp.concatenate([p1, p2, p3, dot(maps[3], maps[4], precision=HIGHEST)], axis=1)
    own, first, second = moments(rhs[...], rhs[...], bases[...], chain[...])
    z = scalars[Z]
    for i in range(out.shape[0]):
        offset = jnp.bitwise_xor(z, i)
        skeleton = jnp.where(offset == 4, skeletons[2], skeletons[0])
        out[i, 0:16, :] = first
        out[i, 16:32, :] = second
        out[i, 32:48, :] = own
        out[i, 48:112, :] = jnp.concatenate([skeleton, skeletons[1]], axis=1)


def matern(first, second):
    turned = first.T
    squares = (
        jnp.sum(turned * turned, axis=1, keepdims=True)
        + jnp.sum(second * second, axis=0, keepdims=True)
        - 2.0 * dot(turned, second, precision=HIGHEST)
    )
    s = SCALE * jnp.sqrt(jnp.maximum(squares, 0.0))
    return (1.0 + s + s * s * (1.0 / 3.0)) * jnp.exp(-s)


def coupling_kernel(scalars, skeletons, from_z, from_x, tops, chain, after, out):
    z, x, core = scalars[Z], scalars[X], scalars[CORE]
    o0, o1, o2, o3 = scalars[O0], scalars[O1], scalars[O2], scalars[O3]
    partners = [
        from_z[jnp.bitwise_xor(z, o0), 48:112, 0:64],
        from_z[jnp.bitwise_xor(z, o1 * 2), 48:112, 64:128],
        from_x[jnp.bitwise_xor(x, o2 // 2), :, 0:64],
        from_x[jnp.bitwise_xor(x, o3), :, 64:128],
    ]
    pieces = []
    for h in range(4):
        coupling = matern(skeletons[h], partners[h])
        if h > 0:
            coupling = dot(chain[:, (h - 1) * 64 : h * 64], coupling, precision=HIGHEST)
        pieces.append(coupling)
    out[:, 0:256] = jnp.concatenate(pieces, axis=1)
    others = []
    masks = []
    for flip in (0, 1):
        for y in range(4):
            side = jnp.bitwise_xor(core, flip)
            others.append(tops[y, side])
            hits = sum((scalars[TOPS + j] == y * 2 + side).astype(F32) for j in range(4))
            masks.append(jnp.full((64, 64), hits, F32))
    top = matern(tops[scalars[Y], core], jnp.concatenate(others, axis=1))
    top = top * jnp.concatenate(masks, axis=1)
    whole = dot(chain[:, 128:192], chain[:, 192:256], precision=HIGHEST)
    out[:, 256:768] = dot(whole, top, precision=HIGHEST)


def three(a):
    high = a.astype(BF16).astype(F32)
    middle = (a - high).astype(BF16).astype(F32)
    return high, middle, a - high - middle


def build_kernel(scalars, own, *refs, choice):
    if choice is None:
        vector_ref, begin, after, whole, near, aug, squares, kernel, sems = refs
        slot = 0
        near[...] = NOISE * begin[...]
    else:
        yes, no, begin, after, previous, whole, near, aug, squares, kernel, sems = refs
        slot = (choice + 1) // 2
        near[...] = begin[...]
        take = scalars[O0] == choice
    leaf = own.shape[1]

    high, low = split(own[...] * SCALE)
    h32, l32 = high.astype(F32), low.astype(F32)
    sums = three(jnp.sum(h32 * h32 + 2.0 * (h32 * l32), axis=0, keepdims=True))
    row = lax.broadcasted_iota(jnp.int32, (16, leaf), 0)
    tail = jnp.where(row < 3, 1.0, 0.0)
    for i in range(3):
        tail = jnp.where(row == 3 + i, sums[i], tail)
    aug[0:64, :] = high
    aug[64:128, :] = low
    aug[128:192, :] = high
    aug[192:208, :] = tail.astype(BF16)

    def tile(t, carry):
        start = pl.multiple_of(t * TILE, TILE)
        cols = pl.ds(start, TILE)
        if choice is None:
            points = own[:, cols]
            vector = vector_ref[:, cols]
        else:
            points = jnp.where(take, yes[0:64, cols], no[0:64, cols])
            vector = jnp.where(take, yes[64:80, cols], no[64:80, cols])
        high, low = split((points * SCALE).T)
        h32, l32 = high.astype(F32), low.astype(F32)
        sums = three(jnp.sum(h32 * h32 + 2.0 * (h32 * l32), axis=1, keepdims=True))
        lane = lax.broadcasted_iota(jnp.int32, (TILE, 16), 1)
        tail = jnp.where((lane >= 3) & (lane < 6), 1.0, 0.0)
        for i in range(3):
            tail = jnp.where(lane == i, sums[i], tail)
        left = jnp.concatenate([-2.0 * h32, -2.0 * h32, -2.0 * l32, tail], axis=1).astype(BF16)
        squares[...] = dot(left, aug[...])
        wide = 512
        tall = 32

        def entries(i, carry):
            r = pl.multiple_of(i * tall, tall)
            for c in range(0, leaf, wide):
                s2 = jnp.maximum(squares[pl.ds(r, tall), c : c + wide], 0.0)
                s = s2 * lax.rsqrt(jnp.maximum(s2, 1e-30))
                value = (1.0 + s + s2 * (1.0 / 3.0)) * jnp.exp2(s * -LOG2E)
                high, low = split(value)
                kernel[t, 0, pl.ds(r, tall), c : c + wide] = high
                kernel[t, 1, pl.ds(r, tall), c : c + wide] = low
            return carry

        lax.fori_loop(0, TILE // tall, entries, 0, unroll=2)
        pair = stacked(vector)
        near[...] += halves(dot(pair, kernel[t, 0]) + dot(pair, kernel[t, 1]))
        pltpu.make_async_copy(kernel.at[t], whole.at[slot, :, cols, :], sems.at[t]).start()
        return carry

    tiles = leaf // TILE
    lax.fori_loop(0, tiles, tile, 0)
    for t in range(tiles):
        rows = pl.ds(t * TILE, TILE)
        pltpu.make_async_copy(kernel.at[t], whole.at[slot, :, rows, :], sems.at[t]).wait()


def near_kernel(scalars, v, v1, v2, v3, kernels, out, held, sems):
    leaf = kernels.shape[2]
    tiles = leaf // TILE
    copies = []
    for e in range(3):
        for t in range(tiles):
            rows = pl.ds(t * TILE, TILE)
            copies.append(
                pltpu.make_async_copy(
                    kernels.at[e, :, rows, :], held.at[e, :, rows, :], sems.at[e * tiles + t]
                )
            )
    for copy in copies:
        copy.start()
    o0 = scalars[O0]
    own = v[:, 0:leaf]
    second = jnp.where(o0 == 1, v2[:, 0:leaf], v1[:, 0:leaf])
    third = jnp.where(o0 == 3, v2[:, 0:leaf], v3[:, 0:leaf])
    total = None
    for e, vector in enumerate((own, second, third)):
        pair = stacked(vector)
        for t in range(tiles):
            rows = slice(t * TILE, (t + 1) * TILE)
            copies[e * tiles + t].wait()
            part = dot(pair[:, rows], held[e, 0, rows, :]) + dot(pair[:, rows], held[e, 1, rows, :])
            total = part if total is None else total + part
    out[:, 0:leaf] = NOISE * own + halves(total)
    out[:, leaf:] = jnp.where(
        o0 == 1, v1[:, leaf:], jnp.where(o0 == 2, v2[:, leaf:], v3[:, leaf:])
    )


def first_middle_kernel(scalars, received, chain, skeletons, after, moved, low, out, pairs):
    middle_kernel(scalars, received, chain, low, out, first=True)
    third = jnp.where(
        scalars[O2] % 2 == 1,
        received[jnp.bitwise_xor(scalars[Z], 4), 48:112, 0:64],
        skeletons[2],
    )
    pair = jnp.concatenate([third, skeletons[3]], axis=1)
    for i in range(pairs.shape[0]):
        pairs[i] = pair


def middle_kernel(scalars, received, chain, low, out, first=False):
    z, o0, o1, o2 = scalars[Z], scalars[O0], scalars[O1], scalars[O2]
    left = lax.broadcasted_iota(jnp.int32, (16, 128), 1) < 64
    sums = [jnp.zeros((16, 128), F32) for _ in range(3)]
    for i in range(received.shape[0]):
        offset = jnp.bitwise_xor(z, i)
        hit1 = offset // 2 == o1
        hit2 = offset // 4 == jnp.bitwise_and(o2, 1)
        sums[0] += jnp.where(left | hit1, received[i, 0:16, :], 0.0)
        sums[1] += jnp.where(~left | hit2, received[i, 16:32, :], 0.0)
        if first:
            sums[2] += jnp.where(offset == o0, received[i, 32:48, :], 0.0)
    low[...] = jnp.concatenate([sums[2][:, 0:64], sums[0][:, 64:128]], axis=1)
    top = dot(sums[1][:, 64:128], chain[:, 192:256], precision=HIGHEST)
    last = jnp.concatenate([top, sums[0][:, 0:64]], axis=1)
    for i in range(out.shape[0]):
        out[i, 0:16, :] = sums[1]
        out[i, 16:32, :] = last


def gather_kernel(scalars, received, *refs):
    high, out = refs[-2:]
    x, y, o2, o3 = scalars[X], scalars[Y], scalars[O2], scalars[O3]
    left = lax.broadcasted_iota(jnp.int32, (16, 128), 1) < 64
    total = jnp.zeros((16, 128), F32)
    for j in range(4):
        top = jnp.zeros((16, 128), F32)
        for i in range(4):
            p = j * 4 + i
            offset = jnp.bitwise_xor(x, i)
            here = y == j
            hit2 = here & (offset == o2 // 2)
            hit3 = here & (offset == o3)
            total += jnp.where((left & hit2) | (~left & hit3), received[p, 0:16, :], 0.0)
            top += received[p, 16:32, :]
        out[j * 16 : (j + 1) * 16, :] = top
    high[...] = total


def apply_far(low, high, mine, other, table, bases, near):
    leaf = bases.shape[1]
    if near.shape[1] > leaf:
        parts = [near[:, leaf : leaf + 64], low[:, 64:128], high[...]]
    else:
        parts = [low[...], high[...]]
    for side in (mine, other):
        parts += [side[j * 16 : (j + 1) * 16, 0:64] for j in range(4)]
    field = dot(jnp.concatenate(parts, axis=1), table[...], 1, 1, precision=HIGHEST)
    pair = stacked(field)
    far = halves(dot(pair, bases[0:64, :]) + dot(pair, bases[64:128, :]))
    total = sum(side[j * 16 : (j + 1) * 16, 64:128] for side in (mine, other) for j in range(4))
    return near[:, 0:leaf] + far, total[:, 0:1]


def first_kernel(low, high, mine, other, table, bases, near, chain, v1, out):
    image, _ = apply_far(low, high, mine, other, table, bases, near)
    write_moments(v1, out, image, image, bases, chain)


def second_kernel(low, high, mine, other, table, bases, near, chain, v2, scaled, sums, out):
    image, norm = apply_far(low, high, mine, other, table, bases, near)
    v2[...] = image
    sums[...] = jnp.broadcast_to(norm, sums.shape)
    write_moments(scaled, out, image / jnp.sqrt(norm), image, bases, chain)


def third_kernel(low, high, mine, other, table, bases, near, chain, v1, sums, image, step, out):
    product, along = apply_far(low, high, mine, other, table, bases, near)
    norm = sums[:, 0:1]
    size = norm / along
    new = v1[:, 0 : product.shape[1]] - (size * jnp.sqrt(norm)) * product
    step[...] = jnp.broadcast_to(size, step.shape)
    write_moments(image, out, new, new, bases, chain)


def diagonal():
    rows = lax.broadcasted_iota(jnp.int32, (16, 128), 0)
    return rows == lax.broadcasted_iota(jnp.int32, (16, 128), 1)


def fourth_kernel(low, high, mine, other, table, bases, near, v2, sums, along, fresh, out):
    product, norm = apply_far(low, high, mine, other, table, bases, near)
    new = product + (norm / sums[:, 0:1]) * v2[...]
    along[...] = new
    fresh[...] = jnp.broadcast_to(norm, fresh.shape)
    share = jnp.sum(new * new, axis=1, keepdims=True)
    line = jnp.sum(jnp.where(diagonal(), share, 0.0), axis=0, keepdims=True)
    for i in range(out.shape[0]):
        out[i] = jnp.broadcast_to(line, (8, 128))


def spread_kernel(received, out):
    total = received[0]
    for i in range(1, received.shape[0]):
        total = total + received[i]
    for i in range(out.shape[0]):
        out[i] = total


def last_kernel(shares, rhs, v1, v2, image, along, sums, fresh, step, iterate, residual):
    leaf = rhs.shape[1]
    norm = fresh[:, 0:1]
    first = step[:, 0:1]
    line = sum(shares[i, 0:1, :] for i in range(shares.shape[0]))
    second = norm / jnp.sum(jnp.where(diagonal(), line, 0.0), axis=1, keepdims=True)
    beta = norm / sums[:, 0:1]
    start = v1[:, 0:leaf]
    iterate[...] = first * start + second * (image[:, 0:leaf] + beta * start)
    residual[...] = rhs[...] - first * v2[...] - second * along[...]


SMEM = pl.BlockSpec(memory_space=pltpu.SMEM)
VMEM = pl.BlockSpec(memory_space=pltpu.VMEM)


def shaped(*shape, dtype=F32):
    return jax.ShapeDtypeStruct(shape, dtype)


MIB = 1024 * 1024
ANY = pl.BlockSpec(memory_space=pl.ANY)


def call(kernel, outs, scalars, arrays, name, after=(), limit=16, flops=100000, scratch=(), alias=None):
    return pl.pallas_call(
        kernel,
        out_shape=outs,
        in_specs=[SMEM] * len(scalars) + [VMEM] * len(arrays) + [ANY] * len(after),
        out_specs=jax.tree.map(lambda a: VMEM if len(a.shape) < 4 else ANY, outs),
        scratch_shapes=list(scratch),
        input_output_aliases=alias or {},
        name=name,
        compiler_params=pltpu.CompilerParams(vmem_limit_bytes=limit * MIB),
        cost_estimate=pl.CostEstimate(flops=flops, bytes_accessed=500000, transcendentals=0),
    )(*scalars, *arrays, *after)


def build(scalars, own, others, choice, near, after, name, kernels=()):
    leaf = own.shape[1]
    tiles = leaf // TILE
    return call(
        functools.partial(build_kernel, choice=choice),
        (shaped(3, 2, leaf, leaf, dtype=BF16), shaped(16, leaf)),
        [scalars],
        [own, *others, near],
        name,
        after=[*after, *kernels],
        limit=50,
        flops=4000000000,
        alias={3 + len(others) + len(after): 0} if kernels else None,
        scratch=[
            pltpu.VMEM((DEPTH, leaf), BF16),
            pltpu.VMEM((TILE, leaf), F32),
            pltpu.VMEM((tiles, 2, TILE, leaf), BF16),
            pltpu.SemaphoreType.DMA((tiles,)),
        ],
    )


def near_product(scalars, vectors, kernels):
    leaf = kernels.shape[2]
    return call(
        near_kernel,
        shaped(*vectors[0].shape),
        [scalars],
        vectors,
        "near",
        after=[kernels],
        limit=50,
        flops=4000000000,
        scratch=[
            pltpu.VMEM((3, 2, leaf, leaf), BF16),
            pltpu.SemaphoreType.DMA((3 * leaf // TILE,)),
        ],
    )


def to_group(v):
    return [lax.ppermute(v, "z", [(i, i ^ o) for i in range(8)]) for o in (1, 2, 3)]


def other_core(v):
    return lax.ppermute(v, "core", [(0, 1), (1, 0)])


def over_z(v):
    return lax.all_to_all(v, "z", 0, 0)


def over_yx(v):
    return lax.all_to_all(v, ("y", "x"), 0, 0)


def local(
    rhs,
    embeddings,
    leaf_order,
    basis,
    transfer_maps,
    skeletons,
    top_skeletons,
    near_lists,
    far_lists,
    top_lists,
):
    y, core, x, z = (lax.axis_index(a) for a in ("y", "core", "x", "z"))
    top = y * 2 + core
    leaf = top * 32 + x * 8 + z
    offsets = jnp.bitwise_xor(
        far_lists[:, 0], jnp.right_shift(leaf, jnp.arange(4, dtype=jnp.int32))
    )
    partners = lax.dynamic_index_in_dim(top_lists, top, 0, keepdims=False)
    scalars = jnp.concatenate([jnp.stack([z, x, y, core]), offsets, partners]).astype(jnp.int32)
    chain_skeletons = skeletons[:, 0]
    tops = top_skeletons.reshape(4, 2, 64, 64)

    moved = to_group(jnp.concatenate([embeddings, rhs], axis=0))
    bases, chain, outgoing = call(
        prepare_kernel,
        (shaped(128, 1024, dtype=BF16), shaped(64, 256), shaped(8, 112, 128)),
        [scalars],
        [leaf_order, basis, transfer_maps[:, 0], chain_skeletons, rhs],
        "prepare",
        limit=50,
    )

    def gather(spread, after):
        high, mine = call(
            gather_kernel,
            (shaped(16, 128), shaped(64, 128)),
            [scalars],
            [spread],
            "gather",
            after=after,
        )
        return high, mine, other_core(mine)

    received = over_z(outgoing)
    kernels, near = build(scalars, embeddings, [rhs], None, rhs, [chain], "build_own")
    low, wide, pairs = call(
        first_middle_kernel,
        (shaped(16, 128), shaped(16, 32, 128), shaped(4, 64, 128)),
        [scalars],
        [received, chain, chain_skeletons],
        "middle",
        after=[near, moved[0]],
    )
    spread = over_yx(wide)
    from_x = lax.all_to_all(pairs, "x", 0, 0)
    kernels, near = build(
        scalars, embeddings, [moved[1], moved[0]], 1, near, [low], "build_a", [kernels]
    )
    high, mine, other = gather(spread, [near, from_x])
    kernels, near = build(
        scalars, embeddings, [moved[1], moved[2]], 3, near, [high], "build_b", [kernels]
    )
    table = call(
        coupling_kernel,
        shaped(64, 768),
        [scalars],
        [chain_skeletons, received, from_x, tops, chain],
        "coupling",
        after=[near],
    )
    far = (low, high, mine, other)

    def operate(extended, outgoing):
        moved = to_group(extended)
        low, wide = call(
            middle_kernel,
            (shaped(16, 128), shaped(16, 32, 128)),
            [scalars],
            [over_z(outgoing), chain],
            "middle",
        )
        near = near_product(scalars, [extended, *moved], kernels)
        high, mine, other = gather(over_yx(wide), [near])
        return low, high, mine, other, table, bases, near

    row = shaped(16, 1024)
    long = shaped(16, 1152)
    thin = shaped(16, 128)
    wire = shaped(8, 32, 128)
    v1, outgoing = call(
        first_kernel,
        (long, wire),
        [],
        [*far, table, bases, near, chain],
        "first",
    )
    v2, scaled, sums, outgoing = call(
        second_kernel, (row, long, thin, wire), [], [*operate(v1, outgoing), chain], "second"
    )
    image, step, outgoing = call(
        third_kernel,
        (long, thin, wire),
        [],
        [*operate(scaled, outgoing), chain, v1, sums],
        "third",
    )
    along, fresh, outgoing = call(
        fourth_kernel,
        (row, thin, shaped(32, 8, 128)),
        [],
        [*operate(image, outgoing), v2, sums],
        "fourth",
    )
    received = lax.all_to_all(outgoing, ("x", "z"), 0, 0)
    wide = call(spread_kernel, shaped(8, 8, 128), [], [received], "spread")
    shares = lax.all_to_all(wide, ("y", "core"), 0, 0)
    return call(
        last_kernel,
        (row, row),
        [],
        [shares, rhs, v1, v2, image, along, sums, fresh, step],
        "last",
    )


def solution(mesh):
    axes = ("y", "core", "x", "z")
    fine = Mesh(mesh.devices.reshape(4, 2, 4, 8), axes)
    placed = (
        P(None, axes),
        P(None, axes),
        P(axes, None),
        P(None, axes),
        P(None, axes, None, None),
        P(None, axes, None, None),
        P(),
        P(axes, None),
        P(None, axes),
        P(),
    )
    return jax.shard_map(
        local,
        mesh=fine,
        in_specs=placed,
        out_specs=(P(None, axes), P(None, axes)),
        check_vma=False,
    )
```

```python
import functools
import math

import jax
import jax.numpy as jnp
from jax import lax
from jax.experimental import pallas as pl
from jax.experimental.pallas import tpu as pltpu
from jax.sharding import Mesh
from jax.sharding import PartitionSpec as P

F32 = jnp.float32
BF16 = jnp.bfloat16
HIGHEST = lax.Precision.HIGHEST
NOISE = 0.5
SCALE = math.sqrt(5.0) / 2.8
LOG2E = math.log2(math.e)
DEPTH = 208
TILE = 256

Z, X, Y, CORE, O0, O1, O2, O3, TOPS = range(9)


def dot(a, b, ca=1, cb=0, precision=None):
    return lax.dot_general(
        a, b, (((ca,), (cb,)), ((), ())), precision=precision, preferred_element_type=F32
    )


def split(a):
    high = a.astype(BF16)
    return high, (a - high.astype(F32)).astype(BF16)


def stacked(a):
    return jnp.concatenate(split(a), axis=0)


def halves(a):
    n = a.shape[0] // 2
    return a[:n] + a[n:]


def paired(a, axis):
    return jnp.concatenate(split(a), axis=axis)


def times(a, pair):
    both = halves(dot(stacked(a), pair))
    n = both.shape[1] // 2
    return both[:, :n] + both[:, n:]


def times_t(a, pair):
    both = halves(dot(stacked(a), pair, 1, 1))
    n = both.shape[1] // 2
    return both[:, :n] + both[:, n:]


def square_sum(v):
    return jnp.broadcast_to(jnp.sum(v * v, axis=1, keepdims=True), (v.shape[0], 64))


def moments(v, bases, chain):
    own = times_t(v, bases)
    lifted = times(own, chain)
    return jnp.concatenate([own, lifted[:, 0:64]], axis=1), lifted[:, 64:192], lifted[:, 192:256]


def write_moments(extended, out, v, weighed, bases, chain):
    own, middle, top = moments(v, bases[...], chain[...])
    extended[:, 0 : v.shape[1]] = v
    extended[:, v.shape[1] :] = own
    last = jnp.concatenate([top, square_sum(weighed)], axis=1)
    for i in range(out.shape[0]):
        out[i, 0:16, :] = middle
        out[i, 16:32, :] = last


def packed(skeleton):
    return jnp.concatenate([skeleton[0:32], skeleton[32:64]], axis=1)


def unpacked(block):
    return jnp.concatenate([block[:, 0:64], block[:, 64:128]], axis=0)


def skeleton_offsets(scalars):
    o0, o1 = scalars[O0], scalars[O1]
    second = jnp.where(o1 > 1, o1 * 2, jnp.where(o0 == 2, 3, 2))
    return o0, second, jnp.where(o1 == 3, 4, 7)


def prepare_kernel(
    scalars, order, basis, maps, skeletons, rhs, points, bases, chain, tail, wire, all_rows
):
    all_rows[0:64, :] = points[...]
    all_rows[64:80, :] = rhs[...]
    both = stacked(basis[...])
    leaf = basis.shape[1]
    for t in range(leaf // TILE):
        rows = lax.broadcasted_iota(jnp.int32, (TILE, leaf), 0) + t * TILE
        one_hot = jnp.where(rows == order[...], 1.0, 0.0).astype(BF16)
        bases[:, t * TILE : (t + 1) * TILE] = dot(both, one_hot, 1, 1).astype(BF16)
    p1 = maps[0]
    p2 = dot(p1, maps[1], precision=HIGHEST)
    p3 = dot(p2, maps[2], precision=HIGHEST)
    e34 = dot(maps[3], maps[4], precision=HIGHEST)
    p5 = dot(p3, e34, precision=HIGHEST)
    tail[...] = e34
    chain[...] = paired(jnp.concatenate([p1, p2, p3, p5], axis=1), 1)
    own, middle, _ = moments(rhs[...], bases[...], chain[...])
    _, k1, k2 = skeleton_offsets(scalars)
    blocks = [packed(skeletons[h]) for h in range(3)]
    for i in range(wire.shape[0]):
        offset = jnp.bitwise_xor(scalars[Z], i)
        wire[i, 0:16, :] = own
        wire[i, 16:32, :] = middle
        block = jnp.where(offset == k1, blocks[1], blocks[0])
        wire[i, 32:64, :] = jnp.where(offset == k2, blocks[2], block)


def middle_kernel(scalars, received, tail, skeletons, after, low, out, second):
    z, o0, o1, o2 = scalars[Z], scalars[O0], scalars[O1], scalars[O2]
    left = lax.broadcasted_iota(jnp.int32, (16, 128), 1) < 64
    sums = [jnp.zeros((16, 128), F32) for _ in range(2)]
    for i in range(received.shape[0]):
        offset = jnp.bitwise_xor(z, i)
        hit0 = offset == o0
        hit1 = offset // 2 == o1
        hit2 = offset // 4 == jnp.bitwise_and(o2, 1)
        sums[0] += jnp.where((left & hit0) | (~left & hit1), received[i, 0:16, :], 0.0)
        sums[1] += jnp.where(~left | hit2, received[i, 16:32, :], 0.0)
    low[...] = sums[0]
    top = dot(sums[1][:, 64:128], tail[...], precision=HIGHEST)
    last = jnp.concatenate([top, jnp.zeros_like(top)], axis=1)
    for i in range(out.shape[0]):
        out[i, 0:16, :] = sums[1]
        out[i, 16:32, :] = last
        out[i, 32:64, :] = packed(skeletons[3])
    k2 = skeleton_offsets(scalars)[2]
    across = received[jnp.bitwise_xor(z, k2), 32:64, :]
    second[...] = jnp.where(o2 % 2 == 1, across, packed(skeletons[2]))


def matern(first, second):
    turned = first.T
    squares = (
        jnp.sum(turned * turned, axis=1, keepdims=True)
        + jnp.sum(second * second, axis=0, keepdims=True)
        - 2.0 * dot(turned, second, precision=HIGHEST)
    )
    s = SCALE * jnp.sqrt(jnp.maximum(squares, 0.0))
    return (1.0 + s + s * s * (1.0 / 3.0)) * jnp.exp(-s)


def top_kernel(scalars, skeletons, from_yx, tops, tail, out):
    x, y, core = scalars[X], scalars[Y], scalars[CORE]
    partner = unpacked(from_yx[y * 4 + jnp.bitwise_xor(x, scalars[O3]), 32:64, :])
    others = []
    masks = []
    for flip in (0, 1):
        for j in range(4):
            side = jnp.bitwise_xor(core, flip)
            others.append(tops[j, side])
            hits = sum((scalars[TOPS + k] == j * 2 + side).astype(F32) for k in range(4))
            masks.append(jnp.full((64, 64), hits, F32))
    top = matern(tops[y, core], jnp.concatenate(others, axis=1))
    top = dot(tail[...], top * jnp.concatenate(masks, axis=1), precision=HIGHEST)
    out[...] = paired(jnp.concatenate([matern(skeletons[3], partner), top], axis=1), 0)


def low_couplings(scalars, skeletons, from_z, second, chain):
    z = scalars[Z]
    k0, k1, _ = skeleton_offsets(scalars)
    down = chain[:, 0:256].astype(F32) + chain[:, 256:512].astype(F32)
    partners = [from_z[jnp.bitwise_xor(z, k), 32:64, :] for k in (k0, k1)] + [second]
    pieces = []
    for h in range(3):
        coupling = matern(skeletons[h], unpacked(partners[h]))
        if h > 0:
            coupling = dot(down[:, (h - 1) * 64 : h * 64], coupling, precision=HIGHEST)
        pieces.append(coupling)
    return paired(jnp.concatenate(pieces + [down[:, 128:192]], axis=1), 0)


def three(a):
    high = a.astype(BF16).astype(F32)
    middle = (a - high).astype(BF16).astype(F32)
    return high, middle, a - high - middle


def augment(points, target, turned):
    leaf = points.shape[1]
    high, low = split(points * SCALE)
    h32, l32 = high.astype(F32), low.astype(F32)
    sums = three(jnp.sum(h32 * h32 + 2.0 * (h32 * l32), axis=0, keepdims=True))
    row = lax.broadcasted_iota(jnp.int32, (16, leaf), 0)
    first, ones = (0, 3) if turned else (3, 0)
    rest = jnp.where((row >= ones) & (row < ones + 3), 1.0, 0.0)
    for i in range(3):
        rest = jnp.where(row == first + i, sums[i], rest)
    if turned:
        high, low = (-2.0 * h32).astype(BF16), (-2.0 * l32).astype(BF16)
    target[0:64, :] = high
    target[64:128, :] = high if turned else low
    target[128:192, :] = low if turned else high
    target[192:208, :] = rest.astype(BF16)


def entries(squares, kernel):
    wide = 512
    tall = 32
    for r in range(0, squares.shape[0], tall):
        for c in range(0, squares.shape[1], wide):
            s2 = jnp.maximum(squares[r : r + tall, c : c + wide], 1e-30)
            s = s2 * lax.rsqrt(s2)
            value = (1.0 + s + s2 * (1.0 / 3.0)) * jnp.exp2(s * -LOG2E)
            high, low = split(value)
            kernel[0, r : r + tall, c : c + wide] = high
            kernel[1, r : r + tall, c : c + wide] = low


def build_kernel(scalars, own, *refs, choice):
    if choice is None:
        begin, after, whole, near, aug, left, squares, kernel, sems = refs
        both = own[...]
        near[...] = NOISE * begin[...]
        slot = 0
    else:
        yes, no, begin, after, previous, whole, near, aug, left, squares, kernel, sems = refs
        both = jnp.where(scalars[O0] == choice, yes[...], no[...])
        near[...] = begin[...]
        slot = (choice + 1) // 2
    augment(own[0:64, :], aug, False)
    augment(both[0:64, :], left, True)
    pair = stacked(both[64:80, :])
    leaf = own.shape[1]
    tiles = leaf // TILE
    copies = []
    total = None
    squares[0] = dot(left[:, 0:TILE], aug[...], 0, 0)
    for t in range(tiles):
        cols = slice(t * TILE, (t + 1) * TILE)
        if t + 1 < tiles:
            squares[(t + 1) % 2] = dot(left[:, (t + 1) * TILE : (t + 2) * TILE], aug[...], 0, 0)
        entries(squares.at[t % 2], kernel.at[t])
        part = dot(pair[:, cols], kernel[t, 0]) + dot(pair[:, cols], kernel[t, 1])
        total = part if total is None else total + part
        rows = pl.ds(t * TILE, TILE)
        copies.append(
            pltpu.make_async_copy(kernel.at[t], whole.at[slot, :, rows, :], sems.at[t])
        )
        copies[t].start()
    near[...] += halves(total)
    for copy in copies:
        copy.wait()


def near_kernel(scalars, v, v1, v2, v3, kernels, after, out, held, sems):
    leaf = kernels.shape[2]
    tiles = leaf // TILE
    copies = []
    for e in range(3):
        for t in range(tiles):
            rows = pl.ds(t * TILE, TILE)
            copies.append(
                pltpu.make_async_copy(
                    kernels.at[e, :, rows, :], held.at[e, :, rows, :], sems.at[e * tiles + t]
                )
            )
    for copy in copies:
        copy.start()
    o0 = scalars[O0]
    own = v[:, 0:leaf]
    second = jnp.where(o0 == 1, v2[:, 0:leaf], v1[:, 0:leaf])
    third = jnp.where(o0 == 3, v2[:, 0:leaf], v3[:, 0:leaf])
    total = None
    for e, vector in enumerate((own, second, third)):
        pair = stacked(vector)
        for t in range(tiles):
            rows = slice(t * TILE, (t + 1) * TILE)
            copies[e * tiles + t].wait()
            part = dot(pair[:, rows], held[e, 0, rows, :]) + dot(pair[:, rows], held[e, 1, rows, :])
            total = part if total is None else total + part
    out[:, 0:leaf] = NOISE * own + halves(total)
    out[:, leaf:] = jnp.where(
        o0 == 1, v1[:, leaf:], jnp.where(o0 == 2, v2[:, leaf:], v3[:, leaf:])
    )


def gather_kernel(scalars, received, *refs):
    high, out = refs[-2:]
    x, y, o2, o3 = scalars[X], scalars[Y], scalars[O2], scalars[O3]
    left = lax.broadcasted_iota(jnp.int32, (16, 128), 1) < 64
    total = jnp.zeros((16, 128), F32)
    for j in range(4):
        top = jnp.zeros((16, 128), F32)
        for i in range(4):
            p = j * 4 + i
            offset = jnp.bitwise_xor(x, i)
            here = y == j
            hit2 = here & (offset == o2 // 2)
            hit3 = here & (offset == o3)
            total += jnp.where((left & hit2) | (~left & hit3), received[p, 0:16, :], 0.0)
            top += received[p, 16:32, :]
        out[j * 16 : (j + 1) * 16, :] = top
    high[...] = total


def field_at_three(high, mine, other, table):
    parts = [high[:, 64:128]]
    for side in (mine, other):
        parts += [side[j * 16 : (j + 1) * 16, 0:64] for j in range(4)]
    return times_t(jnp.concatenate(parts, axis=1), table[...])


def lower_kernel(high, mine, other, table, own, *refs):
    out = refs[-1]
    start = own.shape[1] - 128
    field = field_at_three(high, mine, other, table)
    norm = sum(side[j * 16 : (j + 1) * 16, 64:128] for side in (mine, other) for j in range(4))
    first = jnp.concatenate([field, norm], axis=1)
    second = jnp.concatenate([own[:, start + 64 :], high[:, 0:64]], axis=1)
    for i in range(out.shape[0]):
        out[i, 0:16, :] = first
        out[i, 16:32, :] = second


def add_far(moments_in, table, bases, near):
    pair = stacked(times_t(moments_in, table[...]))
    far = halves(dot(pair, bases[0:64, :]) + dot(pair, bases[64:128, :]))
    return near[:, 0 : far.shape[1]] + far


def apply_far(scalars, received, table, bases, near):
    leaf = bases.shape[1]
    z, o1, o2 = scalars[Z], scalars[O1], scalars[O2]
    left = lax.broadcasted_iota(jnp.int32, (16, 128), 1) < 64
    sums = [jnp.zeros((16, 128), F32) for _ in range(2)]
    for i in range(received.shape[0]):
        offset = jnp.bitwise_xor(z, i)
        hit1 = offset // 2 == o1
        hit2 = offset // 4 == jnp.bitwise_and(o2, 1)
        sums[0] += received[i, 0:16, :]
        sums[1] += jnp.where((left & hit1) | (~left & hit2), received[i, 16:32, :], 0.0)
    parts = [near[:, leaf : leaf + 64], sums[1], sums[0][:, 0:64]]
    return add_far(jnp.concatenate(parts, axis=1), table, bases, near), sums[0][:, 64:65]


def first_kernel(
    scalars,
    low,
    high,
    mine,
    other,
    top_table,
    from_z,
    second,
    moved,
    skeletons,
    bases,
    near,
    chain,
    table,
    v1,
    out,
):
    across = jnp.where(scalars[O2] > 1, moved[...], second[...])
    table[...] = low_couplings(scalars, skeletons, from_z, across, chain)
    field = field_at_three(high, mine, other, top_table)
    parts = [low[...], high[:, 0:64], field]
    image = add_far(jnp.concatenate(parts, axis=1), table, bases, near)
    write_moments(v1, out, image, image, bases, chain)


def second_kernel(scalars, received, table, bases, near, chain, v2, scaled, sums, out):
    image, norm = apply_far(scalars, received, table, bases, near)
    v2[...] = image
    sums[...] = jnp.broadcast_to(norm, sums.shape)
    write_moments(scaled, out, image / jnp.sqrt(norm), image, bases, chain)


def third_kernel(scalars, received, table, bases, near, chain, v1, sums, image, step, out):
    product, along = apply_far(scalars, received, table, bases, near)
    norm = sums[:, 0:1]
    size = norm / along
    new = v1[:, 0 : product.shape[1]] - (size * jnp.sqrt(norm)) * product
    step[...] = jnp.broadcast_to(size, step.shape)
    write_moments(image, out, new, new, bases, chain)


def diagonal():
    rows = lax.broadcasted_iota(jnp.int32, (16, 128), 0)
    return rows == lax.broadcasted_iota(jnp.int32, (16, 128), 1)


def fourth_kernel(scalars, received, table, bases, near, v2, sums, along, fresh, out):
    product, norm = apply_far(scalars, received, table, bases, near)
    new = product + (norm / sums[:, 0:1]) * v2[...]
    along[...] = new
    fresh[...] = jnp.broadcast_to(norm, fresh.shape)
    share = jnp.sum(new * new, axis=1, keepdims=True)
    line = jnp.sum(jnp.where(diagonal(), share, 0.0), axis=0, keepdims=True)
    for i in range(out.shape[0]):
        out[i] = jnp.broadcast_to(line, (8, 128))


def spread_kernel(received, out):
    total = received[0]
    for i in range(1, received.shape[0]):
        total = total + received[i]
    for i in range(out.shape[0]):
        out[i] = total


def last_kernel(shares, rhs, v1, v2, image, along, sums, fresh, step, iterate, residual):
    leaf = rhs.shape[1]
    norm = fresh[:, 0:1]
    first = step[:, 0:1]
    line = sum(shares[i, 0:1, :] for i in range(shares.shape[0]))
    second = norm / jnp.sum(jnp.where(diagonal(), line, 0.0), axis=1, keepdims=True)
    beta = norm / sums[:, 0:1]
    start = v1[:, 0:leaf]
    iterate[...] = first * start + second * (image[:, 0:leaf] + beta * start)
    residual[...] = rhs[...] - first * v2[...] - second * along[...]


SMEM = pl.BlockSpec(memory_space=pltpu.SMEM)
VMEM = pl.BlockSpec(memory_space=pltpu.VMEM)


def shaped(*shape, dtype=F32):
    return jax.ShapeDtypeStruct(shape, dtype)


MIB = 1024 * 1024
ANY = pl.BlockSpec(memory_space=pl.ANY)


def call(kernel, outs, scalars, arrays, name, after=(), limit=16, flops=100000, scratch=(), alias=None):
    return pl.pallas_call(
        kernel,
        out_shape=outs,
        in_specs=[SMEM] * len(scalars) + [VMEM] * len(arrays) + [ANY] * len(after),
        out_specs=jax.tree.map(lambda a: VMEM if len(a.shape) < 4 else ANY, outs),
        scratch_shapes=list(scratch),
        input_output_aliases=alias or {},
        name=name,
        compiler_params=pltpu.CompilerParams(vmem_limit_bytes=limit * MIB),
        cost_estimate=pl.CostEstimate(flops=flops, bytes_accessed=500000, transcendentals=0),
    )(*scalars, *arrays, *after)


def build(scalars, own, others, choice, near, after, name, kernels=()):
    leaf = own.shape[1]
    tiles = leaf // TILE
    return call(
        functools.partial(build_kernel, choice=choice),
        (shaped(3, 2, leaf, leaf, dtype=BF16), shaped(16, leaf)),
        [scalars],
        [own, *others, near],
        name,
        after=[*after, *kernels],
        limit=50,
        flops=4000000000,
        alias={3 + len(others) + len(after): 0} if kernels else None,
        scratch=[
            pltpu.VMEM((DEPTH, leaf), BF16),
            pltpu.VMEM((DEPTH, leaf), BF16),
            pltpu.VMEM((2, TILE, leaf), F32),
            pltpu.VMEM((tiles, 2, TILE, leaf), BF16),
            pltpu.SemaphoreType.DMA((tiles,)),
        ],
    )


def near_product(scalars, vectors, kernels, after):
    leaf = kernels.shape[2]
    return call(
        near_kernel,
        shaped(*vectors[0].shape),
        [scalars],
        vectors,
        "near",
        after=[kernels, after],
        limit=50,
        flops=4000000000,
        scratch=[
            pltpu.VMEM((3, 2, leaf, leaf), BF16),
            pltpu.SemaphoreType.DMA((3 * leaf // TILE,)),
        ],
    )


def along_z(v, offset):
    return lax.ppermute(v, "z", [(i, i ^ offset) for i in range(8)])


def other_core(v):
    return lax.ppermute(v, "core", [(0, 1), (1, 0)])


def over_z(v):
    return lax.all_to_all(v, "z", 0, 0)


def over_yx(v):
    return lax.all_to_all(v, ("y", "x"), 0, 0)


def local(
    rhs,
    embeddings,
    leaf_order,
    basis,
    transfer_maps,
    skeletons,
    top_skeletons,
    near_lists,
    far_lists,
    top_lists,
):
    y, core, x, z = (lax.axis_index(a) for a in ("y", "core", "x", "z"))
    top = y * 2 + core
    leaf = top * 32 + x * 8 + z
    offsets = jnp.bitwise_xor(
        far_lists[:, 0], jnp.right_shift(leaf, jnp.arange(4, dtype=jnp.int32))
    )
    partners = lax.dynamic_index_in_dim(top_lists, top, 0, keepdims=False)
    scalars = jnp.concatenate([jnp.stack([z, x, y, core]), offsets, partners]).astype(jnp.int32)
    chain_skeletons = skeletons[:, 0]
    tops = top_skeletons.reshape(4, 2, 64, 64)

    row = shaped(16, 1024)
    long = shaped(16, 1152)
    thin = shaped(16, 128)
    wire = shaped(16, 32, 128)
    bases, chain, tail, outgoing, both = call(
        prepare_kernel,
        (
            shaped(128, 1024, dtype=BF16),
            shaped(64, 512, dtype=BF16),
            shaped(64, 64),
            shaped(8, 64, 128),
            shaped(80, 1024),
        ),
        [scalars],
        [leaf_order, basis, transfer_maps[:, 0], chain_skeletons, rhs, embeddings],
        "prepare",
        limit=60,
    )

    def gather(spread, after=()):
        high, mine = call(
            gather_kernel, (thin, shaped(64, 128)), [scalars], [spread], "gather", after=after
        )
        return high, mine, other_core(mine)

    one = along_z(both, 1)
    two = along_z(both, 2)
    three_off = along_z(two, 1)
    from_z = over_z(outgoing)
    kernels, near = build(scalars, both, [], None, rhs, [chain], "build_own")
    low, outgoing, second = call(
        middle_kernel,
        (thin, shaped(16, 64, 128), shaped(32, 128)),
        [scalars],
        [from_z, tail, chain_skeletons],
        "middle",
        after=[near],
    )
    from_yx = over_yx(outgoing)
    moved = lax.ppermute(second, "x", [(i, i ^ 1) for i in range(4)])
    kernels, near = build(scalars, both, [two, one], 1, near, [low], "build_a", [kernels])
    spread = gather(from_yx, [near])
    top_table = call(
        top_kernel,
        shaped(128, 576, dtype=BF16),
        [scalars],
        [chain_skeletons, from_yx, tops, tail],
        "tops",
    )
    kernels, near = build(scalars, both, [two, three_off], 3, near, [low], "build_b", [kernels])
    table, v1, outgoing = call(
        first_kernel,
        (shaped(128, 256, dtype=BF16), long, wire),
        [scalars],
        [low, *spread, top_table, from_z, second, moved, chain_skeletons, bases, near, chain],
        "first",
    )

    def operate(extended, outgoing):
        moved = [along_z(extended, o) for o in (1, 2, 3)]
        spread = gather(over_yx(outgoing))
        lower = call(
            lower_kernel,
            shaped(8, 32, 128),
            [],
            [*spread, top_table, extended],
            "lower",
            after=moved,
        )
        near = near_product(scalars, [extended, *moved], kernels, lower)
        return over_z(lower), table, bases, near

    v2, scaled, sums, outgoing = call(
        second_kernel, (row, long, thin, wire), [scalars], [*operate(v1, outgoing), chain], "second"
    )
    image, step, outgoing = call(
        third_kernel,
        (long, thin, wire),
        [scalars],
        [*operate(scaled, outgoing), chain, v1, sums],
        "third",
    )
    along, fresh, outgoing = call(
        fourth_kernel,
        (row, thin, shaped(32, 8, 128)),
        [scalars],
        [*operate(image, outgoing), v2, sums],
        "fourth",
    )
    received = lax.all_to_all(outgoing, ("x", "z"), 0, 0)
    wide = call(spread_kernel, shaped(8, 8, 128), [], [received], "spread")
    shares = lax.all_to_all(wide, ("y", "core"), 0, 0)
    return call(
        last_kernel,
        (row, row),
        [],
        [shares, rhs, v1, v2, image, along, sums, fresh, step],
        "last",
    )


def solution(mesh):
    axes = ("y", "core", "x", "z")
    fine = Mesh(mesh.devices.reshape(4, 2, 4, 8), axes)
    placed = (
        P(None, axes),
        P(None, axes),
        P(axes, None),
        P(None, axes),
        P(None, axes, None, None),
        P(None, axes, None, None),
        P(),
        P(axes, None),
        P(None, axes),
        P(),
    )
    return jax.shard_map(
        local,
        mesh=fine,
        in_specs=placed,
        out_specs=(P(None, axes), P(None, axes)),
        check_vma=False,
    )
```

```python
import functools
import math

import jax
import jax.numpy as jnp
from jax import lax
from jax.experimental import pallas as pl
from jax.experimental.pallas import tpu as pltpu
from jax.sharding import Mesh
from jax.sharding import PartitionSpec as P

F32 = jnp.float32
BF16 = jnp.bfloat16
HIGHEST = lax.Precision.HIGHEST
NOISE = 0.5
SCALE = math.sqrt(5.0) / 2.8
LOG2E = math.log2(math.e)
DEPTH = 208
TILE = 256

Z, X, Y, CORE, O0, O1, O2, O3 = range(8)


def dot(a, b, ca=1, cb=0, precision=None):
    return lax.dot_general(
        a, b, (((ca,), (cb,)), ((), ())), precision=precision, preferred_element_type=F32
    )


def split(a):
    high = a.astype(BF16)
    return high, (a - high.astype(F32)).astype(BF16)


def stacked(a):
    return jnp.concatenate(split(a), axis=0)


def halves(a):
    n = a.shape[0] // 2
    return a[:n] + a[n:]


def places(partners):
    y, core, x, z = (lax.axis_index(a) for a in ("y", "core", "x", "z"))
    leaf = ((y * 2 + core) * 4 + x) * 8 + z
    return [z, x, y, core] + [jnp.bitwise_xor(partners[h], leaf // 2**h) for h in range(4)]


def paired(a, axis):
    return jnp.concatenate(split(a), axis=axis)


def times(a, pair):
    both = halves(dot(stacked(a), pair))
    n = both.shape[1] // 2
    return both[:, :n] + both[:, n:]


def times_t(a, pair):
    both = halves(dot(stacked(a), pair, 1, 1))
    n = both.shape[1] // 2
    return both[:, :n] + both[:, n:]


def square_sum(v):
    return jnp.broadcast_to(jnp.sum(v * v, axis=1, keepdims=True), (v.shape[0], 64))


def moments(v, bases, chain):
    own = times_t(v, bases)
    lifted = times(own, chain)
    return jnp.concatenate([own, lifted[:, 0:64]], axis=1), lifted[:, 64:192], lifted[:, 192:256]


def write_moments(extended, out, v, weighed, bases, chain):
    own, middle, top = moments(v, bases[...], chain[...])
    extended[:, 0 : v.shape[1]] = v
    extended[:, v.shape[1] :] = own
    last = jnp.concatenate([top, square_sum(weighed)], axis=1)
    for i in range(out.shape[0]):
        out[i, 0:16, :] = middle
        out[i, 16:32, :] = last


def packed(skeleton):
    return jnp.concatenate([skeleton[0:32], skeleton[32:64]], axis=1)


def unpacked(block):
    return jnp.concatenate([block[:, 0:64], block[:, 64:128]], axis=0)


def skeleton_offsets(scalars):
    o0, o1 = scalars[O0], scalars[O1]
    second = jnp.where(o1 > 1, o1 * 2, jnp.where(o0 == 2, 3, 2))
    return o0, second, jnp.where(o1 == 3, 4, 7)


def prepare_kernel(scalars, order, basis, maps, skeletons, rhs, bases, chain, tail, wire):
    both = stacked(basis[...])
    leaf = basis.shape[1]
    for t in range(leaf // TILE):
        rows = lax.broadcasted_iota(jnp.int32, (TILE, leaf), 0) + t * TILE
        one_hot = jnp.where(rows == order[...], 1.0, 0.0).astype(BF16)
        bases[:, t * TILE : (t + 1) * TILE] = dot(both, one_hot, 1, 1).astype(BF16)
    p1 = maps[0]
    p2 = dot(p1, maps[1], precision=HIGHEST)
    p3 = dot(p2, maps[2], precision=HIGHEST)
    e34 = dot(maps[3], maps[4], precision=HIGHEST)
    p5 = dot(p3, e34, precision=HIGHEST)
    tail[...] = e34
    chain[...] = paired(jnp.concatenate([p1, p2, p3, p5], axis=1), 1)
    own, middle, _ = moments(rhs[...], bases[...], chain[...])
    _, k1, k2 = skeleton_offsets(scalars)
    blocks = [packed(skeletons[h]) for h in range(3)]
    for i in range(wire.shape[0]):
        offset = jnp.bitwise_xor(scalars[Z], i)
        wire[i, 0:16, :] = own
        wire[i, 16:32, :] = middle
        block = jnp.where(offset == k1, blocks[1], blocks[0])
        wire[i, 32:64, :] = jnp.where(offset == k2, blocks[2], block)


def middle_kernel(scalars, received, tail, skeletons, after, low, out, second):
    z, o0, o1, o2 = scalars[Z], scalars[O0], scalars[O1], scalars[O2]
    left = lax.broadcasted_iota(jnp.int32, (16, 128), 1) < 64
    sums = [jnp.zeros((16, 128), F32) for _ in range(2)]
    for i in range(received.shape[0]):
        offset = jnp.bitwise_xor(z, i)
        hit0 = offset == o0
        hit1 = offset // 2 == o1
        hit2 = offset // 4 == jnp.bitwise_and(o2, 1)
        sums[0] += jnp.where((left & hit0) | (~left & hit1), received[i, 0:16, :], 0.0)
        sums[1] += jnp.where(~left | hit2, received[i, 16:32, :], 0.0)
    low[...] = sums[0]
    top = dot(sums[1][:, 64:128], tail[...], precision=HIGHEST)
    last = jnp.concatenate([top, jnp.zeros_like(top)], axis=1)
    for i in range(out.shape[0]):
        out[i, 0:16, :] = sums[1]
        out[i, 16:32, :] = last
        out[i, 32:64, :] = packed(skeletons[3])
    k2 = skeleton_offsets(scalars)[2]
    across = received[jnp.bitwise_xor(z, k2), 32:64, :]
    second[...] = jnp.where(o2 % 2 == 1, across, packed(skeletons[2]))


def matern(first, second):
    turned = first.T
    squares = (
        jnp.sum(turned * turned, axis=1, keepdims=True)
        + jnp.sum(second * second, axis=0, keepdims=True)
        - 2.0 * dot(turned, second, precision=HIGHEST)
    )
    s = SCALE * jnp.sqrt(jnp.maximum(squares, 0.0))
    return (1.0 + s + s * s * (1.0 / 3.0)) * jnp.exp(-s)


def top_kernel(scalars, listed, skeletons, from_yx, tops, tail, out):
    x, y, core = scalars[X], scalars[Y], scalars[CORE]
    partner = unpacked(from_yx[y * 4 + jnp.bitwise_xor(x, scalars[O3]), 32:64, :])
    others = []
    masks = []
    for flip in (0, 1):
        for j in range(4):
            side = jnp.bitwise_xor(core, flip)
            others.append(tops[j, side])
            hits = sum((listed[k] == j * 2 + side).astype(F32) for k in range(4))
            masks.append(jnp.full((64, 64), hits, F32))
    top = matern(tops[y, core], jnp.concatenate(others, axis=1))
    top = dot(tail[...], top * jnp.concatenate(masks, axis=1), precision=HIGHEST)
    out[...] = paired(jnp.concatenate([matern(skeletons[3], partner), top], axis=1), 0)


def low_kernel(scalars, skeletons, from_z, second, moved, chain, out):
    z = scalars[Z]
    second = jnp.where(scalars[O2] > 1, moved[...], second[...])
    k0, k1, _ = skeleton_offsets(scalars)
    down = chain[:, 0:256].astype(F32) + chain[:, 256:512].astype(F32)
    partners = [from_z[jnp.bitwise_xor(z, k), 32:64, :] for k in (k0, k1)] + [second]
    pieces = []
    for h in range(3):
        coupling = matern(skeletons[h], unpacked(partners[h]))
        if h > 0:
            coupling = dot(down[:, (h - 1) * 64 : h * 64], coupling, precision=HIGHEST)
        pieces.append(coupling)
    out[...] = paired(jnp.concatenate(pieces + [down[:, 128:192]], axis=1), 0)


def three(a):
    high = a.astype(BF16).astype(F32)
    middle = (a - high).astype(BF16).astype(F32)
    return high, middle, a - high - middle


def augment(points, target, turned):
    leaf = points.shape[1]
    high, low = split(points * SCALE)
    h32, l32 = high.astype(F32), low.astype(F32)
    sums = three(jnp.sum(h32 * h32 + 2.0 * (h32 * l32), axis=0, keepdims=True))
    row = lax.broadcasted_iota(jnp.int32, (16, leaf), 0)
    first, ones = (0, 3) if turned else (3, 0)
    rest = jnp.where((row >= ones) & (row < ones + 3), 1.0, 0.0)
    for i in range(3):
        rest = jnp.where(row == first + i, sums[i], rest)
    if turned:
        high, low = (-2.0 * h32).astype(BF16), (-2.0 * l32).astype(BF16)
    target[0:64, :] = high
    target[64:128, :] = high if turned else low
    target[128:192, :] = low if turned else high
    target[192:208, :] = rest.astype(BF16)


def entries(squares, kernel):
    wide = 512
    tall = 32
    for r in range(0, squares.shape[0], tall):
        for c in range(0, squares.shape[1], wide):
            s2 = jnp.maximum(squares[r : r + tall, c : c + wide], 1e-30)
            s = s2 * lax.rsqrt(s2)
            value = (1.0 + s + s2 * (1.0 / 3.0)) * jnp.exp2(s * -LOG2E)
            high, low = split(value)
            kernel[0, r : r + tall, c : c + wide] = high
            kernel[1, r : r + tall, c : c + wide] = low


def build_kernel(scalars, own, *refs, choice):
    if choice is None:
        whole, near, aug, left, squares, kernel, sems = refs[-7:]
        both = own[...]
        near[...] = NOISE * own[64:80, :]
        slot = 0
    else:
        yes, no, begin = refs[:3]
        whole, near, aug, left, squares, kernel, sems = refs[-7:]
        both = jnp.where(scalars[O0] == choice, yes[...], no[...])
        near[...] = begin[...]
        slot = (choice + 1) // 2
    augment(own[0:64, :], aug, False)
    augment(both[0:64, :], left, True)
    pair = stacked(both[64:80, :])
    leaf = own.shape[1]
    tiles = leaf // TILE
    copies = []
    total = None
    squares[0] = dot(left[:, 0:TILE], aug[...], 0, 0)
    for t in range(tiles):
        cols = slice(t * TILE, (t + 1) * TILE)
        if t + 1 < tiles:
            squares[(t + 1) % 2] = dot(left[:, (t + 1) * TILE : (t + 2) * TILE], aug[...], 0, 0)
        entries(squares.at[t % 2], kernel.at[t])
        part = dot(pair[:, cols], kernel[t, 0]) + dot(pair[:, cols], kernel[t, 1])
        total = part if total is None else total + part
        rows = pl.ds(t * TILE, TILE)
        copies.append(
            pltpu.make_async_copy(kernel.at[t], whole.at[slot, :, rows, :], sems.at[t])
        )
        copies[t].start()
    near[...] += halves(total)
    for copy in copies:
        copy.wait()


def near_kernel(scalars, v, v1, v2, v3, kernels, after, out, held, sems):
    leaf = kernels.shape[2]
    tiles = leaf // TILE
    copies = []
    for e in range(3):
        for t in range(tiles):
            rows = pl.ds(t * TILE, TILE)
            copies.append(
                pltpu.make_async_copy(
                    kernels.at[e, :, rows, :], held.at[e, :, rows, :], sems.at[e * tiles + t]
                )
            )
    for copy in copies:
        copy.start()
    o0 = scalars[O0]
    own = v[:, 0:leaf]
    second = jnp.where(o0 == 1, v2[:, 0:leaf], v1[:, 0:leaf])
    third = jnp.where(o0 == 3, v2[:, 0:leaf], v3[:, 0:leaf])
    total = None
    for e, vector in enumerate((own, second, third)):
        pair = stacked(vector)
        for t in range(tiles):
            rows = slice(t * TILE, (t + 1) * TILE)
            copies[e * tiles + t].wait()
            part = dot(pair[:, rows], held[e, 0, rows, :]) + dot(pair[:, rows], held[e, 1, rows, :])
            total = part if total is None else total + part
    out[:, 0:leaf] = NOISE * own + halves(total)
    out[:, leaf:] = jnp.where(
        o0 == 1, v1[:, leaf:], jnp.where(o0 == 2, v2[:, leaf:], v3[:, leaf:])
    )


def gather_kernel(scalars, received, *refs):
    high, out = refs[-2:]
    x, y, o2, o3 = scalars[X], scalars[Y], scalars[O2], scalars[O3]
    left = lax.broadcasted_iota(jnp.int32, (16, 128), 1) < 64
    total = jnp.zeros((16, 128), F32)
    for j in range(4):
        top = jnp.zeros((16, 128), F32)
        for i in range(4):
            p = j * 4 + i
            offset = jnp.bitwise_xor(x, i)
            here = y == j
            hit2 = here & (offset == o2 // 2)
            hit3 = here & (offset == o3)
            total += jnp.where((left & hit2) | (~left & hit3), received[p, 0:16, :], 0.0)
            top += received[p, 16:32, :]
        out[j * 16 : (j + 1) * 16, :] = top
    high[...] = total


def field_at_three(high, mine, other, table):
    parts = [high[:, 64:128]]
    for side in (mine, other):
        parts += [side[j * 16 : (j + 1) * 16, 0:64] for j in range(4)]
    return times_t(jnp.concatenate(parts, axis=1), table[...])


def lower_kernel(high, mine, other, table, own, *refs):
    out = refs[-1]
    start = own.shape[1] - 128
    field = field_at_three(high, mine, other, table)
    norm = sum(side[j * 16 : (j + 1) * 16, 64:128] for side in (mine, other) for j in range(4))
    first = jnp.concatenate([field, norm], axis=1)
    second = jnp.concatenate([own[:, start + 64 :], high[:, 0:64]], axis=1)
    for i in range(out.shape[0]):
        out[i, 0:16, :] = first
        out[i, 16:32, :] = second


def add_far(moments_in, table, bases, near):
    pair = stacked(times_t(moments_in, table[...]))
    far = halves(dot(pair, bases[0:64, :]) + dot(pair, bases[64:128, :]))
    return near[:, 0 : far.shape[1]] + far


def apply_far(scalars, received, table, bases, near):
    leaf = bases.shape[1]
    z, o1, o2 = scalars[Z], scalars[O1], scalars[O2]
    left = lax.broadcasted_iota(jnp.int32, (16, 128), 1) < 64
    sums = [jnp.zeros((16, 128), F32) for _ in range(2)]
    for i in range(received.shape[0]):
        offset = jnp.bitwise_xor(z, i)
        hit1 = offset // 2 == o1
        hit2 = offset // 4 == jnp.bitwise_and(o2, 1)
        sums[0] += received[i, 0:16, :]
        sums[1] += jnp.where((left & hit1) | (~left & hit2), received[i, 16:32, :], 0.0)
    parts = [near[:, leaf : leaf + 64], sums[1], sums[0][:, 0:64]]
    return add_far(jnp.concatenate(parts, axis=1), table, bases, near), sums[0][:, 64:65]


def first_kernel(low, high, mine, other, top_table, table, bases, near, chain, v1, out):
    field = field_at_three(high, mine, other, top_table)
    parts = [low[...], high[:, 0:64], field]
    image = add_far(jnp.concatenate(parts, axis=1), table, bases, near)
    write_moments(v1, out, image, image, bases, chain)


def second_kernel(scalars, received, table, bases, near, chain, v2, scaled, sums, out):
    image, norm = apply_far(scalars, received, table, bases, near)
    v2[...] = image
    sums[...] = jnp.broadcast_to(norm, sums.shape)
    write_moments(scaled, out, image / jnp.sqrt(norm), image, bases, chain)


def third_kernel(scalars, received, table, bases, near, chain, v1, sums, image, step, out):
    product, along = apply_far(scalars, received, table, bases, near)
    norm = sums[:, 0:1]
    size = norm / along
    new = v1[:, 0 : product.shape[1]] - (size * jnp.sqrt(norm)) * product
    step[...] = jnp.broadcast_to(size, step.shape)
    write_moments(image, out, new, new, bases, chain)


def diagonal():
    rows = lax.broadcasted_iota(jnp.int32, (16, 128), 0)
    return rows == lax.broadcasted_iota(jnp.int32, (16, 128), 1)


def fourth_kernel(scalars, received, table, bases, near, v2, sums, along, fresh, out):
    product, norm = apply_far(scalars, received, table, bases, near)
    new = product + (norm / sums[:, 0:1]) * v2[...]
    along[...] = new
    fresh[...] = jnp.broadcast_to(norm, fresh.shape)
    share = jnp.sum(new * new, axis=1, keepdims=True)
    line = jnp.sum(jnp.where(diagonal(), share, 0.0), axis=0, keepdims=True)
    for i in range(out.shape[0]):
        out[i] = jnp.broadcast_to(line, (8, 128))


def spread_kernel(received, out):
    total = received[0]
    for i in range(1, received.shape[0]):
        total = total + received[i]
    for i in range(out.shape[0]):
        out[i] = total


def last_kernel(shares, rhs, v1, v2, image, along, sums, fresh, step, iterate, residual):
    leaf = rhs.shape[1]
    norm = fresh[:, 0:1]
    first = step[:, 0:1]
    line = sum(shares[i, 0:1, :] for i in range(shares.shape[0]))
    second = norm / jnp.sum(jnp.where(diagonal(), line, 0.0), axis=1, keepdims=True)
    beta = norm / sums[:, 0:1]
    start = v1[:, 0:leaf]
    iterate[...] = first * start + second * (image[:, 0:leaf] + beta * start)
    residual[...] = rhs[...] - first * v2[...] - second * along[...]


SMEM = pl.BlockSpec(memory_space=pltpu.SMEM)
VMEM = pl.BlockSpec(memory_space=pltpu.VMEM)


def shaped(*shape, dtype=F32):
    return jax.ShapeDtypeStruct(shape, dtype)


MIB = 1024 * 1024
ANY = pl.BlockSpec(memory_space=pl.ANY)


def call(kernel, outs, scalars, arrays, name, after=(), limit=16, flops=100000, scratch=(), alias=None):
    body = kernel
    if scalars:
        body = lambda far, *refs: kernel(places(far), *refs)
    return pl.pallas_call(
        body,
        out_shape=outs,
        in_specs=[SMEM] * len(scalars) + [VMEM] * len(arrays) + [ANY] * len(after),
        out_specs=jax.tree.map(lambda a: VMEM if len(a.shape) < 4 else ANY, outs),
        scratch_shapes=list(scratch),
        input_output_aliases=alias or {},
        name=name,
        compiler_params=pltpu.CompilerParams(vmem_limit_bytes=limit * MIB),
        cost_estimate=pl.CostEstimate(flops=flops, bytes_accessed=500000, transcendentals=0),
    )(*scalars, *arrays, *after)


def build(scalars, own, others, choice, near, after, name, kernels=()):
    leaf = own.shape[1]
    tiles = leaf // TILE
    return call(
        functools.partial(build_kernel, choice=choice),
        (shaped(3, 2, leaf, leaf, dtype=BF16), shaped(16, leaf)),
        [scalars],
        [own, *others, *([] if near is None else [near])],
        name,
        after=[*after, *kernels],
        limit=50,
        flops=4000000000,
        alias={3 + len(others) + len(after): 0} if kernels else None,
        scratch=[
            pltpu.VMEM((DEPTH, leaf), BF16),
            pltpu.VMEM((DEPTH, leaf), BF16),
            pltpu.VMEM((2, TILE, leaf), F32),
            pltpu.VMEM((tiles, 2, TILE, leaf), BF16),
            pltpu.SemaphoreType.DMA((tiles,)),
        ],
    )


def near_product(scalars, vectors, kernels, after):
    leaf = kernels.shape[2]
    return call(
        near_kernel,
        shaped(*vectors[0].shape),
        [scalars],
        vectors,
        "near",
        after=[kernels, after],
        limit=50,
        flops=4000000000,
        scratch=[
            pltpu.VMEM((3, 2, leaf, leaf), BF16),
            pltpu.SemaphoreType.DMA((3 * leaf // TILE,)),
        ],
    )


def along_z(v, offset):
    return lax.ppermute(v, "z", [(i, i ^ offset) for i in range(8)])


def other_core(v):
    return lax.ppermute(v, "core", [(0, 1), (1, 0)])


def over_z(v):
    return lax.all_to_all(v, "z", 0, 0)


def over_yx(v):
    return lax.all_to_all(v, ("y", "x"), 0, 0)


def local(
    rhs,
    embeddings,
    leaf_order,
    basis,
    transfer_maps,
    skeletons,
    top_skeletons,
    near_lists,
    far_lists,
    top_lists,
):
    top = lax.axis_index("y") * 2 + lax.axis_index("core")
    listed = lax.dynamic_index_in_dim(top_lists, top, 0, keepdims=False)
    scalars = far_lists[:, 0]
    chain_skeletons = skeletons[:, 0]
    tops = top_skeletons.reshape(4, 2, 64, 64)

    row = shaped(16, 1024)
    long = shaped(16, 1152)
    thin = shaped(16, 128)
    wire = shaped(16, 32, 128)
    both = jnp.concatenate([embeddings, rhs], axis=0)
    one = along_z(both, 1)
    two = along_z(both, 2)
    three_off = along_z(two, 1)
    bases, chain, tail, outgoing = call(
        prepare_kernel,
        (
            shaped(128, 1024, dtype=BF16),
            shaped(64, 512, dtype=BF16),
            shaped(64, 64),
            shaped(8, 64, 128),
        ),
        [scalars],
        [leaf_order, basis, transfer_maps[:, 0], chain_skeletons, rhs],
        "prepare",
        limit=60,
    )

    def gather(spread, after=()):
        high, mine = call(
            gather_kernel, (thin, shaped(64, 128)), [scalars], [spread], "gather", after=after
        )
        return high, mine, other_core(mine)

    from_z = over_z(outgoing)
    kernels, near = build(scalars, both, [], None, None, [two], "build_own")
    low, outgoing, second = call(
        middle_kernel,
        (thin, shaped(16, 64, 128), shaped(32, 128)),
        [scalars],
        [from_z, tail, chain_skeletons],
        "middle",
        after=[near],
    )
    from_yx = over_yx(outgoing)
    moved = lax.ppermute(second, "x", [(i, i ^ 1) for i in range(4)])
    kernels, near = build(
        scalars, both, [two, one], 1, near, [low, three_off], "build_a", [kernels]
    )
    kernels, near = build(scalars, both, [two, three_off], 3, near, [low], "build_b", [kernels])
    table = call(
        low_kernel,
        shaped(128, 256, dtype=BF16),
        [scalars],
        [chain_skeletons, from_z, second, moved, chain],
        "couplings",
    )
    spread = gather(from_yx, [near, table])
    top_table = call(
        top_kernel,
        shaped(128, 576, dtype=BF16),
        [scalars, listed],
        [chain_skeletons, from_yx, tops, tail],
        "tops",
    )
    v1, outgoing = call(
        first_kernel,
        (long, wire),
        [],
        [low, *spread, top_table, table, bases, near, chain],
        "first",
    )

    def operate(extended, outgoing):
        moved = [along_z(extended, o) for o in (1, 2, 3)]
        spread = gather(over_yx(outgoing))
        lower = call(
            lower_kernel,
            shaped(8, 32, 128),
            [],
            [*spread, top_table, extended],
            "lower",
            after=moved,
        )
        near = near_product(scalars, [extended, *moved], kernels, lower)
        return over_z(lower), table, bases, near

    v2, scaled, sums, outgoing = call(
        second_kernel, (row, long, thin, wire), [scalars], [*operate(v1, outgoing), chain], "second"
    )
    image, step, outgoing = call(
        third_kernel,
        (long, thin, wire),
        [scalars],
        [*operate(scaled, outgoing), chain, v1, sums],
        "third",
    )
    along, fresh, outgoing = call(
        fourth_kernel,
        (row, thin, shaped(32, 8, 128)),
        [scalars],
        [*operate(image, outgoing), v2, sums],
        "fourth",
    )
    received = lax.all_to_all(outgoing, ("x", "z"), 0, 0)
    wide = call(spread_kernel, shaped(8, 8, 128), [], [received], "spread")
    shares = lax.all_to_all(wide, ("y", "core"), 0, 0)
    return call(
        last_kernel,
        (row, row),
        [],
        [shares, rhs, v1, v2, image, along, sums, fresh, step],
        "last",
    )


def solution(mesh):
    axes = ("y", "core", "x", "z")
    fine = Mesh(mesh.devices.reshape(4, 2, 4, 8), axes)
    placed = (
        P(None, axes),
        P(None, axes),
        P(axes, None),
        P(None, axes),
        P(None, axes, None, None),
        P(None, axes, None, None),
        P(),
        P(axes, None),
        P(None, axes),
        P(),
    )
    return jax.shard_map(
        local,
        mesh=fine,
        in_specs=placed,
        out_specs=(P(None, axes), P(None, axes)),
        check_vma=False,
    )
```

```python
import functools
import math

import jax
import jax.numpy as jnp
from jax import lax
from jax.experimental import pallas as pl
from jax.experimental.pallas import tpu as pltpu
from jax.sharding import Mesh
from jax.sharding import PartitionSpec as P

F32 = jnp.float32
BF16 = jnp.bfloat16
HIGHEST = lax.Precision.HIGHEST
NOISE = 0.5
SCALE = math.sqrt(5.0) / 2.8
LOG2E = math.log2(math.e)
DEPTH = 208
TILE = 256

Z, X, Y, CORE, O0, O1, O2, O3 = range(8)


def dot(a, b, ca=1, cb=0, precision=None):
    return lax.dot_general(
        a, b, (((ca,), (cb,)), ((), ())), precision=precision, preferred_element_type=F32
    )


def split(a):
    high = a.astype(BF16)
    return high, (a - high.astype(F32)).astype(BF16)


def stacked(a):
    return jnp.concatenate(split(a), axis=0)


def halves(a):
    n = a.shape[0] // 2
    return a[:n] + a[n:]


def places(partners):
    y, core, x, z = (lax.axis_index(a) for a in ("y", "core", "x", "z"))
    leaf = ((y * 2 + core) * 4 + x) * 8 + z
    return [z, x, y, core] + [jnp.bitwise_xor(partners[h], leaf // 2**h) for h in range(4)]


def paired(a, axis):
    return jnp.concatenate(split(a), axis=axis)


def times(a, pair):
    both = halves(dot(stacked(a), pair))
    n = both.shape[1] // 2
    return both[:, :n] + both[:, n:]


def times_t(a, pair):
    both = halves(dot(stacked(a), pair, 1, 1))
    n = both.shape[1] // 2
    return both[:, :n] + both[:, n:]


def square_sum(v):
    return jnp.broadcast_to(jnp.sum(v * v, axis=1, keepdims=True), (v.shape[0], 64))


def moments(v, bases, chain):
    own = times_t(v, bases)
    lifted = times(own, chain)
    return jnp.concatenate([own, lifted[:, 0:64]], axis=1), lifted[:, 64:192], lifted[:, 192:256]


def write_moments(extended, out, v, weighed, bases, chain):
    own, middle, top = moments(v, bases[...], chain[...])
    extended[:, 0 : v.shape[1]] = v
    extended[:, v.shape[1] :] = own
    last = jnp.concatenate([top, square_sum(weighed)], axis=1)
    for i in range(out.shape[0]):
        out[i, 0:16, :] = middle
        out[i, 16:32, :] = last


def packed(skeleton):
    return jnp.concatenate([skeleton[0:32], skeleton[32:64]], axis=1)


def unpacked(block):
    return jnp.concatenate([block[:, 0:64], block[:, 64:128]], axis=0)


def skeleton_offsets(scalars):
    o0, o1 = scalars[O0], scalars[O1]
    second = jnp.where(o1 > 1, o1 * 2, jnp.where(o0 == 2, 3, 2))
    return o0, second, jnp.where(o1 == 3, 4, 7)


def prepare_kernel(
    scalars, order, basis, maps, skeletons, rhs, bases, chain, tail, own, wire, second
):
    both = stacked(basis[...])
    leaf = basis.shape[1]
    for t in range(leaf // TILE):
        rows = lax.broadcasted_iota(jnp.int32, (TILE, leaf), 0) + t * TILE
        one_hot = jnp.where(rows == order[...], 1.0, 0.0).astype(BF16)
        bases[:, t * TILE : (t + 1) * TILE] = dot(both, one_hot, 1, 1).astype(BF16)
    p1 = maps[0]
    p2 = dot(p1, maps[1], precision=HIGHEST)
    p3 = dot(p2, maps[2], precision=HIGHEST)
    e34 = dot(maps[3], maps[4], precision=HIGHEST)
    p5 = dot(p3, e34, precision=HIGHEST)
    tail[...] = e34
    chain[...] = paired(jnp.concatenate([p1, p2, p3, p5], axis=1), 1)
    first, middle, top = moments(rhs[...], bases[...], chain[...])
    own[...] = first
    last = jnp.concatenate([top, jnp.zeros_like(top)], axis=1)
    for i in range(wire.shape[0]):
        wire[i, 0:16, :] = middle
        wire[i, 16:32, :] = last
        wire[i, 32:64, :] = packed(skeletons[3])
    second[...] = packed(skeletons[2])


def matern(first, second):
    turned = first.T
    squares = (
        jnp.sum(turned * turned, axis=1, keepdims=True)
        + jnp.sum(second * second, axis=0, keepdims=True)
        - 2.0 * dot(turned, second, precision=HIGHEST)
    )
    s = SCALE * jnp.sqrt(jnp.maximum(squares, 0.0))
    return (1.0 + s + s * s * (1.0 / 3.0)) * jnp.exp(-s)


def top_kernel(scalars, listed, skeletons, from_yx, tops, tail, out):
    x, y, core = scalars[X], scalars[Y], scalars[CORE]
    partner = unpacked(from_yx[y * 4 + jnp.bitwise_xor(x, scalars[O3]), 32:64, :])
    others = []
    masks = []
    for flip in (0, 1):
        for j in range(4):
            side = jnp.bitwise_xor(core, flip)
            others.append(tops[j, side])
            hits = sum((listed[k] == j * 2 + side).astype(F32) for k in range(4))
            masks.append(jnp.full((64, 64), hits, F32))
    top = matern(tops[y, core], jnp.concatenate(others, axis=1))
    top = dot(tail[...], top * jnp.concatenate(masks, axis=1), precision=HIGHEST)
    out[...] = paired(jnp.concatenate([matern(skeletons[3], partner), top], axis=1), 0)


def low_couplings(scalars, skeletons, from_z, chain):
    z = scalars[Z]
    down = chain[:, 0:256].astype(F32) + chain[:, 256:512].astype(F32)
    pieces = []
    for h, offset in enumerate(skeleton_offsets(scalars)):
        if h == 2:
            offset = jnp.where(scalars[O2] % 2 == 1, offset, 0)
        partner = unpacked(from_z[jnp.bitwise_xor(z, offset), 48:80, :])
        coupling = matern(skeletons[h], partner)
        if h > 0:
            coupling = dot(down[:, (h - 1) * 64 : h * 64], coupling, precision=HIGHEST)
        pieces.append(coupling)
    return paired(jnp.concatenate(pieces + [down[:, 128:192]], axis=1), 0)


def three(a):
    high = a.astype(BF16).astype(F32)
    middle = (a - high).astype(BF16).astype(F32)
    return high, middle, a - high - middle


def augment(points, target, turned):
    leaf = points.shape[1]
    high, low = split(points * SCALE)
    h32, l32 = high.astype(F32), low.astype(F32)
    sums = three(jnp.sum(h32 * h32 + 2.0 * (h32 * l32), axis=0, keepdims=True))
    row = lax.broadcasted_iota(jnp.int32, (16, leaf), 0)
    first, ones = (0, 3) if turned else (3, 0)
    rest = jnp.where((row >= ones) & (row < ones + 3), 1.0, 0.0)
    for i in range(3):
        rest = jnp.where(row == first + i, sums[i], rest)
    if turned:
        high, low = (-2.0 * h32).astype(BF16), (-2.0 * l32).astype(BF16)
    target[0:64, :] = high
    target[64:128, :] = high if turned else low
    target[128:192, :] = low if turned else high
    target[192:208, :] = rest.astype(BF16)


def entries(squares, kernel):
    wide = 512
    tall = 32
    for r in range(0, squares.shape[0], tall):
        for c in range(0, squares.shape[1], wide):
            s2 = jnp.maximum(squares[r : r + tall, c : c + wide], 1e-30)
            s = s2 * lax.rsqrt(s2)
            value = (1.0 + s + s2 * (1.0 / 3.0)) * jnp.exp2(s * -LOG2E)
            high, low = split(value)
            kernel[0, r : r + tall, c : c + wide] = high
            kernel[1, r : r + tall, c : c + wide] = low


def build_kernel(scalars, own, *refs, choice):
    if choice is None:
        whole, near, aug, left, squares, kernel, sems = refs[-7:]
        both = own[...]
        near[...] = NOISE * own[64:80, :]
        slot = 0
    else:
        yes, no, begin = refs[:3]
        whole, near, aug, left, squares, kernel, sems = refs[-7:]
        both = jnp.where(scalars[O0] == choice, yes[...], no[...])
        near[...] = begin[...]
        slot = (choice + 1) // 2
    augment(own[0:64, :], aug, False)
    augment(both[0:64, :], left, True)
    pair = stacked(both[64:80, :])
    leaf = own.shape[1]
    tiles = leaf // TILE
    copies = []
    total = None
    squares[0] = dot(left[:, 0:TILE], aug[...], 0, 0)
    for t in range(tiles):
        cols = slice(t * TILE, (t + 1) * TILE)
        if t + 1 < tiles:
            squares[(t + 1) % 2] = dot(left[:, (t + 1) * TILE : (t + 2) * TILE], aug[...], 0, 0)
        entries(squares.at[t % 2], kernel.at[t])
        part = dot(pair[:, cols], kernel[t, 0]) + dot(pair[:, cols], kernel[t, 1])
        total = part if total is None else total + part
        rows = pl.ds(t * TILE, TILE)
        copies.append(
            pltpu.make_async_copy(kernel.at[t], whole.at[slot, :, rows, :], sems.at[t])
        )
        copies[t].start()
    near[...] += halves(total)
    for copy in copies:
        copy.wait()


def near_kernel(scalars, v, v1, v2, v3, kernels, after, out, held, sems):
    leaf = kernels.shape[2]
    tiles = leaf // TILE
    copies = []
    for e in range(3):
        for t in range(tiles):
            rows = pl.ds(t * TILE, TILE)
            copies.append(
                pltpu.make_async_copy(
                    kernels.at[e, :, rows, :], held.at[e, :, rows, :], sems.at[e * tiles + t]
                )
            )
    for copy in copies:
        copy.start()
    o0 = scalars[O0]
    own = v[:, 0:leaf]
    second = jnp.where(o0 == 1, v2[:, 0:leaf], v1[:, 0:leaf])
    third = jnp.where(o0 == 3, v2[:, 0:leaf], v3[:, 0:leaf])
    total = None
    for e, vector in enumerate((own, second, third)):
        pair = stacked(vector)
        for t in range(tiles):
            rows = slice(t * TILE, (t + 1) * TILE)
            copies[e * tiles + t].wait()
            part = dot(pair[:, rows], held[e, 0, rows, :]) + dot(pair[:, rows], held[e, 1, rows, :])
            total = part if total is None else total + part
    out[:, 0:leaf] = NOISE * own + halves(total)
    out[:, leaf:] = jnp.where(
        o0 == 1, v1[:, leaf:], jnp.where(o0 == 2, v2[:, leaf:], v3[:, leaf:])
    )


def gather_kernel(scalars, received, *refs):
    high, out = refs[-2:]
    x, y, o2, o3 = scalars[X], scalars[Y], scalars[O2], scalars[O3]
    left = lax.broadcasted_iota(jnp.int32, (16, 128), 1) < 64
    total = jnp.zeros((16, 128), F32)
    for j in range(4):
        top = jnp.zeros((16, 128), F32)
        for i in range(4):
            p = j * 4 + i
            offset = jnp.bitwise_xor(x, i)
            here = y == j
            hit2 = here & (offset == o2 // 2)
            hit3 = here & (offset == o3)
            total += jnp.where((left & hit2) | (~left & hit3), received[p, 0:16, :], 0.0)
            top += received[p, 16:32, :]
        out[j * 16 : (j + 1) * 16, :] = top
    high[...] = total


def lower_kernel(high, mine, other, table, own, *refs):
    out = refs[-1]
    start = own.shape[1] - 128
    parts = [high[:, 64:128]]
    for side in (mine, other):
        parts += [side[j * 16 : (j + 1) * 16, 0:64] for j in range(4)]
    field = times_t(jnp.concatenate(parts, axis=1), table[...])
    norm = sum(side[j * 16 : (j + 1) * 16, 64:128] for side in (mine, other) for j in range(4))
    first = jnp.concatenate([field, norm], axis=1)
    second = jnp.concatenate([own[:, start + 64 :], high[:, 0:64]], axis=1)
    for i in range(out.shape[0]):
        out[i, 0:16, :] = first
        out[i, 16:32, :] = second


def first_lower_kernel(scalars, high, mine, other, table, own, skeletons, second, moved, out):
    lower_kernel(high, mine, other, table, own, out)
    _, k1, k2 = skeleton_offsets(scalars)
    third = jnp.where(scalars[O2] > 1, moved[...], second[...])
    blocks = [packed(skeletons[0]), packed(skeletons[1]), third]
    for i in range(out.shape[0]):
        offset = jnp.bitwise_xor(scalars[Z], i)
        block = jnp.where(offset == k1, blocks[1], blocks[0])
        out[i, 32:48, :] = own[...]
        out[i, 48:80, :] = jnp.where((offset == k2) | (offset == 0), blocks[2], block)


def apply_far(scalars, received, table, bases, near):
    leaf = bases.shape[1]
    z, o0, o1, o2 = scalars[Z], scalars[O0], scalars[O1], scalars[O2]
    left = lax.broadcasted_iota(jnp.int32, (16, 128), 1) < 64
    sums = [jnp.zeros((16, 128), F32) for _ in range(3)]
    for i in range(received.shape[0]):
        offset = jnp.bitwise_xor(z, i)
        hit1 = offset // 2 == o1
        hit2 = offset // 4 == jnp.bitwise_and(o2, 1)
        sums[0] += received[i, 0:16, :]
        sums[1] += jnp.where((left & hit1) | (~left & hit2), received[i, 16:32, :], 0.0)
        if received.shape[1] > 32:
            sums[2] += jnp.where(offset == o0, received[i, 32:48, :], 0.0)
    moment = sums[2] if received.shape[1] > 32 else near[:, leaf : leaf + 128]
    parts = [moment[:, 0:64], sums[1], sums[0][:, 0:64]]
    field = times_t(jnp.concatenate(parts, axis=1), table[...])
    pair = stacked(field)
    far = halves(dot(pair, bases[0:64, :]) + dot(pair, bases[64:128, :]))
    return near[:, 0:leaf] + far, sums[0][:, 64:65]


def first_kernel(scalars, received, skeletons, bases, near, chain, table, v1, out):
    table[...] = low_couplings(scalars, skeletons, received, chain)
    image, _ = apply_far(scalars, received, table, bases, near)
    write_moments(v1, out, image, image, bases, chain)


def second_kernel(scalars, received, table, bases, near, chain, v2, scaled, sums, out):
    image, norm = apply_far(scalars, received, table, bases, near)
    v2[...] = image
    sums[...] = jnp.broadcast_to(norm, sums.shape)
    write_moments(scaled, out, image / jnp.sqrt(norm), image, bases, chain)


def third_kernel(scalars, received, table, bases, near, chain, v1, sums, image, step, out):
    product, along = apply_far(scalars, received, table, bases, near)
    norm = sums[:, 0:1]
    size = norm / along
    new = v1[:, 0 : product.shape[1]] - (size * jnp.sqrt(norm)) * product
    step[...] = jnp.broadcast_to(size, step.shape)
    write_moments(image, out, new, new, bases, chain)


def diagonal():
    rows = lax.broadcasted_iota(jnp.int32, (16, 128), 0)
    return rows == lax.broadcasted_iota(jnp.int32, (16, 128), 1)


def fourth_kernel(scalars, received, table, bases, near, v2, sums, along, fresh, out):
    product, norm = apply_far(scalars, received, table, bases, near)
    new = product + (norm / sums[:, 0:1]) * v2[...]
    along[...] = new
    fresh[...] = jnp.broadcast_to(norm, fresh.shape)
    share = jnp.sum(new * new, axis=1, keepdims=True)
    line = jnp.sum(jnp.where(diagonal(), share, 0.0), axis=0, keepdims=True)
    out[...] = jnp.broadcast_to(line, out.shape)


def last_kernel(shares, rhs, v1, v2, image, along, sums, fresh, step, iterate, residual):
    leaf = rhs.shape[1]
    norm = fresh[:, 0:1]
    first = step[:, 0:1]
    line = jnp.sum(shares[...], axis=0, keepdims=True)
    second = norm / jnp.sum(jnp.where(diagonal(), line, 0.0), axis=1, keepdims=True)
    beta = norm / sums[:, 0:1]
    start = v1[:, 0:leaf]
    iterate[...] = first * start + second * (image[:, 0:leaf] + beta * start)
    residual[...] = rhs[...] - first * v2[...] - second * along[...]


SMEM = pl.BlockSpec(memory_space=pltpu.SMEM)
VMEM = pl.BlockSpec(memory_space=pltpu.VMEM)


def shaped(*shape, dtype=F32):
    return jax.ShapeDtypeStruct(shape, dtype)


MIB = 1024 * 1024
ANY = pl.BlockSpec(memory_space=pl.ANY)


def call(kernel, outs, scalars, arrays, name, after=(), limit=16, flops=100000, scratch=(), alias=None):
    def body(*refs):
        if scalars:
            kernel(places(refs[0]), *refs[1:])
        else:
            kernel(*refs)

    return pl.pallas_call(
        body,
        out_shape=outs,
        in_specs=[SMEM] * len(scalars) + [VMEM] * len(arrays) + [ANY] * len(after),
        out_specs=jax.tree.map(lambda a: VMEM if len(a.shape) < 4 else ANY, outs),
        scratch_shapes=list(scratch),
        input_output_aliases=alias or {},
        name=name,
        compiler_params=pltpu.CompilerParams(vmem_limit_bytes=limit * MIB),
        cost_estimate=pl.CostEstimate(flops=flops, bytes_accessed=500000, transcendentals=0),
    )(*scalars, *arrays, *after)


def build(scalars, own, others, choice, near, after, name, kernels=()):
    leaf = own.shape[1]
    tiles = leaf // TILE
    return call(
        functools.partial(build_kernel, choice=choice),
        (shaped(3, 2, leaf, leaf, dtype=BF16), shaped(16, leaf)),
        [scalars],
        [own, *others, *([] if near is None else [near])],
        name,
        after=[*after, *kernels],
        limit=50,
        flops=4000000000,
        alias={3 + len(others) + len(after): 0} if kernels else None,
        scratch=[
            pltpu.VMEM((DEPTH, leaf), BF16),
            pltpu.VMEM((DEPTH, leaf), BF16),
            pltpu.VMEM((2, TILE, leaf), F32),
            pltpu.VMEM((tiles, 2, TILE, leaf), BF16),
            pltpu.SemaphoreType.DMA((tiles,)),
        ],
    )


def near_product(scalars, vectors, kernels, after):
    leaf = kernels.shape[2]
    return call(
        near_kernel,
        shaped(*vectors[0].shape),
        [scalars],
        vectors,
        "near",
        after=[kernels, after],
        limit=50,
        flops=4000000000,
        scratch=[
            pltpu.VMEM((3, 2, leaf, leaf), BF16),
            pltpu.SemaphoreType.DMA((3 * leaf // TILE,)),
        ],
    )


def along_z(v, offset):
    return lax.ppermute(v, "z", [(i, i ^ offset) for i in range(8)])


def other_core(v):
    return lax.ppermute(v, "core", [(0, 1), (1, 0)])


def over_z(v):
    return lax.all_to_all(v, "z", 0, 0)


def over_yx(v):
    return lax.all_to_all(v, ("y", "x"), 0, 0)


def local(
    rhs,
    embeddings,
    leaf_order,
    basis,
    transfer_maps,
    skeletons,
    top_skeletons,
    near_lists,
    far_lists,
    top_lists,
):
    top = lax.axis_index("y") * 2 + lax.axis_index("core")
    listed = lax.dynamic_index_in_dim(top_lists, top, 0, keepdims=False)
    scalars = far_lists[:, 0]
    chain_skeletons = skeletons[:, 0]
    tops = top_skeletons.reshape(4, 2, 64, 64)

    row = shaped(16, 1024)
    long = shaped(16, 1152)
    thin = shaped(16, 128)
    wire = shaped(16, 32, 128)
    both = jnp.concatenate([embeddings, rhs], axis=0)
    one = along_z(both, 1)
    two = along_z(both, 2)
    three_off = along_z(two, 1)
    bases, chain, tail, own, outgoing, second = call(
        prepare_kernel,
        (
            shaped(128, 1024, dtype=BF16),
            shaped(64, 512, dtype=BF16),
            shaped(64, 64),
            thin,
            shaped(16, 64, 128),
            shaped(32, 128),
        ),
        [scalars],
        [leaf_order, basis, transfer_maps[:, 0], chain_skeletons, rhs],
        "prepare",
        limit=60,
    )

    def gather(spread, after=()):
        high, mine = call(
            gather_kernel, (thin, shaped(64, 128)), [scalars], [spread], "gather", after=after
        )
        return high, mine, other_core(mine)

    kernels, near = build(scalars, both, [], None, None, [two], "build_own")
    from_yx = over_yx(outgoing)
    second_moved = lax.ppermute(second, "x", [(i, i ^ 1) for i in range(4)])
    spread = gather(from_yx, [near])
    top_table = call(
        top_kernel,
        shaped(128, 576, dtype=BF16),
        [scalars, listed],
        [chain_skeletons, from_yx, tops, tail],
        "tops",
    )
    outgoing = call(
        first_lower_kernel,
        shaped(8, 80, 128),
        [scalars],
        [*spread, top_table, own, chain_skeletons, second, second_moved],
        "lower",
    )
    kernels, near = build(
        scalars, both, [two, one], 1, near, [outgoing], "build_a", [kernels]
    )
    kernels, near = build(
        scalars, both, [two, three_off], 3, near, [outgoing], "build_b", [kernels]
    )
    table, v1, outgoing = call(
        first_kernel,
        (shaped(128, 256, dtype=BF16), long, wire),
        [scalars],
        [over_z(outgoing), chain_skeletons, bases, near, chain],
        "first",
    )

    def operate(extended, outgoing):
        moved = [along_z(extended, o) for o in (1, 2, 3)]
        spread = gather(over_yx(outgoing))
        lower = call(
            lower_kernel,
            shaped(8, 32, 128),
            [],
            [*spread, top_table, extended],
            "lower",
            after=moved,
        )
        near = near_product(scalars, [extended, *moved], kernels, lower)
        return over_z(lower), table, bases, near

    v2, scaled, sums, outgoing = call(
        second_kernel, (row, long, thin, wire), [scalars], [*operate(v1, outgoing), chain], "second"
    )
    image, step, outgoing = call(
        third_kernel,
        (long, thin, wire),
        [scalars],
        [*operate(scaled, outgoing), chain, v1, sums],
        "third",
    )
    along, fresh, outgoing = call(
        fourth_kernel,
        (row, thin, shaped(256, 128)),
        [scalars],
        [*operate(image, outgoing), v2, sums],
        "fourth",
    )
    shares = lax.all_to_all(outgoing, ("y", "core", "x", "z"), 0, 0, tiled=True)
    return call(
        last_kernel,
        (row, row),
        [],
        [shares, rhs, v1, v2, image, along, sums, fresh, step],
        "last",
    )


def solution(mesh):
    axes = ("y", "core", "x", "z")
    fine = Mesh(mesh.devices.reshape(4, 2, 4, 8), axes)
    placed = (
        P(None, axes),
        P(None, axes),
        P(axes, None),
        P(None, axes),
        P(None, axes, None, None),
        P(None, axes, None, None),
        P(),
        P(axes, None),
        P(None, axes),
        P(),
    )
    return jax.shard_map(
        local,
        mesh=fine,
        in_specs=placed,
        out_specs=(P(None, axes), P(None, axes)),
        check_vma=False,
    )
```

```python
import functools
import math

import jax
import jax.numpy as jnp
from jax import lax
from jax.experimental import pallas as pl
from jax.experimental.pallas import tpu as pltpu
from jax.sharding import Mesh
from jax.sharding import PartitionSpec as P

F32 = jnp.float32
BF16 = jnp.bfloat16
HIGHEST = lax.Precision.HIGHEST
NOISE = 0.5
SCALE = math.sqrt(5.0) / 2.8
LOG2E = math.log2(math.e)
DEPTH = 208
TILE = 256

Z, X, Y, CORE, O0, O1, O2, O3 = range(8)


def dot(a, b, ca=1, cb=0, precision=None):
    return lax.dot_general(
        a, b, (((ca,), (cb,)), ((), ())), precision=precision, preferred_element_type=F32
    )


def split(a):
    high = a.astype(BF16)
    return high, (a - high.astype(F32)).astype(BF16)


def stacked(a):
    return jnp.concatenate(split(a), axis=0)


def halves(a):
    n = a.shape[0] // 2
    return a[:n] + a[n:]


def places(partners):
    y, core, x, z = (lax.axis_index(a) for a in ("y", "core", "x", "z"))
    leaf = ((y * 2 + core) * 4 + x) * 8 + z
    return [z, x, y, core] + [jnp.bitwise_xor(partners[h], leaf // 2**h) for h in range(4)]


def paired(a, axis):
    return jnp.concatenate(split(a), axis=axis)


def times(a, pair):
    both = halves(dot(stacked(a), pair))
    n = both.shape[1] // 2
    return both[:, :n] + both[:, n:]


def times_t(a, pair):
    both = halves(dot(stacked(a), pair, 1, 1))
    n = both.shape[1] // 2
    return both[:, :n] + both[:, n:]


def square_sum(v):
    return jnp.broadcast_to(jnp.sum(v * v, axis=1, keepdims=True), (v.shape[0], 64))


def lift(own, chain):
    lifted = times(own, chain)
    return jnp.concatenate([own, lifted[:, 0:64]], axis=1), lifted[:, 64:192], lifted[:, 192:256]


def send(block, out, sems):
    copies = [pltpu.make_async_copy(block, out.at[i], sems.at[i]) for i in range(out.shape[0])]
    for copy in copies:
        copy.start()
    return copies


def write_moments(extended, out, block, sems, v, own, weighed, chain):
    first, middle, top = lift(own, chain[...])
    block[0:16, :] = middle
    block[16:32, :] = jnp.concatenate([top, square_sum(weighed)], axis=1)
    copies = send(block, out, sems)
    extended[:, 0 : v.shape[1]] = v
    extended[:, v.shape[1] :] = first
    for copy in copies:
        copy.wait()


def packed(skeleton):
    return jnp.concatenate([skeleton[0:32], skeleton[32:64]], axis=1)


def unpacked(block):
    return jnp.concatenate([block[:, 0:64], block[:, 64:128]], axis=0)


def skeleton_offsets(scalars):
    o0, o1 = scalars[O0], scalars[O1]
    second = jnp.where(o1 > 1, o1 * 2, jnp.where(o0 == 2, 3, 2))
    return o0, second, jnp.where(o1 == 3, 4, 7)


def prepare_kernel(
    scalars, order, basis, maps, skeletons, rhs, bases, chain, tail, gram, own, wire, second
):
    both = stacked(basis[...])
    leaf = basis.shape[1]
    for t in range(leaf // TILE):
        rows = lax.broadcasted_iota(jnp.int32, (TILE, leaf), 0) + t * TILE
        one_hot = jnp.where(rows == order[...], 1.0, 0.0).astype(BF16)
        bases[:, t * TILE : (t + 1) * TILE] = dot(both, one_hot, 1, 1).astype(BF16)
    p1 = maps[0]
    p2 = dot(p1, maps[1], precision=HIGHEST)
    p3 = dot(p2, maps[2], precision=HIGHEST)
    e34 = dot(maps[3], maps[4], precision=HIGHEST)
    p5 = dot(p3, e34, precision=HIGHEST)
    tail[...] = e34
    chain[...] = paired(jnp.concatenate([p1, p2, p3, p5], axis=1), 1)
    products = dot(bases[...], bases[...], 1, 1)
    products = halves(products[:, 0:64] + products[:, 64:128])
    gram[...] = paired(products, 1)
    first, middle, top = lift(times_t(rhs[...], bases[...]), chain[...])
    own[...] = first
    last = jnp.concatenate([top, jnp.zeros_like(top)], axis=1)
    for i in range(wire.shape[0]):
        wire[i, 0:16, :] = middle
        wire[i, 16:32, :] = last
        wire[i, 32:64, :] = packed(skeletons[3])
    second[...] = packed(skeletons[2])


def matern(first, second):
    turned = first.T
    squares = (
        jnp.sum(turned * turned, axis=1, keepdims=True)
        + jnp.sum(second * second, axis=0, keepdims=True)
        - 2.0 * dot(turned, second, precision=HIGHEST)
    )
    s = SCALE * jnp.sqrt(jnp.maximum(squares, 0.0))
    return (1.0 + s + s * s * (1.0 / 3.0)) * jnp.exp(-s)


def top_kernel(scalars, listed, skeletons, from_yx, tops, tail, out):
    x, y, core = scalars[X], scalars[Y], scalars[CORE]
    partner = unpacked(from_yx[y * 4 + jnp.bitwise_xor(x, scalars[O3]), 32:64, :])
    others = []
    masks = []
    for flip in (0, 1):
        for j in range(4):
            side = jnp.bitwise_xor(core, flip)
            others.append(tops[j, side])
            hits = sum((listed[k] == j * 2 + side).astype(F32) for k in range(4))
            masks.append(jnp.full((64, 64), hits, F32))
    top = matern(tops[y, core], jnp.concatenate(others, axis=1))
    top = dot(tail[...], top * jnp.concatenate(masks, axis=1), precision=HIGHEST)
    out[...] = paired(jnp.concatenate([matern(skeletons[3], partner), top], axis=1), 0)


def low_couplings(scalars, skeletons, from_z, chain):
    z = scalars[Z]
    down = chain[:, 0:256].astype(F32) + chain[:, 256:512].astype(F32)
    pieces = []
    for h, offset in enumerate(skeleton_offsets(scalars)):
        if h == 2:
            offset = jnp.where(scalars[O2] % 2 == 1, offset, 0)
        partner = unpacked(from_z[jnp.bitwise_xor(z, offset), 32:64, :])
        coupling = matern(skeletons[h], partner)
        if h > 0:
            coupling = dot(down[:, (h - 1) * 64 : h * 64], coupling, precision=HIGHEST)
        pieces.append(coupling)
    return paired(jnp.concatenate(pieces + [down[:, 128:192]], axis=1), 0)


def three(a):
    high = a.astype(BF16).astype(F32)
    middle = (a - high).astype(BF16).astype(F32)
    return high, middle, a - high - middle


def augment(points, target, turned):
    leaf = points.shape[1]
    high, low = split(points * SCALE)
    h32, l32 = high.astype(F32), low.astype(F32)
    sums = three(jnp.sum(h32 * h32 + 2.0 * (h32 * l32), axis=0, keepdims=True))
    row = lax.broadcasted_iota(jnp.int32, (16, leaf), 0)
    first, ones = (0, 3) if turned else (3, 0)
    rest = jnp.where((row >= ones) & (row < ones + 3), 1.0, 0.0)
    for i in range(3):
        rest = jnp.where(row == first + i, sums[i], rest)
    if turned:
        high, low = (-2.0 * h32).astype(BF16), (-2.0 * l32).astype(BF16)
    target[0:64, :] = high
    target[64:128, :] = high if turned else low
    target[128:192, :] = low if turned else high
    target[192:208, :] = rest.astype(BF16)


def entries(squares, kernel):
    wide = 512
    tall = 32
    for r in range(0, squares.shape[0], tall):
        for c in range(0, squares.shape[1], wide):
            s2 = jnp.maximum(squares[r : r + tall, c : c + wide], 1e-30)
            s = s2 * lax.rsqrt(s2)
            value = (1.0 + s + s2 * (1.0 / 3.0)) * jnp.exp2(s * -LOG2E)
            high, low = split(value)
            kernel[0, r : r + tall, c : c + wide] = high
            kernel[1, r : r + tall, c : c + wide] = low


def build_kernel(scalars, own, *refs, choice):
    if choice is None:
        whole, near, aug, left, squares, kernel, sems = refs[-7:]
        both = own[...]
        near[...] = NOISE * own[64:80, :]
        slot = 0
    else:
        yes, no, begin = refs[:3]
        whole, near, aug, left, squares, kernel, sems = refs[-7:]
        both = jnp.where(scalars[O0] == choice, yes[...], no[...])
        near[...] = begin[...]
        slot = (choice + 1) // 2
    augment(own[0:64, :], aug, False)
    augment(both[0:64, :], left, True)
    pair = stacked(both[64:80, :])
    leaf = own.shape[1]
    tiles = leaf // TILE
    copies = []
    total = None
    squares[0] = dot(left[:, 0:TILE], aug[...], 0, 0)
    for t in range(tiles):
        cols = slice(t * TILE, (t + 1) * TILE)
        if t + 1 < tiles:
            squares[(t + 1) % 2] = dot(left[:, (t + 1) * TILE : (t + 2) * TILE], aug[...], 0, 0)
        entries(squares.at[t % 2], kernel.at[t])
        part = dot(pair[:, cols], kernel[t, 0]) + dot(pair[:, cols], kernel[t, 1])
        total = part if total is None else total + part
        rows = pl.ds(t * TILE, TILE)
        copies.append(
            pltpu.make_async_copy(kernel.at[t], whole.at[slot, :, rows, :], sems.at[t])
        )
        copies[t].start()
    near[...] += halves(total)
    for copy in copies:
        copy.wait()


def near_kernel(scalars, v, v1, v2, v3, bases, kernels, after, out, held, sems):
    leaf = kernels.shape[2]
    tiles = leaf // TILE
    copies = []
    for e in range(3):
        for t in range(tiles):
            rows = pl.ds(t * TILE, TILE)
            copies.append(
                pltpu.make_async_copy(
                    kernels.at[e, :, rows, :], held.at[e, :, rows, :], sems.at[e * tiles + t]
                )
            )
    for copy in copies:
        copy.start()
    o0 = scalars[O0]
    own = v[:, 0:leaf]
    second = jnp.where(o0 == 1, v2[:, 0:leaf], v1[:, 0:leaf])
    third = jnp.where(o0 == 3, v2[:, 0:leaf], v3[:, 0:leaf])
    total = None
    for e, vector in enumerate((own, second, third)):
        pair = stacked(vector)
        for t in range(tiles):
            rows = slice(t * TILE, (t + 1) * TILE)
            copies[e * tiles + t].wait()
            part = dot(pair[:, rows], held[e, 0, rows, :]) + dot(pair[:, rows], held[e, 1, rows, :])
            total = part if total is None else total + part
    result = NOISE * own + halves(total)
    partner = jnp.where(o0 == 1, v1[:, leaf:], jnp.where(o0 == 2, v2[:, leaf:], v3[:, leaf:]))
    out[:, 0:leaf] = result
    out[:, leaf:] = jnp.concatenate([partner[:, 0:64], times_t(result, bases[...])], axis=1)


def gather_kernel(scalars, received, *refs):
    high, out = refs[-2:]
    x, y, o2, o3 = scalars[X], scalars[Y], scalars[O2], scalars[O3]
    left = lax.broadcasted_iota(jnp.int32, (16, 128), 1) < 64
    total = jnp.zeros((16, 128), F32)
    for j in range(4):
        top = jnp.zeros((16, 128), F32)
        for i in range(4):
            p = j * 4 + i
            offset = jnp.bitwise_xor(x, i)
            here = y == j
            hit2 = here & (offset == o2 // 2)
            hit3 = here & (offset == o3)
            total += jnp.where((left & hit2) | (~left & hit3), received[p, 0:16, :], 0.0)
            top += received[p, 16:32, :]
        out[j * 16 : (j + 1) * 16, :] = top
    high[...] = total


def lower_blocks(high, mine, other, table, own):
    start = own.shape[1] - 128
    parts = [high[:, 64:128]]
    for side in (mine, other):
        parts += [side[j * 16 : (j + 1) * 16, 0:64] for j in range(4)]
    field = times_t(jnp.concatenate(parts, axis=1), table[...])
    return field, jnp.concatenate([own[:, start + 64 :], high[:, 0:64]], axis=1)


def lower_kernel(high, mine, other, table, own, *refs):
    out, block, sems = refs[-3:]
    field, second = lower_blocks(high, mine, other, table, own)
    norm = sum(side[j * 16 : (j + 1) * 16, 64:128] for side in (mine, other) for j in range(4))
    block[0:16, :] = jnp.concatenate([field, norm], axis=1)
    block[16:32, :] = second
    for copy in send(block, out, sems):
        copy.wait()


def first_lower_kernel(scalars, high, mine, other, table, own, skeletons, second, moved, out):
    field, lifted = lower_blocks(high, mine, other, table, own)
    first = jnp.concatenate([field, own[:, 0:64]], axis=1)
    _, k1, k2 = skeleton_offsets(scalars)
    third = jnp.where(scalars[O2] > 1, moved[...], second[...])
    blocks = [packed(skeletons[0]), packed(skeletons[1]), third]
    for i in range(out.shape[0]):
        offset = jnp.bitwise_xor(scalars[Z], i)
        block = jnp.where(offset == k1, blocks[1], blocks[0])
        out[i, 0:16, :] = first
        out[i, 16:32, :] = lifted
        out[i, 32:64, :] = jnp.where((offset == k2) | (offset == 0), blocks[2], block)


def apply_far(scalars, received, table, bases, near):
    leaf = bases.shape[1]
    z, o0, o1, o2 = scalars[Z], scalars[O0], scalars[O1], scalars[O2]
    start = received.shape[1] > 32
    left = lax.broadcasted_iota(jnp.int32, (16, 128), 1) < 64
    sums = [jnp.zeros((16, 128), F32) for _ in range(2)]
    for i in range(received.shape[0]):
        offset = jnp.bitwise_xor(z, i)
        hit1 = offset // 2 == o1
        hit2 = offset // 4 == jnp.bitwise_and(o2, 1)
        block = received[i, 0:16, :]
        sums[0] += jnp.where(left | (offset == o0), block, 0.0) if start else block
        sums[1] += jnp.where((left & hit1) | (~left & hit2), received[i, 16:32, :], 0.0)
    moment = sums[0][:, 64:128] if start else near[:, leaf : leaf + 64]
    parts = [moment, sums[1], sums[0][:, 0:64]]
    field = times_t(jnp.concatenate(parts, axis=1), table[...])
    pair = stacked(field)
    far = halves(dot(pair, bases[0:64, :]) + dot(pair, bases[64:128, :]))
    return near[:, 0:leaf] + far, sums[0][:, 64:65], field


def moment_of(near, field, gram):
    return near[:, near.shape[1] - 64 :] + times(field, gram[...])


def first_kernel(
    scalars, received, skeletons, bases, near, chain, table, v1, out, block, sems
):
    table[...] = low_couplings(scalars, skeletons, received, chain)
    image, _, _ = apply_far(scalars, received, table, bases, near)
    own = times_t(image, bases[...])
    write_moments(v1, out, block, sems, image, own, image, chain)


def second_kernel(
    scalars, received, table, bases, near, gram, chain, v2, scaled, sums, out, block, sems
):
    image, norm, field = apply_far(scalars, received, table, bases, near)
    v2[...] = image
    sums[...] = jnp.broadcast_to(norm, sums.shape)
    size = 1.0 / jnp.sqrt(norm)
    own = moment_of(near, field, gram) * size
    write_moments(scaled, out, block, sems, image * size, own, image, chain)


def third_kernel(
    scalars, received, table, bases, near, gram, chain, v1, sums, image, step, out, block, sems
):
    product, along, field = apply_far(scalars, received, table, bases, near)
    leaf = product.shape[1]
    norm = sums[:, 0:1]
    size = norm / along
    back = size * jnp.sqrt(norm)
    new = v1[:, 0:leaf] - back * product
    own = v1[:, leaf : leaf + 64] - back * moment_of(near, field, gram)
    step[...] = jnp.broadcast_to(size, step.shape)
    write_moments(image, out, block, sems, new, own, new, chain)


def diagonal():
    rows = lax.broadcasted_iota(jnp.int32, (16, 128), 0)
    return rows == lax.broadcasted_iota(jnp.int32, (16, 128), 1)


def fourth_kernel(scalars, received, table, bases, near, v2, sums, along, fresh, out):
    product, norm, _ = apply_far(scalars, received, table, bases, near)
    new = product + (norm / sums[:, 0:1]) * v2[...]
    along[...] = new
    fresh[...] = jnp.broadcast_to(norm, fresh.shape)
    share = jnp.sum(new * new, axis=1, keepdims=True)
    line = jnp.sum(jnp.where(diagonal(), share, 0.0), axis=0, keepdims=True)
    out[...] = jnp.broadcast_to(line, out.shape)


def last_kernel(shares, rhs, v1, v2, image, along, sums, fresh, step, iterate, residual):
    leaf = rhs.shape[1]
    norm = fresh[:, 0:1]
    first = step[:, 0:1]
    line = jnp.sum(shares[...], axis=0, keepdims=True)
    second = norm / jnp.sum(jnp.where(diagonal(), line, 0.0), axis=1, keepdims=True)
    beta = norm / sums[:, 0:1]
    start = v1[:, 0:leaf]
    iterate[...] = first * start + second * (image[:, 0:leaf] + beta * start)
    residual[...] = rhs[...] - first * v2[...] - second * along[...]


SMEM = pl.BlockSpec(memory_space=pltpu.SMEM)
VMEM = pl.BlockSpec(memory_space=pltpu.VMEM)


def shaped(*shape, dtype=F32):
    return jax.ShapeDtypeStruct(shape, dtype)


MIB = 1024 * 1024
ANY = pl.BlockSpec(memory_space=pl.ANY)


def call(kernel, outs, scalars, arrays, name, after=(), limit=16, flops=100000, scratch=(), alias=None):
    def body(*refs):
        if scalars:
            kernel(places(refs[0]), *refs[1:])
        else:
            kernel(*refs)

    return pl.pallas_call(
        body,
        out_shape=outs,
        in_specs=[SMEM] * len(scalars) + [VMEM] * len(arrays) + [ANY] * len(after),
        out_specs=jax.tree.map(lambda a: ANY if len(a.shape) == 4 or a.shape[1:] == (32, 128) else VMEM, outs),
        scratch_shapes=list(scratch),
        input_output_aliases=alias or {},
        name=name,
        compiler_params=pltpu.CompilerParams(vmem_limit_bytes=limit * MIB),
        cost_estimate=pl.CostEstimate(flops=flops, bytes_accessed=500000, transcendentals=0),
    )(*scalars, *arrays, *after)


def block(copies):
    return [pltpu.VMEM((32, 128), F32), pltpu.SemaphoreType.DMA((copies,))]


def build(scalars, own, others, choice, near, after, name, kernels=()):
    leaf = own.shape[1]
    tiles = leaf // TILE
    return call(
        functools.partial(build_kernel, choice=choice),
        (shaped(3, 2, leaf, leaf, dtype=BF16), shaped(16, leaf)),
        [scalars],
        [own, *others, *([] if near is None else [near])],
        name,
        after=[*after, *kernels],
        limit=50,
        flops=4000000000,
        alias={3 + len(others) + len(after): 0} if kernels else None,
        scratch=[
            pltpu.VMEM((DEPTH, leaf), BF16),
            pltpu.VMEM((DEPTH, leaf), BF16),
            pltpu.VMEM((2, TILE, leaf), F32),
            pltpu.VMEM((tiles, 2, TILE, leaf), BF16),
            pltpu.SemaphoreType.DMA((tiles,)),
        ],
    )


def near_product(scalars, vectors, bases, kernels, after):
    leaf = kernels.shape[2]
    return call(
        near_kernel,
        shaped(*vectors[0].shape),
        [scalars],
        [*vectors, bases],
        "near",
        after=[kernels, after],
        limit=50,
        flops=4000000000,
        scratch=[
            pltpu.VMEM((3, 2, leaf, leaf), BF16),
            pltpu.SemaphoreType.DMA((3 * leaf // TILE,)),
        ],
    )


def along_z(v, offset):
    return lax.ppermute(v, "z", [(i, i ^ offset) for i in range(8)])


def other_core(v):
    return lax.ppermute(v, "core", [(0, 1), (1, 0)])


def over_z(v):
    return lax.all_to_all(v, "z", 0, 0)


def over_yx(v):
    return lax.all_to_all(v, ("y", "x"), 0, 0)


def local(
    rhs,
    embeddings,
    leaf_order,
    basis,
    transfer_maps,
    skeletons,
    top_skeletons,
    near_lists,
    far_lists,
    top_lists,
):
    top = lax.axis_index("y") * 2 + lax.axis_index("core")
    listed = lax.dynamic_index_in_dim(top_lists, top, 0, keepdims=False)
    scalars = far_lists[:, 0]
    chain_skeletons = skeletons[:, 0]
    tops = top_skeletons.reshape(4, 2, 64, 64)

    row = shaped(16, 1024)
    long = shaped(16, 1152)
    thin = shaped(16, 128)
    wire = shaped(16, 32, 128)
    both = jnp.concatenate([embeddings, rhs], axis=0)
    one = along_z(both, 1)
    two = along_z(both, 2)
    three_off = along_z(two, 1)
    bases, chain, tail, gram, own, outgoing, second = call(
        prepare_kernel,
        (
            shaped(128, 1024, dtype=BF16),
            shaped(64, 512, dtype=BF16),
            shaped(64, 64),
            shaped(64, 128, dtype=BF16),
            thin,
            shaped(16, 64, 128),
            shaped(32, 128),
        ),
        [scalars],
        [leaf_order, basis, transfer_maps[:, 0], chain_skeletons, rhs],
        "prepare",
        limit=60,
    )

    def gather(spread, after=()):
        high, mine = call(
            gather_kernel, (thin, shaped(64, 128)), [scalars], [spread], "gather", after=after
        )
        return high, mine, other_core(mine)

    kernels, near = build(scalars, both, [], None, None, [two], "build_own")
    from_yx = over_yx(outgoing)
    second_moved = lax.ppermute(second, "x", [(i, i ^ 1) for i in range(4)])
    spread = gather(from_yx, [near])
    top_table = call(
        top_kernel,
        shaped(128, 576, dtype=BF16),
        [scalars, listed],
        [chain_skeletons, from_yx, tops, tail],
        "tops",
    )
    outgoing = call(
        first_lower_kernel,
        shaped(8, 64, 128),
        [scalars],
        [*spread, top_table, own, chain_skeletons, second, second_moved],
        "lower",
    )
    kernels, near = build(
        scalars, both, [two, one], 1, near, [outgoing], "build_a", [kernels]
    )
    kernels, near = build(
        scalars, both, [two, three_off], 3, near, [outgoing], "build_b", [kernels]
    )
    table, v1, outgoing = call(
        first_kernel,
        (shaped(128, 256, dtype=BF16), long, wire),
        [scalars],
        [over_z(outgoing), chain_skeletons, bases, near, chain],
        "first",
        scratch=block(16),
    )

    def operate(extended, outgoing):
        moved = [along_z(extended, o) for o in (1, 2, 3)]
        spread = gather(over_yx(outgoing))
        lower = call(
            lower_kernel,
            shaped(8, 32, 128),
            [],
            [*spread, top_table, extended],
            "lower",
            after=moved,
            scratch=block(8),
        )
        near = near_product(scalars, [extended, *moved], bases, kernels, lower)
        return over_z(lower), table, bases, near

    v2, scaled, sums, outgoing = call(
        second_kernel,
        (row, long, thin, wire),
        [scalars],
        [*operate(v1, outgoing), gram, chain],
        "second",
        scratch=block(16),
    )
    image, step, outgoing = call(
        third_kernel,
        (long, thin, wire),
        [scalars],
        [*operate(scaled, outgoing), gram, chain, v1, sums],
        "third",
        scratch=block(16),
    )
    along, fresh, outgoing = call(
        fourth_kernel,
        (row, thin, shaped(256, 128)),
        [scalars],
        [*operate(image, outgoing), v2, sums],
        "fourth",
    )
    shares = lax.all_to_all(outgoing, ("y", "core", "x", "z"), 0, 0, tiled=True)
    return call(
        last_kernel,
        (row, row),
        [],
        [shares, rhs, v1, v2, image, along, sums, fresh, step],
        "last",
    )


def solution(mesh):
    axes = ("y", "core", "x", "z")
    fine = Mesh(mesh.devices.reshape(4, 2, 4, 8), axes)
    placed = (
        P(None, axes),
        P(None, axes),
        P(axes, None),
        P(None, axes),
        P(None, axes, None, None),
        P(None, axes, None, None),
        P(),
        P(axes, None),
        P(None, axes),
        P(),
    )
    return jax.shard_map(
        local,
        mesh=fine,
        in_specs=placed,
        out_specs=(P(None, axes), P(None, axes)),
        check_vma=False,
    )
```

```python
import functools
import math

import jax
import jax.numpy as jnp
from jax import lax
from jax.experimental import pallas as pl
from jax.experimental.pallas import tpu as pltpu
from jax.sharding import Mesh
from jax.sharding import PartitionSpec as P

F32 = jnp.float32
BF16 = jnp.bfloat16
HIGHEST = lax.Precision.HIGHEST
NOISE = 0.5
SCALE = math.sqrt(5.0) / 2.8
LOG2E = math.log2(math.e)
DEPTH = 208
TILE = 256

Z, X, Y, CORE, O0, O1, O2, O3 = range(8)


def dot(a, b, ca=1, cb=0, precision=None):
    return lax.dot_general(
        a, b, (((ca,), (cb,)), ((), ())), precision=precision, preferred_element_type=F32
    )


def split(a):
    high = a.astype(BF16)
    return high, (a - high.astype(F32)).astype(BF16)


def stacked(a):
    return jnp.concatenate(split(a), axis=0)


def halves(a):
    n = a.shape[0] // 2
    return a[:n] + a[n:]


def places(partners):
    y, core, x, z = (lax.axis_index(a) for a in ("y", "core", "x", "z"))
    leaf = ((y * 2 + core) * 4 + x) * 8 + z
    return [z, x, y, core] + [jnp.bitwise_xor(partners[h], leaf // 2**h) for h in range(4)]


def paired(a, axis):
    return jnp.concatenate(split(a), axis=axis)


def times(a, pair):
    both = halves(dot(stacked(a), pair))
    n = both.shape[1] // 2
    return both[:, :n] + both[:, n:]


def times_t(a, pair):
    both = halves(dot(stacked(a), pair, 1, 1))
    n = both.shape[1] // 2
    return both[:, :n] + both[:, n:]


def square_sum(v):
    return jnp.broadcast_to(jnp.sum(v * v, axis=1, keepdims=True), (v.shape[0], 64))


def lift(own, chain):
    lifted = times(own, chain)
    return jnp.concatenate([own, lifted[:, 0:64]], axis=1), lifted[:, 64:192], lifted[:, 192:256]


def write_moments(extended, out, v, own, weighed, chain):
    first, middle, top = lift(own, chain[...])
    last = jnp.concatenate([top, square_sum(weighed)], axis=1)
    for i in range(out.shape[0]):
        out[i, 0:16, :] = middle
        out[i, 16:32, :] = last
    extended[:, 0 : v.shape[1]] = v
    extended[:, v.shape[1] :] = first


def packed(skeleton):
    return jnp.concatenate([skeleton[0:32], skeleton[32:64]], axis=1)


def unpacked(block):
    return jnp.concatenate([block[:, 0:64], block[:, 64:128]], axis=0)


def skeleton_offsets(scalars):
    o0, o1 = scalars[O0], scalars[O1]
    second = jnp.where(o1 > 1, o1 * 2, jnp.where(o0 == 2, 3, 2))
    return o0, second, jnp.where(o1 == 3, 4, 7)


def prepare_kernel(
    scalars, order, basis, maps, skeletons, rhs, bases, chain, tail, gram, own, wire, second
):
    both = stacked(basis[...])
    leaf = basis.shape[1]
    for t in range(leaf // TILE):
        rows = lax.broadcasted_iota(jnp.int32, (TILE, leaf), 0) + t * TILE
        one_hot = jnp.where(rows == order[...], 1.0, 0.0).astype(BF16)
        bases[:, t * TILE : (t + 1) * TILE] = dot(both, one_hot, 1, 1).astype(BF16)
    p1 = maps[0]
    p2 = dot(p1, maps[1], precision=HIGHEST)
    p3 = dot(p2, maps[2], precision=HIGHEST)
    e34 = dot(maps[3], maps[4], precision=HIGHEST)
    p5 = dot(p3, e34, precision=HIGHEST)
    tail[...] = e34
    chain[...] = paired(jnp.concatenate([p1, p2, p3, p5], axis=1), 1)
    products = dot(bases[...], bases[...], 1, 1)
    products = halves(products[:, 0:64] + products[:, 64:128])
    gram[...] = paired(products, 1)
    first, middle, top = lift(times_t(rhs[...], bases[...]), chain[...])
    own[...] = first
    last = jnp.concatenate([top, jnp.zeros_like(top)], axis=1)
    for i in range(wire.shape[0]):
        wire[i, 0:16, :] = middle
        wire[i, 16:32, :] = last
        wire[i, 32:64, :] = packed(skeletons[3])
    second[...] = packed(skeletons[2])


def matern(first, second):
    turned = first.T
    squares = (
        jnp.sum(turned * turned, axis=1, keepdims=True)
        + jnp.sum(second * second, axis=0, keepdims=True)
        - 2.0 * dot(turned, second, precision=HIGHEST)
    )
    s = SCALE * jnp.sqrt(jnp.maximum(squares, 0.0))
    return (1.0 + s + s * s * (1.0 / 3.0)) * jnp.exp(-s)


def top_kernel(scalars, listed, skeletons, from_yx, tops, tail, out):
    x, y, core = scalars[X], scalars[Y], scalars[CORE]
    partner = unpacked(from_yx[y * 4 + jnp.bitwise_xor(x, scalars[O3]), 32:64, :])
    others = []
    masks = []
    for flip in (0, 1):
        for j in range(4):
            side = jnp.bitwise_xor(core, flip)
            others.append(tops[j, side])
            hits = sum((listed[k] == j * 2 + side).astype(F32) for k in range(4))
            masks.append(jnp.full((64, 64), hits, F32))
    top = matern(tops[y, core], jnp.concatenate(others, axis=1))
    top = dot(tail[...], top * jnp.concatenate(masks, axis=1), precision=HIGHEST)
    out[...] = paired(jnp.concatenate([matern(skeletons[3], partner), top], axis=1), 0)


def low_couplings(scalars, skeletons, from_z, chain):
    z = scalars[Z]
    down = chain[:, 0:256].astype(F32) + chain[:, 256:512].astype(F32)
    pieces = []
    for h, offset in enumerate(skeleton_offsets(scalars)):
        if h == 2:
            offset = jnp.where(scalars[O2] % 2 == 1, offset, 0)
        partner = unpacked(from_z[jnp.bitwise_xor(z, offset), 32:64, :])
        coupling = matern(skeletons[h], partner)
        if h > 0:
            coupling = dot(down[:, (h - 1) * 64 : h * 64], coupling, precision=HIGHEST)
        pieces.append(coupling)
    return paired(jnp.concatenate(pieces + [down[:, 128:192]], axis=1), 0)


def three(a):
    high = a.astype(BF16).astype(F32)
    middle = (a - high).astype(BF16).astype(F32)
    return high, middle, a - high - middle


def augment(points, target, turned):
    leaf = points.shape[1]
    high, low = split(points * SCALE)
    h32, l32 = high.astype(F32), low.astype(F32)
    sums = three(jnp.sum(h32 * h32 + 2.0 * (h32 * l32), axis=0, keepdims=True))
    row = lax.broadcasted_iota(jnp.int32, (16, leaf), 0)
    first, ones = (0, 3) if turned else (3, 0)
    rest = jnp.where((row >= ones) & (row < ones + 3), 1.0, 0.0)
    for i in range(3):
        rest = jnp.where(row == first + i, sums[i], rest)
    if turned:
        high, low = (-2.0 * h32).astype(BF16), (-2.0 * l32).astype(BF16)
    target[0:64, :] = high
    target[64:128, :] = high if turned else low
    target[128:192, :] = low if turned else high
    target[192:208, :] = rest.astype(BF16)


def entries(squares, kernel):
    wide = 512
    tall = 32
    for r in range(0, squares.shape[0], tall):
        for c in range(0, squares.shape[1], wide):
            s2 = jnp.maximum(squares[r : r + tall, c : c + wide], 1e-30)
            s = s2 * lax.rsqrt(s2)
            value = (1.0 + s + s2 * (1.0 / 3.0)) * jnp.exp2(s * -LOG2E)
            high, low = split(value)
            kernel[0, r : r + tall, c : c + wide] = high
            kernel[1, r : r + tall, c : c + wide] = low


def build_kernel(scalars, own, *refs, choice):
    if choice is None:
        whole, near, aug, left, squares, kernel, sems = refs[-7:]
        both = own[...]
        near[...] = NOISE * own[64:80, :]
        slot = 0
    else:
        yes, no, begin = refs[:3]
        whole, near, aug, left, squares, kernel, sems = refs[-7:]
        both = jnp.where(scalars[O0] == choice, yes[...], no[...])
        near[...] = begin[...]
        slot = (choice + 1) // 2
    augment(own[0:64, :], aug, False)
    augment(both[0:64, :], left, True)
    pair = stacked(both[64:80, :])
    leaf = own.shape[1]
    tiles = leaf // TILE
    copies = []
    total = None
    squares[0] = dot(left[:, 0:TILE], aug[...], 0, 0)
    for t in range(tiles):
        cols = slice(t * TILE, (t + 1) * TILE)
        if t + 1 < tiles:
            squares[(t + 1) % 2] = dot(left[:, (t + 1) * TILE : (t + 2) * TILE], aug[...], 0, 0)
        entries(squares.at[t % 2], kernel.at[t])
        part = dot(pair[:, cols], kernel[t, 0]) + dot(pair[:, cols], kernel[t, 1])
        total = part if total is None else total + part
        rows = pl.ds(t * TILE, TILE)
        copies.append(
            pltpu.make_async_copy(kernel.at[t], whole.at[slot, :, rows, :], sems.at[t])
        )
        copies[t].start()
    near[...] += halves(total)
    for copy in copies:
        copy.wait()


def near_kernel(scalars, v, v1, v2, v3, bases, kernels, after, out, held, sems):
    leaf = kernels.shape[2]
    tiles = leaf // TILE
    copies = []
    for e in range(3):
        for t in range(tiles):
            rows = pl.ds(t * TILE, TILE)
            copies.append(
                pltpu.make_async_copy(
                    kernels.at[e, :, rows, :], held.at[e, :, rows, :], sems.at[e * tiles + t]
                )
            )
    for copy in copies:
        copy.start()
    o0 = scalars[O0]
    own = v[:, 0:leaf]
    second = jnp.where(o0 == 1, v2[:, 0:leaf], v1[:, 0:leaf])
    third = jnp.where(o0 == 3, v2[:, 0:leaf], v3[:, 0:leaf])
    total = None
    for e, vector in enumerate((own, second, third)):
        pair = stacked(vector)
        for t in range(tiles):
            rows = slice(t * TILE, (t + 1) * TILE)
            copies[e * tiles + t].wait()
            part = dot(pair[:, rows], held[e, 0, rows, :]) + dot(pair[:, rows], held[e, 1, rows, :])
            total = part if total is None else total + part
    result = NOISE * own + halves(total)
    partner = jnp.where(o0 == 1, v1[:, leaf:], jnp.where(o0 == 2, v2[:, leaf:], v3[:, leaf:]))
    out[:, 0:leaf] = result
    out[:, leaf:] = jnp.concatenate([partner[:, 0:64], times_t(result, bases[...])], axis=1)


def gather_kernel(scalars, received, *refs):
    high, out = refs[-2:]
    x, y, o2, o3 = scalars[X], scalars[Y], scalars[O2], scalars[O3]
    left = lax.broadcasted_iota(jnp.int32, (16, 128), 1) < 64
    total = jnp.zeros((16, 128), F32)
    for j in range(4):
        top = jnp.zeros((16, 128), F32)
        for i in range(4):
            p = j * 4 + i
            offset = jnp.bitwise_xor(x, i)
            here = y == j
            hit2 = here & (offset == o2 // 2)
            hit3 = here & (offset == o3)
            total += jnp.where((left & hit2) | (~left & hit3), received[p, 0:16, :], 0.0)
            top += received[p, 16:32, :]
        out[j * 16 : (j + 1) * 16, :] = top
    high[...] = total


def lower_blocks(high, mine, other, table, own):
    start = own.shape[1] - 128
    parts = [high[:, 64:128]]
    for side in (mine, other):
        parts += [side[j * 16 : (j + 1) * 16, 0:64] for j in range(4)]
    field = times_t(jnp.concatenate(parts, axis=1), table[...])
    return field, jnp.concatenate([own[:, start + 64 :], high[:, 0:64]], axis=1)


def lower_kernel(high, mine, other, table, own, *refs):
    out = refs[-1]
    field, second = lower_blocks(high, mine, other, table, own)
    norm = sum(side[j * 16 : (j + 1) * 16, 64:128] for side in (mine, other) for j in range(4))
    first = jnp.concatenate([field, norm], axis=1)
    for i in range(out.shape[0]):
        out[i, 0:16, :] = first
        out[i, 16:32, :] = second


def first_lower_kernel(scalars, high, mine, other, table, own, skeletons, second, moved, out):
    field, lifted = lower_blocks(high, mine, other, table, own)
    first = jnp.concatenate([field, own[:, 0:64]], axis=1)
    _, k1, k2 = skeleton_offsets(scalars)
    third = jnp.where(scalars[O2] > 1, moved[...], second[...])
    blocks = [packed(skeletons[0]), packed(skeletons[1]), third]
    for i in range(out.shape[0]):
        offset = jnp.bitwise_xor(scalars[Z], i)
        block = jnp.where(offset == k1, blocks[1], blocks[0])
        out[i, 0:16, :] = first
        out[i, 16:32, :] = lifted
        out[i, 32:64, :] = jnp.where((offset == k2) | (offset == 0), blocks[2], block)


def apply_far(scalars, received, table, bases, near):
    leaf = bases.shape[1]
    z, o0, o1, o2 = scalars[Z], scalars[O0], scalars[O1], scalars[O2]
    start = received.shape[1] > 32
    left = lax.broadcasted_iota(jnp.int32, (16, 128), 1) < 64
    sums = [jnp.zeros((16, 128), F32) for _ in range(2)]
    for i in range(received.shape[0]):
        offset = jnp.bitwise_xor(z, i)
        hit1 = offset // 2 == o1
        hit2 = offset // 4 == jnp.bitwise_and(o2, 1)
        block = received[i, 0:16, :]
        sums[0] += jnp.where(left | (offset == o0), block, 0.0) if start else block
        sums[1] += jnp.where((left & hit1) | (~left & hit2), received[i, 16:32, :], 0.0)
    moment = sums[0][:, 64:128] if start else near[:, leaf : leaf + 64]
    parts = [moment, sums[1], sums[0][:, 0:64]]
    field = times_t(jnp.concatenate(parts, axis=1), table[...])
    pair = stacked(field)
    far = halves(dot(pair, bases[0:64, :]) + dot(pair, bases[64:128, :]))
    return near[:, 0:leaf] + far, sums[0][:, 64:65], field


def moment_of(near, field, gram):
    return near[:, near.shape[1] - 64 :] + times(field, gram[...])


def first_kernel(
    scalars, received, skeletons, bases, near, chain, table, v1, out
):
    table[...] = low_couplings(scalars, skeletons, received, chain)
    image, _, _ = apply_far(scalars, received, table, bases, near)
    own = times_t(image, bases[...])
    write_moments(v1, out, image, own, image, chain)


def second_kernel(
    scalars, received, table, bases, near, gram, chain, v2, scaled, sums, out
):
    image, norm, field = apply_far(scalars, received, table, bases, near)
    v2[...] = image
    sums[...] = jnp.broadcast_to(norm, sums.shape)
    size = 1.0 / jnp.sqrt(norm)
    own = moment_of(near, field, gram) * size
    write_moments(scaled, out, image * size, own, image, chain)


def third_kernel(
    scalars, received, table, bases, near, gram, chain, v1, sums, image, step, out
):
    product, along, field = apply_far(scalars, received, table, bases, near)
    leaf = product.shape[1]
    norm = sums[:, 0:1]
    size = norm / along
    back = size * jnp.sqrt(norm)
    new = v1[:, 0:leaf] - back * product
    own = v1[:, leaf : leaf + 64] - back * moment_of(near, field, gram)
    step[...] = jnp.broadcast_to(size, step.shape)
    write_moments(image, out, new, own, new, chain)


def diagonal():
    rows = lax.broadcasted_iota(jnp.int32, (16, 128), 0)
    return rows == lax.broadcasted_iota(jnp.int32, (16, 128), 1)


def fourth_kernel(scalars, received, table, bases, near, v2, sums, along, fresh, out):
    product, norm, _ = apply_far(scalars, received, table, bases, near)
    new = product + (norm / sums[:, 0:1]) * v2[...]
    along[...] = new
    fresh[...] = jnp.broadcast_to(norm, fresh.shape)
    share = jnp.sum(new * new, axis=1, keepdims=True)
    line = jnp.sum(jnp.where(diagonal(), share, 0.0), axis=0, keepdims=True)
    out[...] = jnp.broadcast_to(line, out.shape)


def last_kernel(shares, rhs, v1, v2, image, along, sums, fresh, step, iterate, residual):
    leaf = rhs.shape[1]
    norm = fresh[:, 0:1]
    first = step[:, 0:1]
    line = jnp.sum(shares[...], axis=0, keepdims=True)
    second = norm / jnp.sum(jnp.where(diagonal(), line, 0.0), axis=1, keepdims=True)
    beta = norm / sums[:, 0:1]
    start = v1[:, 0:leaf]
    iterate[...] = first * start + second * (image[:, 0:leaf] + beta * start)
    residual[...] = rhs[...] - first * v2[...] - second * along[...]


SMEM = pl.BlockSpec(memory_space=pltpu.SMEM)
VMEM = pl.BlockSpec(memory_space=pltpu.VMEM)


def shaped(*shape, dtype=F32):
    return jax.ShapeDtypeStruct(shape, dtype)


MIB = 1024 * 1024
ANY = pl.BlockSpec(memory_space=pl.ANY)


def call(kernel, outs, scalars, arrays, name, after=(), limit=16, flops=100000, scratch=(), alias=None):
    def body(*refs):
        if scalars:
            kernel(places(refs[0]), *refs[1:])
        else:
            kernel(*refs)

    return pl.pallas_call(
        body,
        out_shape=outs,
        in_specs=[SMEM] * len(scalars) + [VMEM] * len(arrays) + [ANY] * len(after),
        out_specs=jax.tree.map(lambda a: ANY if len(a.shape) == 4 else VMEM, outs),
        scratch_shapes=list(scratch),
        input_output_aliases=alias or {},
        name=name,
        compiler_params=pltpu.CompilerParams(vmem_limit_bytes=limit * MIB),
        cost_estimate=pl.CostEstimate(flops=flops, bytes_accessed=500000, transcendentals=0),
    )(*scalars, *arrays, *after)


def build(scalars, own, others, choice, near, after, name, kernels=()):
    leaf = own.shape[1]
    tiles = leaf // TILE
    return call(
        functools.partial(build_kernel, choice=choice),
        (shaped(3, 2, leaf, leaf, dtype=BF16), shaped(16, leaf)),
        [scalars],
        [own, *others, *([] if near is None else [near])],
        name,
        after=[*after, *kernels],
        limit=50,
        flops=4000000000,
        alias={3 + len(others) + len(after): 0} if kernels else None,
        scratch=[
            pltpu.VMEM((DEPTH, leaf), BF16),
            pltpu.VMEM((DEPTH, leaf), BF16),
            pltpu.VMEM((2, TILE, leaf), F32),
            pltpu.VMEM((tiles, 2, TILE, leaf), BF16),
            pltpu.SemaphoreType.DMA((tiles,)),
        ],
    )


def near_product(scalars, vectors, bases, kernels, after):
    leaf = kernels.shape[2]
    return call(
        near_kernel,
        shaped(*vectors[0].shape),
        [scalars],
        [*vectors, bases],
        "near",
        after=[kernels, after],
        limit=50,
        flops=4000000000,
        scratch=[
            pltpu.VMEM((3, 2, leaf, leaf), BF16),
            pltpu.SemaphoreType.DMA((3 * leaf // TILE,)),
        ],
    )


def along_z(v, offset):
    return lax.ppermute(v, "z", [(i, i ^ offset) for i in range(8)])


def other_core(v):
    return lax.ppermute(v, "core", [(0, 1), (1, 0)])


def over_z(v):
    return lax.all_to_all(v, "z", 0, 0)


def over_yx(v):
    return lax.all_to_all(v, ("y", "x"), 0, 0)


def local(
    rhs,
    embeddings,
    leaf_order,
    basis,
    transfer_maps,
    skeletons,
    top_skeletons,
    near_lists,
    far_lists,
    top_lists,
):
    top = lax.axis_index("y") * 2 + lax.axis_index("core")
    listed = lax.dynamic_index_in_dim(top_lists, top, 0, keepdims=False)
    scalars = far_lists[:, 0]
    chain_skeletons = skeletons[:, 0]
    tops = top_skeletons.reshape(4, 2, 64, 64)

    row = shaped(16, 1024)
    long = shaped(16, 1152)
    thin = shaped(16, 128)
    wire = shaped(16, 32, 128)
    both = jnp.concatenate([embeddings, rhs], axis=0)
    one = along_z(both, 1)
    two = along_z(both, 2)
    three_off = along_z(two, 1)
    bases, chain, tail, gram, own, outgoing, second = call(
        prepare_kernel,
        (
            shaped(128, 1024, dtype=BF16),
            shaped(64, 512, dtype=BF16),
            shaped(64, 64),
            shaped(64, 128, dtype=BF16),
            thin,
            shaped(16, 64, 128),
            shaped(32, 128),
        ),
        [scalars],
        [leaf_order, basis, transfer_maps[:, 0], chain_skeletons, rhs],
        "prepare",
        limit=60,
    )

    def gather(spread, after=()):
        high, mine = call(
            gather_kernel, (thin, shaped(64, 128)), [scalars], [spread], "gather", after=after
        )
        return high, mine, other_core(mine)

    kernels, near = build(scalars, both, [], None, None, [two], "build_own")
    from_yx = over_yx(outgoing)
    second_moved = lax.ppermute(second, "x", [(i, i ^ 1) for i in range(4)])
    spread = gather(from_yx, [near, second_moved])
    top_table = call(
        top_kernel,
        shaped(128, 576, dtype=BF16),
        [scalars, listed],
        [chain_skeletons, from_yx, tops, tail],
        "tops",
    )
    outgoing = call(
        first_lower_kernel,
        shaped(8, 64, 128),
        [scalars],
        [*spread, top_table, own, chain_skeletons, second, second_moved],
        "lower",
    )
    kernels, near = build(
        scalars, both, [two, one], 1, near, [outgoing, three_off], "build_a", [kernels]
    )
    kernels, near = build(
        scalars, both, [two, three_off], 3, near, [outgoing], "build_b", [kernels]
    )
    table, v1, outgoing = call(
        first_kernel,
        (shaped(128, 256, dtype=BF16), long, wire),
        [scalars],
        [over_z(outgoing), chain_skeletons, bases, near, chain],
        "first",
    )

    def operate(extended, outgoing):
        moved = [along_z(extended, o) for o in (1, 2, 3)]
        spread = gather(over_yx(outgoing))
        lower = call(
            lower_kernel,
            shaped(8, 32, 128),
            [],
            [*spread, top_table, extended],
            "lower",
            after=moved,
        )
        near = near_product(scalars, [extended, *moved], bases, kernels, lower)
        return over_z(lower), table, bases, near

    v2, scaled, sums, outgoing = call(
        second_kernel,
        (row, long, thin, wire),
        [scalars],
        [*operate(v1, outgoing), gram, chain],
        "second",
    )
    image, step, outgoing = call(
        third_kernel,
        (long, thin, wire),
        [scalars],
        [*operate(scaled, outgoing), gram, chain, v1, sums],
        "third",
    )
    along, fresh, outgoing = call(
        fourth_kernel,
        (row, thin, shaped(256, 128)),
        [scalars],
        [*operate(image, outgoing), v2, sums],
        "fourth",
    )
    shares = lax.all_to_all(outgoing, ("y", "core", "x", "z"), 0, 0, tiled=True)
    return call(
        last_kernel,
        (row, row),
        [],
        [shares, rhs, v1, v2, image, along, sums, fresh, step],
        "last",
    )


def solution(mesh):
    axes = ("y", "core", "x", "z")
    fine = Mesh(mesh.devices.reshape(4, 2, 4, 8), axes)
    placed = (
        P(None, axes),
        P(None, axes),
        P(axes, None),
        P(None, axes),
        P(None, axes, None, None),
        P(None, axes, None, None),
        P(),
        P(axes, None),
        P(None, axes),
        P(),
    )
    return jax.shard_map(
        local,
        mesh=fine,
        in_specs=placed,
        out_specs=(P(None, axes), P(None, axes)),
        check_vma=False,
    )
```

```python
import functools
import math

import jax
import jax.numpy as jnp
from jax import lax
from jax.experimental import pallas as pl
from jax.experimental.pallas import tpu as pltpu
from jax.sharding import Mesh
from jax.sharding import PartitionSpec as P

F32 = jnp.float32
BF16 = jnp.bfloat16
HIGHEST = lax.Precision.HIGHEST
NOISE = 0.5
SCALE = math.sqrt(5.0) / 2.8
LOG2E = math.log2(math.e)
DEPTH = 208
TILE = 256
AHEAD = 4

Z, X, Y, CORE, O0, O1, O2, O3 = range(8)


def dot(a, b, ca=1, cb=0, precision=None):
    return lax.dot_general(
        a, b, (((ca,), (cb,)), ((), ())), precision=precision, preferred_element_type=F32
    )


def split(a):
    high = a.astype(BF16)
    return high, (a - high.astype(F32)).astype(BF16)


def stacked(a):
    return jnp.concatenate(split(a), axis=0)


def halves(a):
    n = a.shape[0] // 2
    return a[:n] + a[n:]


def places(partners):
    y, core, x, z = (lax.axis_index(a) for a in ("y", "core", "x", "z"))
    leaf = ((y * 2 + core) * 4 + x) * 8 + z
    return [z, x, y, core] + [jnp.bitwise_xor(partners[h], leaf // 2**h) for h in range(4)]


def paired(a, axis):
    return jnp.concatenate(split(a), axis=axis)


def times(a, pair):
    both = halves(dot(stacked(a), pair))
    n = both.shape[1] // 2
    return both[:, :n] + both[:, n:]


def times_t(a, pair):
    both = halves(dot(stacked(a), pair, 1, 1))
    n = both.shape[1] // 2
    return both[:, :n] + both[:, n:]


def square_sum(v):
    return jnp.broadcast_to(jnp.sum(v * v, axis=1, keepdims=True), (v.shape[0], 64))


def lift(own, chain):
    lifted = times(own, chain)
    return jnp.concatenate([own, lifted[:, 0:64]], axis=1), lifted[:, 64:192], lifted[:, 192:256]


def write_moments(extended, out, v, own, weighed, chain):
    first, middle, top = lift(own, chain[...])
    last = jnp.concatenate([top, square_sum(weighed)], axis=1)
    for i in range(out.shape[0]):
        out[i, 0:16, :] = middle
        out[i, 16:32, :] = last
    extended[:, 0 : v.shape[1]] = v
    extended[:, v.shape[1] :] = first


def packed(skeleton):
    return jnp.concatenate([skeleton[0:32], skeleton[32:64]], axis=1)


def unpacked(block):
    return jnp.concatenate([block[:, 0:64], block[:, 64:128]], axis=0)


def skeleton_offsets(scalars):
    o0, o1 = scalars[O0], scalars[O1]
    second = jnp.where(o1 > 1, o1 * 2, jnp.where(o0 == 2, 3, 2))
    return o0, second, jnp.where(o1 == 3, 4, 7)


def prepare_kernel(
    scalars, order, basis, maps, skeletons, rhs, bases, chain, tail, gram, own, wire, second
):
    both = stacked(basis[...])
    leaf = basis.shape[1]
    for t in range(leaf // TILE):
        rows = lax.broadcasted_iota(jnp.int32, (TILE, leaf), 0) + t * TILE
        one_hot = jnp.where(rows == order[...], 1.0, 0.0).astype(BF16)
        bases[:, t * TILE : (t + 1) * TILE] = dot(both, one_hot, 1, 1).astype(BF16)
    p1 = maps[0]
    p2 = dot(p1, maps[1], precision=HIGHEST)
    p3 = dot(p2, maps[2], precision=HIGHEST)
    e34 = dot(maps[3], maps[4], precision=HIGHEST)
    p5 = dot(p3, e34, precision=HIGHEST)
    tail[...] = e34
    chain[...] = paired(jnp.concatenate([p1, p2, p3, p5], axis=1), 1)
    products = dot(bases[...], bases[...], 1, 1)
    products = halves(products[:, 0:64] + products[:, 64:128])
    gram[...] = paired(products, 1)
    first, middle, top = lift(times_t(rhs[...], bases[...]), chain[...])
    own[...] = first
    last = jnp.concatenate([top, jnp.zeros_like(top)], axis=1)
    for i in range(wire.shape[0]):
        wire[i, 0:16, :] = middle
        wire[i, 16:32, :] = last
        wire[i, 32:64, :] = packed(skeletons[3])
    second[...] = packed(skeletons[2])


def matern(first, second):
    turned = first.T
    squares = (
        jnp.sum(turned * turned, axis=1, keepdims=True)
        + jnp.sum(second * second, axis=0, keepdims=True)
        - 2.0 * dot(turned, second, precision=HIGHEST)
    )
    s = SCALE * jnp.sqrt(jnp.maximum(squares, 0.0))
    return (1.0 + s + s * s * (1.0 / 3.0)) * jnp.exp(-s)


def top_kernel(scalars, listed, skeletons, from_yx, tops, tail, out):
    x, y, core = scalars[X], scalars[Y], scalars[CORE]
    partner = unpacked(from_yx[y * 4 + jnp.bitwise_xor(x, scalars[O3]), 32:64, :])
    others = []
    masks = []
    for flip in (0, 1):
        for j in range(4):
            side = jnp.bitwise_xor(core, flip)
            others.append(tops[j, side])
            hits = sum((listed[k] == j * 2 + side).astype(F32) for k in range(4))
            masks.append(jnp.full((64, 64), hits, F32))
    top = matern(tops[y, core], jnp.concatenate(others, axis=1))
    top = dot(tail[...], top * jnp.concatenate(masks, axis=1), precision=HIGHEST)
    out[...] = paired(jnp.concatenate([matern(skeletons[3], partner), top], axis=1), 0)


def low_couplings(scalars, skeletons, from_z, chain):
    z = scalars[Z]
    down = chain[:, 0:256].astype(F32) + chain[:, 256:512].astype(F32)
    pieces = []
    for h, offset in enumerate(skeleton_offsets(scalars)):
        if h == 2:
            offset = jnp.where(scalars[O2] % 2 == 1, offset, 0)
        partner = unpacked(from_z[jnp.bitwise_xor(z, offset), 32:64, :])
        coupling = matern(skeletons[h], partner)
        if h > 0:
            coupling = dot(down[:, (h - 1) * 64 : h * 64], coupling, precision=HIGHEST)
        pieces.append(coupling)
    return paired(jnp.concatenate(pieces + [down[:, 128:192]], axis=1), 0)


def three(a):
    high = a.astype(BF16).astype(F32)
    middle = (a - high).astype(BF16).astype(F32)
    return high, middle, a - high - middle


def augment(points, target, turned):
    leaf = points.shape[1]
    high, low = split(points * SCALE)
    h32, l32 = high.astype(F32), low.astype(F32)
    sums = three(jnp.sum(h32 * h32 + 2.0 * (h32 * l32), axis=0, keepdims=True))
    row = lax.broadcasted_iota(jnp.int32, (16, leaf), 0)
    first, ones = (0, 3) if turned else (3, 0)
    rest = jnp.where((row >= ones) & (row < ones + 3), 1.0, 0.0)
    for i in range(3):
        rest = jnp.where(row == first + i, sums[i], rest)
    if turned:
        high, low = (-2.0 * h32).astype(BF16), (-2.0 * l32).astype(BF16)
    target[0:64, :] = high
    target[64:128, :] = high if turned else low
    target[128:192, :] = low if turned else high
    target[192:208, :] = rest.astype(BF16)


def entries(squares, kernel):
    wide = 512
    tall = 32
    for r in range(0, squares.shape[0], tall):
        for c in range(0, squares.shape[1], wide):
            s2 = jnp.maximum(squares[r : r + tall, c : c + wide], 1e-30)
            s = s2 * lax.rsqrt(s2)
            value = (1.0 + s + s2 * (1.0 / 3.0)) * jnp.exp2(s * -LOG2E)
            high, low = split(value)
            kernel[0, r : r + tall, c : c + wide] = high
            kernel[1, r : r + tall, c : c + wide] = low


def build_kernel(scalars, own, *refs, choice):
    if choice is None:
        whole, near, aug, left, squares, kernel, sems = refs[-7:]
        both = own[...]
        near[...] = NOISE * own[64:80, :]
        slot = 0
    else:
        yes, no, begin = refs[:3]
        whole, near, aug, left, squares, kernel, sems = refs[-7:]
        both = jnp.where(scalars[O0] == choice, yes[...], no[...])
        near[...] = begin[...]
        slot = (choice + 1) // 2
    augment(own[0:64, :], aug, False)
    augment(both[0:64, :], left, True)
    pair = stacked(both[64:80, :])
    leaf = own.shape[1]
    tiles = leaf // TILE
    copies = []
    total = None
    squares[0] = dot(left[:, 0:TILE], aug[...], 0, 0)
    for t in range(tiles):
        cols = slice(t * TILE, (t + 1) * TILE)
        if t + 1 < tiles:
            squares[(t + 1) % 2] = dot(left[:, (t + 1) * TILE : (t + 2) * TILE], aug[...], 0, 0)
        entries(squares.at[t % 2], kernel.at[t])
        part = dot(pair[:, cols], kernel[t, 0]) + dot(pair[:, cols], kernel[t, 1])
        total = part if total is None else total + part
        rows = pl.ds(t * TILE, TILE)
        copies.append(
            pltpu.make_async_copy(kernel.at[t], whole.at[slot, :, rows, :], sems.at[t])
        )
        copies[t].start()
    near[...] += halves(total)
    for copy in copies:
        copy.wait()


def near_kernel(scalars, v, v1, v2, v3, bases, kernels, after, out, held, sems):
    leaf = kernels.shape[2]
    tiles = leaf // TILE
    copies = []
    for e in range(3):
        for t in range(tiles):
            rows = pl.ds(t * TILE, TILE)
            copies.append(
                pltpu.make_async_copy(
                    kernels.at[e, :, rows, :], held.at[e, :, rows, :], sems.at[e * tiles + t]
                )
            )
    for copy in copies[:AHEAD]:
        copy.start()
    o0 = scalars[O0]
    own = v[:, 0:leaf]
    second = jnp.where(o0 == 1, v2[:, 0:leaf], v1[:, 0:leaf])
    third = jnp.where(o0 == 3, v2[:, 0:leaf], v3[:, 0:leaf])
    total = None
    for e, vector in enumerate((own, second, third)):
        pair = stacked(vector)
        for t in range(tiles):
            rows = slice(t * TILE, (t + 1) * TILE)
            copies[e * tiles + t].wait()
            if e * tiles + t + AHEAD < len(copies):
                copies[e * tiles + t + AHEAD].start()
            part = dot(pair[:, rows], held[e, 0, rows, :]) + dot(pair[:, rows], held[e, 1, rows, :])
            total = part if total is None else total + part
    result = NOISE * own + halves(total)
    partner = jnp.where(o0 == 1, v1[:, leaf:], jnp.where(o0 == 2, v2[:, leaf:], v3[:, leaf:]))
    out[:, 0:leaf] = result
    out[:, leaf:] = jnp.concatenate([partner[:, 0:64], times_t(result, bases[...])], axis=1)


def gather_kernel(scalars, received, *refs):
    high, out = refs[-2:]
    x, y, o2, o3 = scalars[X], scalars[Y], scalars[O2], scalars[O3]
    left = lax.broadcasted_iota(jnp.int32, (16, 128), 1) < 64
    total = jnp.zeros((16, 128), F32)
    for j in range(4):
        top = jnp.zeros((16, 128), F32)
        for i in range(4):
            p = j * 4 + i
            offset = jnp.bitwise_xor(x, i)
            here = y == j
            hit2 = here & (offset == o2 // 2)
            hit3 = here & (offset == o3)
            total += jnp.where((left & hit2) | (~left & hit3), received[p, 0:16, :], 0.0)
            top += received[p, 16:32, :]
        out[j * 16 : (j + 1) * 16, :] = top
    high[...] = total


def lower_blocks(high, mine, other, table, own):
    start = own.shape[1] - 128
    parts = [high[:, 64:128]]
    for side in (mine, other):
        parts += [side[j * 16 : (j + 1) * 16, 0:64] for j in range(4)]
    field = times_t(jnp.concatenate(parts, axis=1), table[...])
    return field, jnp.concatenate([own[:, start + 64 :], high[:, 0:64]], axis=1)


def lower_kernel(high, mine, other, table, own, *refs):
    out = refs[-1]
    field, second = lower_blocks(high, mine, other, table, own)
    norm = sum(side[j * 16 : (j + 1) * 16, 64:128] for side in (mine, other) for j in range(4))
    first = jnp.concatenate([field, norm], axis=1)
    for i in range(out.shape[0]):
        out[i, 0:16, :] = first
        out[i, 16:32, :] = second


def first_lower_kernel(scalars, high, mine, other, table, own, skeletons, second, moved, out):
    field, lifted = lower_blocks(high, mine, other, table, own)
    first = jnp.concatenate([field, own[:, 0:64]], axis=1)
    _, k1, k2 = skeleton_offsets(scalars)
    third = jnp.where(scalars[O2] > 1, moved[...], second[...])
    blocks = [packed(skeletons[0]), packed(skeletons[1]), third]
    for i in range(out.shape[0]):
        offset = jnp.bitwise_xor(scalars[Z], i)
        block = jnp.where(offset == k1, blocks[1], blocks[0])
        out[i, 0:16, :] = first
        out[i, 16:32, :] = lifted
        out[i, 32:64, :] = jnp.where((offset == k2) | (offset == 0), blocks[2], block)


def apply_far(scalars, received, table, bases, near):
    leaf = bases.shape[1]
    z, o0, o1, o2 = scalars[Z], scalars[O0], scalars[O1], scalars[O2]
    start = received.shape[1] > 32
    left = lax.broadcasted_iota(jnp.int32, (16, 128), 1) < 64
    sums = [jnp.zeros((16, 128), F32) for _ in range(2)]
    for i in range(received.shape[0]):
        offset = jnp.bitwise_xor(z, i)
        hit1 = offset // 2 == o1
        hit2 = offset // 4 == jnp.bitwise_and(o2, 1)
        block = received[i, 0:16, :]
        sums[0] += jnp.where(left | (offset == o0), block, 0.0) if start else block
        sums[1] += jnp.where((left & hit1) | (~left & hit2), received[i, 16:32, :], 0.0)
    moment = sums[0][:, 64:128] if start else near[:, leaf : leaf + 64]
    parts = [moment, sums[1], sums[0][:, 0:64]]
    field = times_t(jnp.concatenate(parts, axis=1), table[...])
    pair = stacked(field)
    far = halves(dot(pair, bases[0:64, :]) + dot(pair, bases[64:128, :]))
    return near[:, 0:leaf] + far, sums[0][:, 64:65], field


def moment_of(near, field, gram):
    return near[:, near.shape[1] - 64 :] + times(field, gram[...])


def first_kernel(
    scalars, received, skeletons, bases, near, chain, table, v1, out
):
    table[...] = low_couplings(scalars, skeletons, received, chain)
    image, _, _ = apply_far(scalars, received, table, bases, near)
    own = times_t(image, bases[...])
    write_moments(v1, out, image, own, image, chain)


def second_kernel(
    scalars, received, table, bases, near, gram, chain, v2, scaled, sums, out
):
    image, norm, field = apply_far(scalars, received, table, bases, near)
    v2[...] = image
    sums[...] = jnp.broadcast_to(norm, sums.shape)
    size = 1.0 / jnp.sqrt(norm)
    own = moment_of(near, field, gram) * size
    write_moments(scaled, out, image * size, own, image, chain)


def third_kernel(
    scalars, received, table, bases, near, gram, chain, v1, sums, image, step, out
):
    product, along, field = apply_far(scalars, received, table, bases, near)
    leaf = product.shape[1]
    norm = sums[:, 0:1]
    size = norm / along
    back = size * jnp.sqrt(norm)
    new = v1[:, 0:leaf] - back * product
    own = v1[:, leaf : leaf + 64] - back * moment_of(near, field, gram)
    step[...] = jnp.broadcast_to(size, step.shape)
    write_moments(image, out, new, own, new, chain)


def diagonal():
    rows = lax.broadcasted_iota(jnp.int32, (16, 128), 0)
    return rows == lax.broadcasted_iota(jnp.int32, (16, 128), 1)


def fourth_kernel(scalars, received, table, bases, near, v2, sums, along, fresh, out):
    product, norm, _ = apply_far(scalars, received, table, bases, near)
    new = product + (norm / sums[:, 0:1]) * v2[...]
    along[...] = new
    fresh[...] = jnp.broadcast_to(norm, fresh.shape)
    share = jnp.sum(new * new, axis=1, keepdims=True)
    line = jnp.sum(jnp.where(diagonal(), share, 0.0), axis=0, keepdims=True)
    out[...] = jnp.broadcast_to(line, out.shape)


def last_kernel(shares, rhs, v1, v2, image, along, sums, fresh, step, iterate, residual):
    leaf = rhs.shape[1]
    norm = fresh[:, 0:1]
    first = step[:, 0:1]
    line = jnp.sum(shares[...], axis=0, keepdims=True)
    second = norm / jnp.sum(jnp.where(diagonal(), line, 0.0), axis=1, keepdims=True)
    beta = norm / sums[:, 0:1]
    start = v1[:, 0:leaf]
    iterate[...] = first * start + second * (image[:, 0:leaf] + beta * start)
    residual[...] = rhs[...] - first * v2[...] - second * along[...]


SMEM = pl.BlockSpec(memory_space=pltpu.SMEM)
VMEM = pl.BlockSpec(memory_space=pltpu.VMEM)


def shaped(*shape, dtype=F32):
    return jax.ShapeDtypeStruct(shape, dtype)


MIB = 1024 * 1024
ANY = pl.BlockSpec(memory_space=pl.ANY)


def call(kernel, outs, scalars, arrays, name, after=(), limit=16, flops=100000, scratch=(), alias=None):
    def body(*refs):
        if scalars:
            kernel(places(refs[0]), *refs[1:])
        else:
            kernel(*refs)

    return pl.pallas_call(
        body,
        out_shape=outs,
        in_specs=[SMEM] * len(scalars) + [VMEM] * len(arrays) + [ANY] * len(after),
        out_specs=jax.tree.map(lambda a: ANY if len(a.shape) == 4 else VMEM, outs),
        scratch_shapes=list(scratch),
        input_output_aliases=alias or {},
        name=name,
        compiler_params=pltpu.CompilerParams(vmem_limit_bytes=limit * MIB),
        cost_estimate=pl.CostEstimate(flops=flops, bytes_accessed=500000, transcendentals=0),
    )(*scalars, *arrays, *after)


def build(scalars, own, others, choice, near, after, name, kernels=()):
    leaf = own.shape[1]
    tiles = leaf // TILE
    return call(
        functools.partial(build_kernel, choice=choice),
        (shaped(3, 2, leaf, leaf, dtype=BF16), shaped(16, leaf)),
        [scalars],
        [own, *others, *([] if near is None else [near])],
        name,
        after=[*after, *kernels],
        limit=50,
        flops=4000000000,
        alias={3 + len(others) + len(after): 0} if kernels else None,
        scratch=[
            pltpu.VMEM((DEPTH, leaf), BF16),
            pltpu.VMEM((DEPTH, leaf), BF16),
            pltpu.VMEM((2, TILE, leaf), F32),
            pltpu.VMEM((tiles, 2, TILE, leaf), BF16),
            pltpu.SemaphoreType.DMA((tiles,)),
        ],
    )


def near_product(scalars, vectors, bases, kernels, after):
    leaf = kernels.shape[2]
    return call(
        near_kernel,
        shaped(*vectors[0].shape),
        [scalars],
        [*vectors, bases],
        "near",
        after=[kernels, after],
        limit=50,
        flops=4000000000,
        scratch=[
            pltpu.VMEM((3, 2, leaf, leaf), BF16),
            pltpu.SemaphoreType.DMA((3 * leaf // TILE,)),
        ],
    )


def along_z(v, offset):
    return lax.ppermute(v, "z", [(i, i ^ offset) for i in range(8)])


def other_core(v):
    return lax.ppermute(v, "core", [(0, 1), (1, 0)])


def over_z(v):
    return lax.all_to_all(v, "z", 0, 0)


def over_yx(v):
    return lax.all_to_all(v, ("y", "x"), 0, 0)


def local(
    rhs,
    embeddings,
    leaf_order,
    basis,
    transfer_maps,
    skeletons,
    top_skeletons,
    near_lists,
    far_lists,
    top_lists,
):
    top = lax.axis_index("y") * 2 + lax.axis_index("core")
    listed = lax.dynamic_index_in_dim(top_lists, top, 0, keepdims=False)
    scalars = far_lists[:, 0]
    chain_skeletons = skeletons[:, 0]
    tops = top_skeletons.reshape(4, 2, 64, 64)

    row = shaped(16, 1024)
    long = shaped(16, 1152)
    thin = shaped(16, 128)
    wire = shaped(16, 32, 128)
    both = jnp.concatenate([embeddings, rhs], axis=0)
    one = along_z(both, 1)
    two = along_z(both, 2)
    three_off = along_z(two, 1)
    bases, chain, tail, gram, own, outgoing, second = call(
        prepare_kernel,
        (
            shaped(128, 1024, dtype=BF16),
            shaped(64, 512, dtype=BF16),
            shaped(64, 64),
            shaped(64, 128, dtype=BF16),
            thin,
            shaped(16, 64, 128),
            shaped(32, 128),
        ),
        [scalars],
        [leaf_order, basis, transfer_maps[:, 0], chain_skeletons, rhs],
        "prepare",
        limit=60,
    )

    def gather(spread, after=()):
        high, mine = call(
            gather_kernel, (thin, shaped(64, 128)), [scalars], [spread], "gather", after=after
        )
        return high, mine, other_core(mine)

    kernels, near = build(scalars, both, [], None, None, [two], "build_own")
    from_yx = over_yx(outgoing)
    second_moved = lax.ppermute(second, "x", [(i, i ^ 1) for i in range(4)])
    spread = gather(from_yx, [near, second_moved])
    top_table = call(
        top_kernel,
        shaped(128, 576, dtype=BF16),
        [scalars, listed],
        [chain_skeletons, from_yx, tops, tail],
        "tops",
    )
    outgoing = call(
        first_lower_kernel,
        shaped(8, 64, 128),
        [scalars],
        [*spread, top_table, own, chain_skeletons, second, second_moved],
        "lower",
    )
    kernels, near = build(
        scalars, both, [two, one], 1, near, [outgoing, three_off], "build_a", [kernels]
    )
    kernels, near = build(
        scalars, both, [two, three_off], 3, near, [outgoing], "build_b", [kernels]
    )
    table, v1, outgoing = call(
        first_kernel,
        (shaped(128, 256, dtype=BF16), long, wire),
        [scalars],
        [over_z(outgoing), chain_skeletons, bases, near, chain],
        "first",
    )

    def operate(extended, outgoing):
        moved = [along_z(extended, o) for o in (1, 2, 3)]
        spread = gather(over_yx(outgoing))
        lower = call(
            lower_kernel,
            shaped(8, 32, 128),
            [],
            [*spread, top_table, extended],
            "lower",
            after=moved,
        )
        near = near_product(scalars, [extended, *moved], bases, kernels, lower)
        return over_z(lower), table, bases, near

    v2, scaled, sums, outgoing = call(
        second_kernel,
        (row, long, thin, wire),
        [scalars],
        [*operate(v1, outgoing), gram, chain],
        "second",
    )
    image, step, outgoing = call(
        third_kernel,
        (long, thin, wire),
        [scalars],
        [*operate(scaled, outgoing), gram, chain, v1, sums],
        "third",
    )
    along, fresh, outgoing = call(
        fourth_kernel,
        (row, thin, shaped(256, 128)),
        [scalars],
        [*operate(image, outgoing), v2, sums],
        "fourth",
    )
    shares = lax.all_to_all(outgoing, ("y", "core", "x", "z"), 0, 0, tiled=True)
    return call(
        last_kernel,
        (row, row),
        [],
        [shares, rhs, v1, v2, image, along, sums, fresh, step],
        "last",
    )


def solution(mesh):
    axes = ("y", "core", "x", "z")
    fine = Mesh(mesh.devices.reshape(4, 2, 4, 8), axes)
    placed = (
        P(None, axes),
        P(None, axes),
        P(axes, None),
        P(None, axes),
        P(None, axes, None, None),
        P(None, axes, None, None),
        P(),
        P(axes, None),
        P(None, axes),
        P(),
    )
    return jax.shard_map(
        local,
        mesh=fine,
        in_specs=placed,
        out_specs=(P(None, axes), P(None, axes)),
        check_vma=False,
    )
```

```python
import functools
import math

import jax
import jax.numpy as jnp
from jax import lax
from jax.experimental import pallas as pl
from jax.experimental.pallas import tpu as pltpu
from jax.sharding import Mesh
from jax.sharding import PartitionSpec as P

F32 = jnp.float32
BF16 = jnp.bfloat16
HIGHEST = lax.Precision.HIGHEST
NOISE = 0.5
SCALE = math.sqrt(5.0) / 2.8
LOG2E = math.log2(math.e)
DEPTH = 208
TILE = 256

Z, X, Y, CORE, O0, O1, O2, O3 = range(8)


def dot(a, b, ca=1, cb=0, precision=None):
    return lax.dot_general(
        a, b, (((ca,), (cb,)), ((), ())), precision=precision, preferred_element_type=F32
    )


def split(a):
    high = a.astype(BF16)
    return high, (a - high.astype(F32)).astype(BF16)


def stacked(a):
    return jnp.concatenate(split(a), axis=0)


def halves(a):
    n = a.shape[0] // 2
    return a[:n] + a[n:]


def places(partners):
    y, core, x, z = (lax.axis_index(a) for a in ("y", "core", "x", "z"))
    leaf = ((y * 2 + core) * 4 + x) * 8 + z
    return [z, x, y, core] + [jnp.bitwise_xor(partners[h], leaf // 2**h) for h in range(4)]


def paired(a, axis):
    return jnp.concatenate(split(a), axis=axis)


def times(a, pair):
    both = halves(dot(stacked(a), pair))
    n = both.shape[1] // 2
    return both[:, :n] + both[:, n:]


def times_t(a, pair):
    both = halves(dot(stacked(a), pair, 1, 1))
    n = both.shape[1] // 2
    return both[:, :n] + both[:, n:]


def square_sum(v):
    return jnp.broadcast_to(jnp.sum(v * v, axis=1, keepdims=True), (v.shape[0], 64))


def lift(own, chain):
    lifted = times(own, chain)
    return jnp.concatenate([own, lifted[:, 0:64]], axis=1), lifted[:, 64:192], lifted[:, 192:256]


def write_moments(extended, out, v, own, weighed, chain):
    first, middle, top = lift(own, chain[...])
    last = jnp.concatenate([top, square_sum(weighed)], axis=1)
    for i in range(out.shape[0]):
        out[i, 0:16, :] = middle
        out[i, 16:32, :] = last
    extended[:, 0 : v.shape[1]] = v
    extended[:, v.shape[1] :] = first


def packed(skeleton):
    return jnp.concatenate([skeleton[0:32], skeleton[32:64]], axis=1)


def unpacked(block):
    return jnp.concatenate([block[:, 0:64], block[:, 64:128]], axis=0)


def skeleton_offsets(scalars):
    o0, o1 = scalars[O0], scalars[O1]
    second = jnp.where(o1 > 1, o1 * 2, jnp.where(o0 == 2, 3, 2))
    return o0, second, jnp.where(o1 == 3, 4, 7)


def prepare_kernel(
    scalars, order, basis, maps, skeletons, rhs, bases, chain, tail, gram, own, wire, second
):
    both = stacked(basis[...])
    leaf = basis.shape[1]
    for t in range(leaf // TILE):
        rows = lax.broadcasted_iota(jnp.int32, (TILE, leaf), 0) + t * TILE
        one_hot = jnp.where(rows == order[...], 1.0, 0.0).astype(BF16)
        bases[:, t * TILE : (t + 1) * TILE] = dot(both, one_hot, 1, 1).astype(BF16)
    p1 = maps[0]
    p2 = dot(p1, maps[1], precision=HIGHEST)
    p3 = dot(p2, maps[2], precision=HIGHEST)
    e34 = dot(maps[3], maps[4], precision=HIGHEST)
    p5 = dot(p3, e34, precision=HIGHEST)
    tail[...] = e34
    chain[...] = paired(jnp.concatenate([p1, p2, p3, p5], axis=1), 1)
    products = dot(bases[...], bases[...], 1, 1)
    products = halves(products[:, 0:64] + products[:, 64:128])
    gram[...] = paired(products, 1)
    first, middle, top = lift(times_t(rhs[...], bases[...]), chain[...])
    own[...] = first
    last = jnp.concatenate([top, jnp.zeros_like(top)], axis=1)
    for i in range(wire.shape[0]):
        wire[i, 0:16, :] = middle
        wire[i, 16:32, :] = last
        wire[i, 32:64, :] = packed(skeletons[3])
    second[...] = packed(skeletons[2])


def matern(first, second):
    turned = first.T
    squares = (
        jnp.sum(turned * turned, axis=1, keepdims=True)
        + jnp.sum(second * second, axis=0, keepdims=True)
        - 2.0 * dot(turned, second, precision=HIGHEST)
    )
    s = SCALE * jnp.sqrt(jnp.maximum(squares, 0.0))
    return (1.0 + s + s * s * (1.0 / 3.0)) * jnp.exp(-s)


def top_kernel(scalars, listed, skeletons, from_yx, tops, tail, out):
    x, y, core = scalars[X], scalars[Y], scalars[CORE]
    partner = unpacked(from_yx[y * 4 + jnp.bitwise_xor(x, scalars[O3]), 32:64, :])
    others = []
    masks = []
    for flip in (0, 1):
        for j in range(4):
            side = jnp.bitwise_xor(core, flip)
            others.append(tops[j, side])
            hits = sum((listed[k] == j * 2 + side).astype(F32) for k in range(4))
            masks.append(jnp.full((64, 64), hits, F32))
    top = matern(tops[y, core], jnp.concatenate(others, axis=1))
    top = dot(tail[...], top * jnp.concatenate(masks, axis=1), precision=HIGHEST)
    out[...] = paired(jnp.concatenate([matern(skeletons[3], partner), top], axis=1), 0)


def low_couplings(scalars, skeletons, from_z, chain):
    z = scalars[Z]
    down = chain[:, 0:256].astype(F32) + chain[:, 256:512].astype(F32)
    pieces = []
    for h, offset in enumerate(skeleton_offsets(scalars)):
        if h == 2:
            offset = jnp.where(scalars[O2] % 2 == 1, offset, 0)
        partner = unpacked(from_z[jnp.bitwise_xor(z, offset), 32:64, :])
        coupling = matern(skeletons[h], partner)
        if h > 0:
            coupling = dot(down[:, (h - 1) * 64 : h * 64], coupling, precision=HIGHEST)
        pieces.append(coupling)
    return paired(jnp.concatenate(pieces + [down[:, 128:192]], axis=1), 0)


def three(a):
    high = a.astype(BF16).astype(F32)
    middle = (a - high).astype(BF16).astype(F32)
    return high, middle, a - high - middle


def augment(points, target, turned):
    leaf = points.shape[1]
    high, low = split(points * SCALE)
    h32, l32 = high.astype(F32), low.astype(F32)
    sums = three(jnp.sum(h32 * h32 + 2.0 * (h32 * l32), axis=0, keepdims=True))
    row = lax.broadcasted_iota(jnp.int32, (16, leaf), 0)
    first, ones = (0, 3) if turned else (3, 0)
    rest = jnp.where((row >= ones) & (row < ones + 3), 1.0, 0.0)
    for i in range(3):
        rest = jnp.where(row == first + i, sums[i], rest)
    if turned:
        high, low = (-2.0 * h32).astype(BF16), (-2.0 * l32).astype(BF16)
    target[0:64, :] = high
    target[64:128, :] = high if turned else low
    target[128:192, :] = low if turned else high
    target[192:208, :] = rest.astype(BF16)


def entries(squares, kernel):
    wide = 512
    tall = 32
    for r in range(0, squares.shape[0], tall):
        for c in range(0, squares.shape[1], wide):
            s2 = jnp.maximum(squares[r : r + tall, c : c + wide], 1e-30)
            s = s2 * lax.rsqrt(s2)
            value = (1.0 + s + s2 * (1.0 / 3.0)) * jnp.exp2(s * -LOG2E)
            high, low = split(value)
            kernel[0, r : r + tall, c : c + wide] = high
            kernel[1, r : r + tall, c : c + wide] = low


def build_kernel(scalars, own, *refs, choice):
    if choice is None:
        whole, near, aug, left, squares, kernel, sems = refs[-7:]
        both = own[...]
        near[...] = NOISE * own[64:80, :]
        slot = 0
    else:
        yes, no, begin = refs[:3]
        whole, near, aug, left, squares, kernel, sems = refs[-7:]
        both = jnp.where(scalars[O0] == choice, yes[...], no[...])
        near[...] = begin[...]
        slot = (choice + 1) // 2
    augment(own[0:64, :], aug, False)
    augment(both[0:64, :], left, True)
    pair = stacked(both[64:80, :])
    leaf = own.shape[1]
    tiles = leaf // TILE
    copies = []
    total = None
    squares[0] = dot(left[:, 0:TILE], aug[...], 0, 0)
    for t in range(tiles):
        cols = slice(t * TILE, (t + 1) * TILE)
        if t + 1 < tiles:
            squares[(t + 1) % 2] = dot(left[:, (t + 1) * TILE : (t + 2) * TILE], aug[...], 0, 0)
        entries(squares.at[t % 2], kernel.at[t])
        part = dot(pair[:, cols], kernel[t, 0]) + dot(pair[:, cols], kernel[t, 1])
        total = part if total is None else total + part
        rows = pl.ds(t * TILE, TILE)
        copies.append(
            pltpu.make_async_copy(kernel.at[t], whole.at[slot, :, rows, :], sems.at[t])
        )
        copies[t].start()
    near[...] += halves(total)
    for copy in copies:
        copy.wait()


def near_kernel(scalars, v, v1, v2, v3, bases, kernels, after, out, held, sems):
    leaf = kernels.shape[2]
    tiles = leaf // TILE
    copies = []
    for e in range(3):
        for t in range(tiles):
            rows = pl.ds(t * TILE, TILE)
            copies.append(
                pltpu.make_async_copy(
                    kernels.at[e, :, rows, :], held.at[e, :, rows, :], sems.at[e * tiles + t]
                )
            )
    for copy in copies:
        copy.start()
    o0 = scalars[O0]
    own = v[:, 0:leaf]
    second = jnp.where(o0 == 1, v2[:, 0:leaf], v1[:, 0:leaf])
    third = jnp.where(o0 == 3, v2[:, 0:leaf], v3[:, 0:leaf])
    total = None
    for e, vector in enumerate((own, second, third)):
        pair = stacked(vector)
        for t in range(tiles):
            rows = slice(t * TILE, (t + 1) * TILE)
            copies[e * tiles + t].wait()
            part = dot(pair[:, rows], held[e, 0, rows, :]) + dot(pair[:, rows], held[e, 1, rows, :])
            total = part if total is None else total + part
    result = NOISE * own + halves(total)
    partner = jnp.where(o0 == 1, v1[:, leaf:], jnp.where(o0 == 2, v2[:, leaf:], v3[:, leaf:]))
    out[:, 0:leaf] = result
    out[:, leaf:] = jnp.concatenate([partner[:, 0:64], times_t(result, bases[...])], axis=1)


def gather_kernel(scalars, received, *refs):
    high, out = refs[-2:]
    x, y, o2, o3 = scalars[X], scalars[Y], scalars[O2], scalars[O3]
    left = lax.broadcasted_iota(jnp.int32, (16, 128), 1) < 64
    total = jnp.zeros((16, 128), F32)
    for j in range(4):
        top = jnp.zeros((16, 128), F32)
        for i in range(4):
            p = j * 4 + i
            offset = jnp.bitwise_xor(x, i)
            here = y == j
            hit2 = here & (offset == o2 // 2)
            hit3 = here & (offset == o3)
            total += jnp.where((left & hit2) | (~left & hit3), received[p, 0:16, :], 0.0)
            top += received[p, 16:32, :]
        out[j * 16 : (j + 1) * 16, :] = top
    high[...] = total


def lower_blocks(high, mine, other, table, own):
    start = own.shape[1] - 128
    parts = [high[:, 64:128]]
    for side in (mine, other):
        parts += [side[j * 16 : (j + 1) * 16, 0:64] for j in range(4)]
    field = times_t(jnp.concatenate(parts, axis=1), table[...])
    return field, jnp.concatenate([own[:, start + 64 :], high[:, 0:64]], axis=1)


def lower_kernel(high, mine, other, table, own, *refs):
    out = refs[-1]
    field, second = lower_blocks(high, mine, other, table, own)
    norm = sum(side[j * 16 : (j + 1) * 16, 64:128] for side in (mine, other) for j in range(4))
    first = jnp.concatenate([field, norm], axis=1)
    for i in range(out.shape[0]):
        out[i, 0:16, :] = first
        out[i, 16:32, :] = second


def first_lower_kernel(scalars, high, mine, other, table, own, skeletons, second, moved, out):
    field, lifted = lower_blocks(high, mine, other, table, own)
    first = jnp.concatenate([field, own[:, 0:64]], axis=1)
    _, k1, k2 = skeleton_offsets(scalars)
    third = jnp.where(scalars[O2] > 1, moved[...], second[...])
    blocks = [packed(skeletons[0]), packed(skeletons[1]), third]
    for i in range(out.shape[0]):
        offset = jnp.bitwise_xor(scalars[Z], i)
        block = jnp.where(offset == k1, blocks[1], blocks[0])
        out[i, 0:16, :] = first
        out[i, 16:32, :] = lifted
        out[i, 32:64, :] = jnp.where((offset == k2) | (offset == 0), blocks[2], block)


def apply_far(scalars, received, table, bases, near):
    leaf = bases.shape[1]
    z, o0, o1, o2 = scalars[Z], scalars[O0], scalars[O1], scalars[O2]
    start = received.shape[1] > 32
    left = lax.broadcasted_iota(jnp.int32, (16, 128), 1) < 64
    sums = [jnp.zeros((16, 128), F32) for _ in range(2)]
    for i in range(received.shape[0]):
        offset = jnp.bitwise_xor(z, i)
        hit1 = offset // 2 == o1
        hit2 = offset // 4 == jnp.bitwise_and(o2, 1)
        block = received[i, 0:16, :]
        sums[0] += jnp.where(left | (offset == o0), block, 0.0) if start else block
        sums[1] += jnp.where((left & hit1) | (~left & hit2), received[i, 16:32, :], 0.0)
    moment = sums[0][:, 64:128] if start else near[:, leaf : leaf + 64]
    parts = [moment, sums[1], sums[0][:, 0:64]]
    field = times_t(jnp.concatenate(parts, axis=1), table[...])
    pair = stacked(field)
    far = halves(dot(pair, bases[0:64, :]) + dot(pair, bases[64:128, :]))
    return near[:, 0:leaf] + far, sums[0][:, 64:65], field


def moment_of(near, field, gram):
    return near[:, near.shape[1] - 64 :] + times(field, gram[...])


def first_kernel(
    scalars, received, skeletons, bases, near, chain, table, v1, out
):
    table[...] = low_couplings(scalars, skeletons, received, chain)
    image, _, _ = apply_far(scalars, received, table, bases, near)
    own = times_t(image, bases[...])
    write_moments(v1, out, image, own, image, chain)


def second_kernel(
    scalars, received, table, bases, near, gram, chain, v2, scaled, sums, out
):
    image, norm, field = apply_far(scalars, received, table, bases, near)
    v2[...] = image
    sums[...] = jnp.broadcast_to(norm, sums.shape)
    size = 1.0 / jnp.sqrt(norm)
    own = moment_of(near, field, gram) * size
    write_moments(scaled, out, image * size, own, image, chain)


def third_kernel(
    scalars, received, table, bases, near, gram, chain, v1, sums, image, step, out
):
    product, along, field = apply_far(scalars, received, table, bases, near)
    leaf = product.shape[1]
    norm = sums[:, 0:1]
    size = norm / along
    back = size * jnp.sqrt(norm)
    new = v1[:, 0:leaf] - back * product
    own = v1[:, leaf : leaf + 64] - back * moment_of(near, field, gram)
    step[...] = jnp.broadcast_to(size, step.shape)
    write_moments(image, out, new, own, new, chain)


def diagonal():
    rows = lax.broadcasted_iota(jnp.int32, (16, 128), 0)
    return rows == lax.broadcasted_iota(jnp.int32, (16, 128), 1)


def fourth_kernel(scalars, received, table, bases, near, v2, sums, along, fresh, out):
    product, norm, _ = apply_far(scalars, received, table, bases, near)
    new = product + (norm / sums[:, 0:1]) * v2[...]
    along[...] = new
    fresh[...] = jnp.broadcast_to(norm, fresh.shape)
    share = jnp.sum(new * new, axis=1, keepdims=True)
    line = jnp.sum(jnp.where(diagonal(), share, 0.0), axis=0, keepdims=True)
    out[...] = jnp.broadcast_to(line, out.shape)


def last_kernel(shares, rhs, v1, v2, image, along, sums, fresh, step, iterate, residual):
    leaf = rhs.shape[1]
    norm = fresh[:, 0:1]
    first = step[:, 0:1]
    line = jnp.sum(shares[...], axis=0, keepdims=True)
    second = norm / jnp.sum(jnp.where(diagonal(), line, 0.0), axis=1, keepdims=True)
    beta = norm / sums[:, 0:1]
    start = v1[:, 0:leaf]
    iterate[...] = first * start + second * (image[:, 0:leaf] + beta * start)
    residual[...] = rhs[...] - first * v2[...] - second * along[...]


SMEM = pl.BlockSpec(memory_space=pltpu.SMEM)
VMEM = pl.BlockSpec(memory_space=pltpu.VMEM)


def shaped(*shape, dtype=F32):
    return jax.ShapeDtypeStruct(shape, dtype)


MIB = 1024 * 1024
ANY = pl.BlockSpec(memory_space=pl.ANY)


def call(kernel, outs, scalars, arrays, name, after=(), limit=16, flops=100000, scratch=(), alias=None):
    def body(*refs):
        if scalars:
            kernel(places(refs[0]), *refs[1:])
        else:
            kernel(*refs)

    return pl.pallas_call(
        body,
        out_shape=outs,
        in_specs=[SMEM] * len(scalars) + [VMEM] * len(arrays) + [ANY] * len(after),
        out_specs=jax.tree.map(lambda a: ANY if len(a.shape) == 4 else VMEM, outs),
        scratch_shapes=list(scratch),
        input_output_aliases=alias or {},
        name=name,
        compiler_params=pltpu.CompilerParams(vmem_limit_bytes=limit * MIB),
        cost_estimate=pl.CostEstimate(flops=flops, bytes_accessed=500000, transcendentals=0),
    )(*scalars, *arrays, *after)


def build(scalars, own, others, choice, near, after, name, kernels=()):
    leaf = own.shape[1]
    tiles = leaf // TILE
    return call(
        functools.partial(build_kernel, choice=choice),
        (shaped(3, 2, leaf, leaf, dtype=BF16), shaped(16, leaf)),
        [scalars],
        [own, *others, *([] if near is None else [near])],
        name,
        after=[*after, *kernels],
        limit=50,
        flops=4000000000,
        alias={3 + len(others) + len(after): 0} if kernels else None,
        scratch=[
            pltpu.VMEM((DEPTH, leaf), BF16),
            pltpu.VMEM((DEPTH, leaf), BF16),
            pltpu.VMEM((2, TILE, leaf), F32),
            pltpu.VMEM((tiles, 2, TILE, leaf), BF16),
            pltpu.SemaphoreType.DMA((tiles,)),
        ],
    )


def near_product(scalars, vectors, bases, kernels, after):
    leaf = kernels.shape[2]
    return call(
        near_kernel,
        shaped(*vectors[0].shape),
        [scalars],
        [*vectors, bases],
        "near",
        after=[kernels, after],
        limit=50,
        flops=4000000000,
        scratch=[
            pltpu.VMEM((3, 2, leaf, leaf), BF16),
            pltpu.SemaphoreType.DMA((3 * leaf // TILE,)),
        ],
    )


def along_z(v, offset):
    return lax.ppermute(v, "z", [(i, i ^ offset) for i in range(8)])


def other_core(v):
    return lax.ppermute(v, "core", [(0, 1), (1, 0)])


def over_z(v):
    return lax.all_to_all(v, "z", 0, 0)


def over_yx(v):
    return lax.all_to_all(v, ("y", "x"), 0, 0)


def local(
    rhs,
    embeddings,
    leaf_order,
    basis,
    transfer_maps,
    skeletons,
    top_skeletons,
    near_lists,
    far_lists,
    top_lists,
):
    top = lax.axis_index("y") * 2 + lax.axis_index("core")
    listed = lax.dynamic_index_in_dim(top_lists, top, 0, keepdims=False)
    scalars = far_lists[:, 0]
    chain_skeletons = skeletons[:, 0]
    tops = top_skeletons.reshape(4, 2, 64, 64)

    row = shaped(16, 1024)
    long = shaped(16, 1152)
    thin = shaped(16, 128)
    wire = shaped(16, 32, 128)
    both = jnp.concatenate([embeddings, rhs], axis=0)
    one = along_z(both, 1)
    two = along_z(both, 2)
    three_off = along_z(two, 1)
    bases, chain, tail, gram, own, outgoing, second = call(
        prepare_kernel,
        (
            shaped(128, 1024, dtype=BF16),
            shaped(64, 512, dtype=BF16),
            shaped(64, 64),
            shaped(64, 128, dtype=BF16),
            thin,
            shaped(16, 64, 128),
            shaped(32, 128),
        ),
        [scalars],
        [leaf_order, basis, transfer_maps[:, 0], chain_skeletons, rhs],
        "prepare",
        limit=60,
    )

    def gather(spread, after=()):
        high, mine = call(
            gather_kernel, (thin, shaped(64, 128)), [scalars], [spread], "gather", after=after
        )
        return high, mine, other_core(mine)

    kernels, near = build(scalars, both, [], None, None, [two, one], "build_own")
    from_yx = over_yx(outgoing)
    second_moved = lax.ppermute(second, "x", [(i, i ^ 1) for i in range(4)])
    spread = gather(from_yx, [near, second_moved])
    top_table = call(
        top_kernel,
        shaped(128, 576, dtype=BF16),
        [scalars, listed],
        [chain_skeletons, from_yx, tops, tail],
        "tops",
    )
    outgoing = call(
        first_lower_kernel,
        shaped(8, 64, 128),
        [scalars],
        [*spread, top_table, own, chain_skeletons, second, second_moved],
        "lower",
    )
    kernels, near = build(
        scalars, both, [two, one], 1, near, [outgoing, three_off], "build_a", [kernels]
    )
    kernels, near = build(
        scalars, both, [two, three_off], 3, near, [outgoing], "build_b", [kernels]
    )
    table, v1, outgoing = call(
        first_kernel,
        (shaped(128, 256, dtype=BF16), long, wire),
        [scalars],
        [over_z(outgoing), chain_skeletons, bases, near, chain],
        "first",
    )

    def operate(extended, outgoing):
        moved = [along_z(extended, o) for o in (1, 2, 3)]
        spread = gather(over_yx(outgoing))
        lower = call(
            lower_kernel,
            shaped(8, 32, 128),
            [],
            [*spread, top_table, extended],
            "lower",
            after=moved,
        )
        near = near_product(scalars, [extended, *moved], bases, kernels, lower)
        return over_z(lower), table, bases, near

    v2, scaled, sums, outgoing = call(
        second_kernel,
        (row, long, thin, wire),
        [scalars],
        [*operate(v1, outgoing), gram, chain],
        "second",
    )
    image, step, outgoing = call(
        third_kernel,
        (long, thin, wire),
        [scalars],
        [*operate(scaled, outgoing), gram, chain, v1, sums],
        "third",
    )
    along, fresh, outgoing = call(
        fourth_kernel,
        (row, thin, shaped(256, 128)),
        [scalars],
        [*operate(image, outgoing), v2, sums],
        "fourth",
    )
    shares = lax.all_to_all(outgoing, ("y", "core", "x", "z"), 0, 0, tiled=True)
    return call(
        last_kernel,
        (row, row),
        [],
        [shares, rhs, v1, v2, image, along, sums, fresh, step],
        "last",
    )


def solution(mesh):
    axes = ("y", "core", "x", "z")
    fine = Mesh(mesh.devices.reshape(4, 2, 4, 8), axes)
    placed = (
        P(None, axes),
        P(None, axes),
        P(axes, None),
        P(None, axes),
        P(None, axes, None, None),
        P(None, axes, None, None),
        P(),
        P(axes, None),
        P(None, axes),
        P(),
    )
    return jax.shard_map(
        local,
        mesh=fine,
        in_specs=placed,
        out_specs=(P(None, axes), P(None, axes)),
        check_vma=False,
    )
```
